32 devices in a mesh: owner: 8 (over z, x), helper: 4 (over y, core).
Axes of the slice: x: 2, y: 2, z: 4, core: 2. Of those that a mesh axis runs over, the one named last changes fastest.
Arguments:
- states: bfloat16 [16, 128, 768], P('owner'), may hold values from -6 to 6
- partners: int32 [16, 5], P('owner'), may hold values from -1 to 15, as said below
- self_proj: bfloat16 [3, 768, 768], P(None, None, 'helper'), may hold values from -0.28867513 to 0.28867513
- self_out: bfloat16 [768, 768], P('helper'), may hold values from -0.21875 to 0.21875
- cross_proj: bfloat16 [3, 768, 768], P(None, None, 'helper'), may hold values from -0.28867513 to 0.28867513
- cross_out: bfloat16 [768, 768], P('helper'), may hold values from -0.21875 to 0.21875
- gains: float32 [3, 768], replicated, may hold values from 0.5 to 1.5
Outputs:
- pair_states: bfloat16 [16, 5, 128, 768], P('owner', None, 'helper')
The draws below stay inside these ranges and needn't reach their ends.
Inputs may be any that keep to these rules, and one draw needn't show every extreme that they name: Row i lists the images paired with image i, left-aligned, then -1 in the remaining slots. Pairs are symmetric. Images 2 * o and 2 * o + 1 belong to owner o. With M = 8 owners, every pair joins owner o with owner o + k modulo M for k from 1 to 2 or k = M // 2, or with owner o - k modulo M for k from 1 to 2; each of these 5 owners is joined to o by exactly one pair, so the two images of one owner take part in exactly 5 pairs together, and some image has 5 partners.
All inputs are finite; a program needn't handle non-finite values.
Results may differ from the reference program's by a relative error of at most 0.0095.
Values may be sent and summed in bfloat16 or wider, within the bound.
No kernel may reach another device: no remote copies, remote signals or barrier semaphores. Data moves between devices by JAX's collectives and lax.ppermute only.
A program may use at most 128 MiB of HBM per device.

```python
import jax
import jax.numpy as jnp
from jax import lax

D = 768
HEAD = 64
PATCHES = 128
NEAR = 3
SLOTS = 5
IMAGES = 16


def clipped_normal(key, shape, limit):
    return jnp.clip(jax.random.normal(key, shape, jnp.float32), -limit, limit)


def draw_states(key, part):
    key = jax.random.fold_in(key, 11)
    key_base = jax.random.fold_in(key, 0)
    values = clipped_normal(key_base, (IMAGES, PATCHES, D), 6.0)
    return values.astype(jnp.bfloat16)


def draw_self_proj(key, part):
    key = jax.random.fold_in(key, 23)
    scale = D ** (-0.5)
    values = clipped_normal(key, (3, D, D), 6.0) * scale
    return values.astype(jnp.bfloat16)


def draw_cross_proj(key, part):
    key = jax.random.fold_in(key, 37)
    scale = D ** (-0.5)
    values = clipped_normal(key, (3, D, D), 6.0) * scale
    return values.astype(jnp.bfloat16)


def draw_partners(key, part):
    key = jax.random.fold_in(key, 7)
    owner_count = IMAGES // 2
    half_way = owner_count // 2
    key_level, key_front, key_back = jax.random.split(key, 3)
    level = jax.random.randint(key_level, (owner_count,), 1, 10)
    owner_ids = jnp.arange(owner_count, dtype=jnp.int32)
    offsets = jnp.where(jnp.arange(NEAR, dtype=jnp.int32) == NEAR - 1, half_way, jnp.arange(1, NEAR + 1, dtype=jnp.int32)).astype(jnp.int32)
    is_half = (jnp.arange(NEAR, dtype=jnp.int32) == NEAR - 1)[None, :]
    starts = jnp.logical_or(jnp.logical_not(is_half), owner_ids[:, None] < half_way)
    target = (owner_ids[:, None] + offsets[None, :]) % owner_count
    front_bit = (jax.random.randint(key_front, (owner_count, NEAR), 0, 10) >= level[:, None]).astype(jnp.int32)
    back_bit = (jax.random.randint(key_back, (owner_count, NEAR), 0, 10) >= level[target]).astype(jnp.int32)
    front_bit = jnp.where(owner_ids[:, None] == 0, 0, front_bit)
    back_bit = jnp.where(target == 0, 0, back_bit)
    front_partner = 2 * target + back_bit
    anchor = (owner_ids[:, None] - offsets[None, :]) % owner_count
    offset_index = jnp.broadcast_to(jnp.arange(NEAR, dtype=jnp.int32)[None, :], anchor.shape)
    back_here = back_bit[anchor, offset_index]
    back_live = starts[anchor, offset_index]
    back_partner = 2 * anchor + front_bit[anchor, offset_index]
    listing = []
    for image_bit in range(2):
        forward_list = jnp.where(jnp.logical_and(front_bit == image_bit, starts), front_partner, -1)
        backward_list = jnp.where(jnp.logical_and(back_here == image_bit, back_live), back_partner, -1)
        listing.append(jnp.concatenate([forward_list, backward_list], axis=1))
    candidates = jnp.stack(listing, axis=1).astype(jnp.int32)
    sort_order = jnp.argsort((candidates < 0).astype(jnp.int32), axis=-1, stable=True)
    candidates = jnp.take_along_axis(candidates, sort_order, axis=-1)[:, :, :SLOTS]
    return candidates.reshape(IMAGES, SLOTS).astype(jnp.int32)


def levels(key, extent, pieces, smallest, top_value):
    level, own = 1.0, jax.random.fold_in(key, 6)
    for axis_at, parts in pieces:
        steps = jnp.exp(jax.random.uniform(jax.random.fold_in(own, axis_at), (parts,), jnp.float32, smallest / len(pieces), top_value / len(pieces)))
        level = level * jnp.repeat(steps, extent[axis_at] // parts).reshape([-1 if axis == axis_at else 1 for axis in range(len(extent))])
    return level


def bell_draw(stream_key, extent, deviation, reach, cuts=(), kind=jnp.bfloat16):
    entries = deviation * jax.random.normal(stream_key, extent, jnp.float32)
    if cuts:
        entries = entries * levels(stream_key, extent, cuts, -0.22, 0.18)
    return jnp.clip(entries, -reach, reach).astype(kind)


def setup_inputs(seed: int = 0) -> dict:
    seeds = jax.random.split(jax.random.key(seed), 8)
    return {
        "states": draw_states(jax.random.fold_in(seeds[7], 71), 0),
        "partners": draw_partners(jax.random.fold_in(seeds[7], 71), 0),
        "self_proj": draw_self_proj(jax.random.fold_in(seeds[7], 71), 0),
        "self_out": bell_draw(seeds[3], (D, D), D ** -0.5, 0.21875, ((0, 4),)),
        "cross_proj": draw_cross_proj(jax.random.fold_in(seeds[7], 71), 0),
        "cross_out": bell_draw(seeds[5], (D, D), D ** -0.5, 0.21875, ((0, 4),)),
        "gains": jnp.clip(1.0 + 0.1 * jax.random.normal(seeds[6], (3, D), jnp.float32), 0.5, 1.5),
    }


def rounded(values):
    return lax.optimization_barrier(values.astype(jnp.bfloat16)).astype(jnp.float32)

def norm_rows(values, gain_row):
    row_mean = lax.optimization_barrier(jnp.mean(values, -1, keepdims=True))
    centred = values - row_mean
    row_var = lax.optimization_barrier(jnp.mean(centred * centred, -1, keepdims=True))
    return centred * lax.rsqrt(row_var + 1e-05) * gain_row

def attend(queries, key_rows, value_rows):
    count_n, patch_n, column_n = queries.shape
    head_count = column_n // HEAD
    q_heads = queries.reshape(count_n, patch_n, head_count, HEAD)
    k_heads = key_rows.reshape(count_n, key_rows.shape[1], head_count, HEAD)
    v_heads = value_rows.reshape(count_n, value_rows.shape[1], head_count, HEAD)
    scores = jnp.einsum('nqhe,nkhe->nhqk', q_heads, k_heads) * HEAD ** (-0.5)
    weights = rounded(jax.nn.softmax(scores, axis=-1))
    context = jnp.einsum('nhqk,nkhe->nqhe', weights, v_heads)
    return rounded(context).reshape(count_n, patch_n, column_n)

def reference(states, partners, self_proj, self_out, cross_proj, cross_out, gains):
    as_float = states.astype(jnp.float32)
    normed = rounded(norm_rows(as_float, gains[0]))
    projected = rounded(jnp.einsum('ipd,cdf->cipf', normed, self_proj.astype(jnp.float32)))
    context = attend(projected[0], projected[1], projected[2])
    mixed = as_float + jnp.einsum('ipf,fd->ipd', context, self_out.astype(jnp.float32))
    queries = rounded(jnp.einsum('ipd,df->ipf', rounded(norm_rows(mixed, gains[1])), cross_proj[0].astype(jnp.float32)))
    key_norm = rounded(norm_rows(as_float, gains[2]))
    key_rows = rounded(jnp.einsum('ipd,df->ipf', key_norm, cross_proj[1].astype(jnp.float32)))
    value_rows = rounded(jnp.einsum('ipd,df->ipf', key_norm, cross_proj[2].astype(jnp.float32)))
    out_weight = cross_out.astype(jnp.float32)

    def one_image(inputs):
        image_query, image_mixed, image_partners = inputs
        is_live = image_partners >= 0
        picked = jnp.where(is_live, image_partners, 0).astype(jnp.int32)
        side_keys = key_rows[picked]
        side_values = value_rows[picked]
        side_query = jnp.broadcast_to(image_query[None], side_keys.shape)
        side_context = attend(side_query, side_keys, side_values)
        result = image_mixed[None] + jnp.einsum('spf,fd->spd', side_context, out_weight)
        result = jnp.where(is_live[:, None, None], result, jnp.zeros((), jnp.float32))
        return result.astype(jnp.bfloat16)
    return lax.map(one_image, (queries, mixed, partners))
```

```python
import functools

import jax
import jax.numpy as jnp
from jax import lax
from jax.experimental import pallas as pl
from jax.experimental.pallas import tpu as pltpu
from jax.sharding import PartitionSpec as P

HEAD = 64
F32 = jnp.float32
BF16 = jnp.bfloat16
VMEM_BYTES = 24 * 1024 * 1024

VMEM = pl.BlockSpec(memory_space=pltpu.VMEM)
SMEM = pl.BlockSpec(memory_space=pltpu.SMEM)


def owner_offsets(slot_count, owner_count):
    near = (slot_count - 1) // 2
    ups = list(range(1, near + 1))
    return ups + [owner_count - k for k in ups] + [owner_count // 2]


def nn(left, right):
    return lax.dot_general(left, right, (((1,), (0,)), ((), ())), preferred_element_type=F32)


def nt(left, right):
    return lax.dot_general(left, right, (((1,), (1,)), ((), ())), preferred_element_type=F32)


def norm_core(values):
    row_mean = jnp.mean(values, -1, keepdims=True)
    centred = values - row_mean
    row_var = jnp.mean(centred * centred, -1, keepdims=True)
    return centred * lax.rsqrt(row_var + 1e-05)


def attend(queries, keys_t, values_t):
    row_n, column_n = queries.shape
    head_n = column_n // HEAD
    head_of = lax.broadcasted_iota(jnp.int32, (row_n, column_n), 1) // HEAD
    zero = jnp.zeros((), queries.dtype)
    stacked = jnp.concatenate([jnp.where(head_of == h, queries, zero) for h in range(head_n)], 0)
    scores = nn(stacked.astype(BF16), keys_t)
    top = jnp.max(scores, -1, keepdims=True)
    powers = jnp.exp(scores - top)
    weights = (powers * (1.0 / jnp.sum(powers, -1, keepdims=True))).astype(BF16)
    spread = nt(weights, values_t)
    context = spread[(head_n - 1) * row_n :]
    for h in range(head_n - 1):
        context = jnp.where(head_of == h, spread[h * row_n : (h + 1) * row_n], context)
    return context.astype(BF16)


def joined_image(partners_ref, owner, image_n):
    low = owner * image_n
    found = jnp.int32(0)
    for image in range(1, image_n):
        for slot in range(partners_ref.shape[1]):
            gap = partners_ref[image, slot] - low
            found = jnp.where(jnp.logical_and(gap >= 0, gap < image_n), jnp.int32(image), found)
    return found


def key_value_kernel(offsets, owner_n, states, gains, proj_t, partners, *rest):
    outs, held = rest[:-1], rest[-1]
    image_n, patch_n, width = states.shape
    columns = proj_t.shape[1]
    rows = states[...].reshape(image_n * patch_n, width).astype(F32)
    normed = (norm_core(rows) * gains[2:3, :]).astype(BF16)
    both = proj_t[1:3].reshape(2 * columns, width)
    projected = nt(both, normed).astype(BF16)
    for image in range(image_n):
        held[image] = projected[:, image * patch_n : (image + 1) * patch_n]
    me = lax.axis_index("owner")
    for out, offset in zip(outs, offsets):
        target = lax.rem(me + offset, owner_n)
        out[...] = held[joined_image(partners, target, image_n)]


def self_kernel(states, gains, proj_t, out):
    image_n, patch_n, width = states.shape
    columns = proj_t.shape[1]
    rows = states[...].reshape(image_n * patch_n, width).astype(F32)
    normed = (norm_core(rows) * gains[0:1, :]).astype(BF16)
    queries = nt(normed, proj_t[0]).astype(BF16).astype(F32) * HEAD ** (-0.5)
    key_value = nt(proj_t[1:3].reshape(2 * columns, width), normed).astype(BF16)
    for image in range(image_n):
        span = slice(image * patch_n, (image + 1) * patch_n)
        out[span, :] = attend(queries[span], key_value[:columns, span], key_value[columns:, span])


def cross_kernel(offsets, owner_n, helper_n, states, gains, proj_t, partners, *rest):
    contexts, rest = rest[:helper_n], rest[helper_n:]
    weights, rest = rest[:helper_n], rest[helper_n:]
    arrived, rest = rest[: len(offsets)], rest[len(offsets) :]
    outs, rest = rest[:helper_n], rest[helper_n:]
    own_rows, mixed_ref, query_ref, side_ref = rest
    image_n, patch_n, width = states.shape
    row_n = patch_n // helper_n
    columns = proj_t.shape[1]
    mixed = states[...].reshape(image_n * patch_n, width).astype(F32)
    for context, weight in zip(contexts, weights):
        mixed = mixed + nn(context[...], weight[...])
    mixed_ref[...] = mixed.reshape(image_n, patch_n, width)
    normed = (norm_core(mixed) * gains[1:2, :]).astype(BF16)
    queries = nt(normed, proj_t[0]).astype(BF16).astype(F32) * HEAD ** (-0.5)
    query_ref[...] = queries.reshape(image_n, patch_n, columns)
    me = lax.axis_index("owner")
    for at, (offset, block) in enumerate(zip(offsets, arrived)):
        partner_owner = lax.rem(me + offset, owner_n)
        image = joined_image(partners, partner_owner, image_n)
        side_ref[at] = attend(query_ref[image], block[:columns, :], block[columns:, :])
    helper = lax.axis_index("helper")
    start = pl.multiple_of(helper * row_n, row_n)
    own_rows[...] = mixed_ref[:, pl.ds(start, row_n), :]
    for k, out in enumerate(outs):
        target = jnp.bitwise_xor(helper, k)
        start = pl.multiple_of(target * row_n, row_n)
        out[...] = side_ref[:, pl.ds(start, row_n), :].reshape(len(offsets) * row_n, columns)


def out_kernel(offsets, owner_n, helper_n, partners, own_rows, *rest):
    sides, rest = rest[:helper_n], rest[helper_n:]
    weights, rest = rest[:helper_n], rest[helper_n:]
    out, term_ref = rest
    image_n, row_n, width = own_rows.shape
    terms = nn(sides[0][...], weights[0][...])
    for side, weight in zip(sides[1:], weights[1:]):
        terms = terms + nn(side[...], weight[...])
    term_ref[...] = terms.reshape(len(offsets), row_n, width)
    me = lax.axis_index("owner")
    for image in range(image_n):
        for slot in range(partners.shape[1]):
            partner = partners[image, slot]
            which = jnp.int32(0)
            for at, offset in enumerate(offsets):
                gap = partner - lax.rem(me + offset, owner_n) * image_n
                which = jnp.where(jnp.logical_and(gap >= 0, gap < image_n), jnp.int32(at), which)
            value = (own_rows[image] + term_ref[which]).astype(BF16)
            out[image, slot] = jnp.where(partner >= 0, value, jnp.zeros_like(value))


def local(owner_n, helper_n, states, partners, self_proj, self_out, cross_proj, cross_out, gains):
    image_n, patch_n, width = states.shape
    slot_n = partners.shape[1]
    columns = self_proj.shape[2]
    row_n = patch_n // helper_n
    offsets = owner_offsets(slot_n, owner_n)
    pair_n = len(offsets)
    self_proj_t = jnp.swapaxes(self_proj, 1, 2)
    cross_proj_t = jnp.swapaxes(cross_proj, 1, 2)

    def across(value, k):
        return lax.ppermute(value, "helper", [(j, j ^ k) for j in range(helper_n)])

    def gather(value):
        blocks = {0: value}
        bit = helper_n // 2
        while bit:
            blocks.update({k ^ bit: across(block, bit) for k, block in list(blocks.items())})
            bit //= 2
        return [blocks[k] for k in range(helper_n)]

    def call(kernel, out_shape, in_specs, scratch=()):
        return pl.pallas_call(
            kernel,
            out_shape=out_shape,
            in_specs=in_specs,
            out_specs=jax.tree.map(lambda _: VMEM, out_shape),
            scratch_shapes=scratch,
            compiler_params=pltpu.CompilerParams(vmem_limit_bytes=VMEM_BYTES),
        )

    shape = jax.ShapeDtypeStruct
    self_weights = gather(self_out)
    with jax.named_scope("cross_keys_values"):
        outgoing = call(
            functools.partial(key_value_kernel, offsets, owner_n),
            [shape((2 * columns, patch_n), BF16)] * pair_n,
            [VMEM, VMEM, VMEM, SMEM],
            [pltpu.VMEM((image_n, 2 * columns, patch_n), BF16)],
        )(states, gains, cross_proj_t, partners)
    arrived = {}
    for offset, block in zip(offsets, outgoing):
        moved = lax.ppermute(block, "owner", [(o, (o + offset) % owner_n) for o in range(owner_n)])
        arrived[(owner_n - offset) % owner_n] = moved
    arrived = [arrived[offset] for offset in offsets]
    with jax.named_scope("self_attention"):
        context = call(
            self_kernel,
            shape((image_n * patch_n, columns), BF16),
            [VMEM, VMEM, VMEM],
        )(states, gains, self_proj_t)
    contexts = gather(context)
    cross_weights = gather(cross_out)
    with jax.named_scope("cross_attention"):
        *sides, own_rows = call(
            functools.partial(cross_kernel, offsets, owner_n, helper_n),
            [shape((pair_n * row_n, columns), BF16)] * helper_n + [shape((image_n, row_n, width), F32)],
            [VMEM, VMEM, VMEM, SMEM] + [VMEM] * (2 * helper_n + pair_n),
            [
                pltpu.VMEM((image_n, patch_n, width), F32),
                pltpu.VMEM((image_n, patch_n, columns), F32),
                pltpu.VMEM((pair_n, patch_n, columns), BF16),
            ],
        )(states, gains, cross_proj_t, partners, *contexts, *self_weights, *arrived)
    sides = [sides[0]] + [across(sides[k], k) for k in range(1, helper_n)]
    with jax.named_scope("pair_output"):
        return call(
            functools.partial(out_kernel, offsets, owner_n, helper_n),
            shape((image_n, slot_n, row_n, width), BF16),
            [SMEM] + [VMEM] * (1 + 2 * helper_n),
            [pltpu.VMEM((pair_n, row_n, width), F32)],
        )(partners, own_rows, *sides, *cross_weights)


def solution(mesh):
    return jax.shard_map(
        functools.partial(local, mesh.shape["owner"], mesh.shape["helper"]),
        mesh=mesh,
        in_specs=(
            P("owner", None, None),
            P("owner", None),
            P(None, None, "helper"),
            P("helper", None),
            P(None, None, "helper"),
            P("helper", None),
            P(),
        ),
        out_specs=P("owner", None, "helper", None),
        check_vma=False,
    )
```

```python
import functools

import jax
import jax.numpy as jnp
from jax import lax
from jax.experimental import pallas as pl
from jax.experimental.pallas import tpu as pltpu
from jax.sharding import PartitionSpec as P

HEAD = 64
LANES = 128
F32 = jnp.float32
BF16 = jnp.bfloat16
VMEM_BYTES = 24 * 1024 * 1024
EARLY_WEIGHT = 3 * 10**9
LATE_WEIGHT = 10**11

VMEM = pl.BlockSpec(memory_space=pltpu.VMEM)
HBM = pl.BlockSpec(memory_space=pltpu.HBM)
ANY = pl.BlockSpec(memory_space=pl.ANY)


def owner_swaps(slot_count, owner_count):
    near = (slot_count - 1) // 2
    swaps = [(owner_count // 2, 0)]
    for k in range(near, 1, -1):
        swaps += [(k, 1), (k, 0)]
    return swaps + [(1, 0), (1, 1)]


def swap_target(owner, swap, owner_count):
    distance, colour = swap
    step = distance & -distance
    if isinstance(owner, int):
        up = (owner // step) % 2 == colour
        return (owner + (distance if up else owner_count - distance)) % owner_count
    up = jnp.bitwise_and(lax.shift_right_logical(owner, step.bit_length() - 1), 1) == colour
    return lax.rem(owner + jnp.where(up, distance, owner_count - distance), owner_count)


def nn(left, right):
    return lax.dot_general(left, right, (((1,), (0,)), ((), ())), preferred_element_type=F32)


def nt(left, right):
    return lax.dot_general(left, right, (((1,), (1,)), ((), ())), preferred_element_type=F32)


def norm_core(values):
    row_mean = jnp.mean(values, -1, keepdims=True)
    centred = values - row_mean
    row_var = jnp.mean(centred * centred, -1, keepdims=True)
    return centred * lax.rsqrt(row_var + 1e-05)


def head_stack(queries):
    head_of = lax.broadcasted_iota(jnp.int32, queries.shape, 1) // HEAD
    zero = jnp.zeros((), queries.dtype)
    return jnp.concatenate(
        [jnp.where(head_of == h, queries, zero) for h in range(queries.shape[1] // HEAD)], 0
    ).astype(BF16)


def attend(stacked, keys_t, values_t):
    column_n = keys_t.shape[0]
    head_n = column_n // HEAD
    row_n = stacked.shape[0] // head_n
    scores = nn(stacked, keys_t)
    powers = jnp.exp(scores - jnp.max(scores, -1, keepdims=True))
    weights = (powers * (1.0 / jnp.sum(powers, -1, keepdims=True))).astype(BF16)
    spread = nt(weights, values_t)
    head_of = lax.broadcasted_iota(jnp.int32, (row_n, column_n), 1) // HEAD
    context = spread[(head_n - 1) * row_n :]
    for h in range(head_n - 1):
        context = jnp.where(head_of == h, spread[h * row_n : (h + 1) * row_n], context)
    return context


def pack(block):
    row_n = block.shape[0]
    tail = block[:, LANES:]
    return jnp.concatenate(
        [block[:, :LANES], jnp.concatenate([tail[: row_n // 2], tail[row_n // 2 :]], 1)], 0
    ).astype(BF16)


def joined_image(partners, owner, image_n):
    low = owner * image_n
    found = jnp.int32(0)
    for image in range(1, image_n):
        for slot in range(partners.shape[1]):
            gap = partners[image, slot] - low
            found = jnp.where(jnp.logical_and(gap >= 0, gap < image_n), jnp.int32(image), found)
    return found


def own_images_kernel(swaps, owner_n, states, gains, self_t, cross_t, partners, weight, *rest):
    outs, rest = rest[: len(swaps)], rest[len(swaps) :]
    context_out, table, weight_out, states_v, gains_v, self_v, cross_v, partners_s, held, sems = rest
    image_n, patch_n, width = states.shape
    columns = self_t.shape[1]
    copies = [
        pltpu.make_async_copy(states, states_v, sems.at[0]),
        pltpu.make_async_copy(gains, gains_v, sems.at[1]),
        pltpu.make_async_copy(cross_t.at[pl.ds(1, 2)], cross_v, sems.at[2]),
        pltpu.make_async_copy(partners, partners_s, sems.at[3]),
        pltpu.make_async_copy(self_t, self_v, sems.at[4]),
        pltpu.make_async_copy(weight, weight_out, sems.at[5]),
    ]
    for copy in copies:
        copy.start()
    copies[0].wait()
    rows = norm_core(states_v[...].reshape(image_n * patch_n, width).astype(F32))
    copies[1].wait()
    normed = (rows * gains_v[2:3, :]).astype(BF16)
    copies[2].wait()
    projected = nt(cross_v[...].reshape(2 * columns, width), normed).astype(BF16)
    for image in range(image_n):
        held[image] = projected[:, image * patch_n : (image + 1) * patch_n]
    copies[3].wait()
    me = lax.axis_index("owner")
    for at, (out, swap) in enumerate(zip(outs, swaps)):
        image = joined_image(partners_s, swap_target(me, swap, owner_n), image_n)
        out[...] = held[image]
        table[at : at + 1, :] = jnp.full((1, LANES), image, jnp.int32)
    normed = (rows * gains_v[0:1, :]).astype(BF16)
    copies[4].wait()
    queries = nt(normed, self_v[0]).astype(BF16).astype(F32) * HEAD ** (-0.5)
    key_value = nt(self_v[1:3].reshape(2 * columns, width), normed).astype(BF16)
    contexts = []
    for image in range(image_n):
        span = slice(image * patch_n, (image + 1) * patch_n)
        contexts.append(
            attend(head_stack(queries[span]), key_value[:columns, span], key_value[columns:, span])
        )
    context_out[...] = pack(jnp.concatenate(contexts, 0))
    copies[5].wait()


def unpack(block):
    row_n = block.shape[0] * 2 // 3
    tail = block[row_n:, :]
    return jnp.concatenate(
        [block[:row_n, :], jnp.concatenate([tail[:, :HEAD], tail[:, HEAD:]], 0)], 1
    )


def partial_kernel(states, own, got, own_weight, got_weight, cross_out, base, sent, weight_v, sems):
    row_all = base.shape[0]
    copies = [
        pltpu.make_async_copy(got_weight, weight_v, sems.at[0]),
        pltpu.make_async_copy(cross_out, sent.at[pl.ds(row_all, cross_out.shape[0])], sems.at[1]),
    ]
    for copy in copies:
        copy.start()
    part = nn(unpack(own[...]), own_weight[...])
    base[...] = states[...].reshape(part.shape).astype(F32)
    copies[0].wait()
    part = part + nn(unpack(got[...]), weight_v[...])
    sent[:row_all, :] = part.astype(BF16)
    base[...] += part
    copies[1].wait()


def query_kernel(helper_n, base, got, gains, proj_t, own_rows, queries_out, mixed_ref):
    mixed = base[...] + got[: base.shape[0], :].astype(F32)
    image_n, row_n, width = own_rows.shape
    patch_n = row_n * helper_n
    mixed_ref[...] = mixed.reshape(image_n, patch_n, width)
    normed = (norm_core(mixed) * gains[1:2, :]).astype(BF16)
    queries = nt(normed, proj_t[0]).astype(BF16).astype(F32) * HEAD ** (-0.5)
    queries_out[...] = queries.reshape(queries_out.shape)
    start = pl.multiple_of(lax.axis_index("helper") * row_n, row_n)
    own_rows[...] = mixed_ref[:, pl.ds(start, row_n), :]


def hand_on_kernel(weight, waited, out, sem):
    del waited
    copy = pltpu.make_async_copy(weight, out, sem)
    copy.start()
    copy.wait()


def cross_pairs(places, helper_n, queries, table, arrived, put):
    for at, (place, block) in enumerate(zip(places, arrived)):
        chosen = queries[0]
        for image in range(1, queries.shape[0]):
            chosen = jnp.where(table[place : place + 1, 0:1] == image, queries[image], chosen)
        columns = block.shape[0] // 2
        context = attend(head_stack(chosen), block[:columns, :], block[columns:, :])
        row_n = context.shape[0] // helper_n
        for helper in range(helper_n):
            put(at, helper, pack(context[helper * row_n : (helper + 1) * row_n]))


def cross_kernel(places, helper_n, queries, table, *rest):
    *arrived, out = rest

    def put(at, helper, rows):
        out[helper, at] = rows

    cross_pairs(places, helper_n, queries, table, arrived, put)


def last_cross_kernel(places, helper_n, queries, table, before, *rest):
    arrived, (*outs, held) = rest[: len(places)], rest[len(places) :]
    first = before.shape[1]
    helper = lax.axis_index("helper")
    for k, out in enumerate(outs):
        out[:first] = before[jnp.bitwise_xor(helper, k)]

    def put(at, helper, rows):
        held[helper, at] = rows

    cross_pairs(places, helper_n, queries, table, arrived, put)
    for k, out in enumerate(outs):
        out[first:] = held[jnp.bitwise_xor(helper, k)]


def side_rows(block):
    row_n = block.shape[1] * 2 // 3
    main, tail = block[:, :row_n, :], block[:, row_n:, :]
    tail = jnp.concatenate([tail[:, :, :HEAD], tail[:, :, HEAD:]], 1)
    return jnp.concatenate([main.reshape(-1, LANES), tail.reshape(-1, HEAD)], 1)


def out_kernel(swaps, owner_n, helper_n, partners, own_rows, *rest):
    sides, rest = rest[:helper_n], rest[helper_n:]
    weights, rest = rest[:helper_n], rest[helper_n:]
    out, term_ref, partners_s, sem = rest
    copy = pltpu.make_async_copy(partners, partners_s, sem)
    copy.start()
    image_n, row_n, width = own_rows.shape
    columns = HEAD + LANES
    terms = None
    for side, weight in zip(sides, weights):
        part = nn(side_rows(side[...]), weight[weight.shape[0] - columns :, :])
        terms = part if terms is None else terms + part
    term_ref[...] = terms.reshape(len(swaps), row_n, width)
    copy.wait()
    me = lax.axis_index("owner")
    lows = [swap_target(me, swap, owner_n) * image_n for swap in swaps]
    for image in range(image_n):
        for slot in range(partners.shape[1]):
            partner = partners_s[image, slot]
            which = jnp.int32(0)
            for at, low in enumerate(lows):
                gap = partner - low
                which = jnp.where(jnp.logical_and(gap >= 0, gap < image_n), jnp.int32(at), which)
            value = (own_rows[image] + term_ref[which]).astype(BF16)
            out[image, slot] = jnp.where(partner >= 0, value, jnp.zeros_like(value))


def local(owner_n, helper_n, states, partners, self_proj, self_out, cross_proj, cross_out, gains):
    image_n, patch_n, width = states.shape
    slot_n = partners.shape[1]
    columns = self_proj.shape[2]
    row_n = patch_n // helper_n
    row_all = image_n * patch_n
    swaps = owner_swaps(slot_n, owner_n)
    pair_n = len(swaps)
    self_proj_t = jnp.swapaxes(self_proj, 1, 2)
    cross_proj_t = jnp.swapaxes(cross_proj, 1, 2)
    chip_hop, core_hop = helper_n // 2, 1

    def across(value, k):
        return lax.ppermute(value, "helper", [(j, j ^ k) for j in range(helper_n)])

    def exchange(value, swap):
        return lax.ppermute(value, "owner", [(o, swap_target(o, swap, owner_n)) for o in range(owner_n)])

    def call(name, kernel, out_shape, in_specs, scratch, *operands, flops=1):
        with jax.named_scope(name):
            return pl.pallas_call(
                kernel,
                out_shape=out_shape,
                in_specs=in_specs,
                out_specs=jax.tree.map(lambda _: VMEM, out_shape),
                scratch_shapes=scratch,
                compiler_params=pltpu.CompilerParams(vmem_limit_bytes=VMEM_BYTES),
                cost_estimate=pl.CostEstimate(flops=flops, bytes_accessed=1, transcendentals=0),
            )(*operands)

    shape = jax.ShapeDtypeStruct
    dma = pltpu.SemaphoreType.DMA
    index_table = pltpu.SMEM(partners.shape, jnp.int32)
    block = shape((2 * columns, patch_n), BF16)

    partners_h = pltpu.with_memory_space_constraint(partners, pltpu.HBM)
    self_out_got = across(self_out, chip_hop)
    *outgoing, context, table, cross_out_own = call(
        "own_images",
        functools.partial(own_images_kernel, swaps, owner_n),
        [block] * pair_n
        + [
            shape((row_all * columns // LANES, LANES), BF16),
            shape((pair_n, LANES), jnp.int32),
            shape(cross_out.shape, BF16),
        ],
        [HBM] * 6,
        [
            pltpu.VMEM(states.shape, BF16),
            pltpu.VMEM(gains.shape, F32),
            pltpu.VMEM((3, columns, width), BF16),
            pltpu.VMEM((2, columns, width), BF16),
            index_table,
            pltpu.VMEM((image_n, 2 * columns, patch_n), BF16),
            dma((6,)),
        ],
        *[pltpu.with_memory_space_constraint(x, pltpu.HBM) for x in (states, gains, self_proj_t, cross_proj_t)],
        partners_h,
        pltpu.with_memory_space_constraint(cross_out, pltpu.HBM),
    )
    context_got = across(context, chip_hop)
    arrived = [exchange(value, swap) for value, swap in zip(outgoing, swaps)]
    near = (slot_n - 1) // 2
    late = list(range(2, 2 * near))
    early = [at for at in range(pair_n) if at not in late]
    cross_out_sent = call(
        "cross_output_rows",
        hand_on_kernel,
        shape(cross_out.shape, BF16),
        [ANY, ANY],
        [dma],
        cross_out_own, context_got,
    )
    cross_out_got = across(cross_out_sent, chip_hop)

    sent_shape = shape((row_all + columns, width), BF16)
    own_shape = shape((image_n, row_n, width), F32)
    query_shape = shape((image_n, patch_n, columns), F32)

    def mixing(states, gains, cross_proj_t, context, context_got, self_out, self_out_got, cross_out):
        base, sent = call(
            "self_output_share",
            partial_kernel,
            [shape((row_all, width), F32), sent_shape],
            [VMEM] * 4 + [ANY, ANY],
            [pltpu.VMEM(self_out.shape, BF16), dma((2,))],
            states, context, context_got, self_out, self_out_got, cross_out,
        )
        got = across(sent, core_hop)
        own_rows, queries = call(
            "mixed_and_queries",
            functools.partial(query_kernel, helper_n),
            [own_shape, query_shape],
            [VMEM] * 4,
            [pltpu.VMEM((image_n, patch_n, width), F32)],
            base, got, gains, cross_proj_t,
        )
        return own_rows, queries, got

    def no_pairs(*operands):
        return tuple(jnp.zeros(made.shape, made.dtype) for made in (own_shape, query_shape, sent_shape))

    own_rows, queries, got = lax.cond(
        lax.axis_index("owner") < owner_n, mixing, no_pairs,
        states, gains, cross_proj_t, context, context_got, self_out, self_out_got, cross_out_own,
    )
    packed = columns * row_n // LANES
    early_sides = call(
        "early_cross_attention",
        functools.partial(cross_kernel, early, helper_n),
        shape((helper_n, len(early), packed, LANES), BF16),
        [VMEM] * (2 + len(early)),
        [],
        queries, table, *[arrived[at] for at in early],
        flops=EARLY_WEIGHT,
    )
    sides = call(
        "late_cross_attention",
        functools.partial(last_cross_kernel, late, helper_n),
        [shape((pair_n, packed, LANES), BF16)] * helper_n,
        [VMEM] * (3 + len(late)),
        [pltpu.VMEM((helper_n, len(late), packed, LANES), BF16)],
        queries, table, early_sides, *[arrived[at] for at in late],
        flops=LATE_WEIGHT,
    )
    sides = [sides[0]] + [across(sides[k], k) for k in range(1, helper_n)]
    weights = {0: cross_out_own, core_hop: got, chip_hop: cross_out_got}
    weights[chip_hop ^ core_hop] = across(cross_out_got, core_hop)
    return call(
        "pair_output",
        functools.partial(out_kernel, [swaps[at] for at in early + late], owner_n, helper_n),
        shape((image_n, slot_n, row_n, width), BF16),
        [HBM] + [VMEM] * (1 + 2 * helper_n),
        [pltpu.VMEM((pair_n, row_n, width), F32), index_table, dma],
        partners_h, own_rows, *sides, *[weights[k] for k in range(helper_n)],
    )


def solution(mesh):
    return jax.shard_map(
        functools.partial(local, mesh.shape["owner"], mesh.shape["helper"]),
        mesh=mesh,
        in_specs=(
            P("owner", None, None),
            P("owner", None),
            P(None, None, "helper"),
            P("helper", None),
            P(None, None, "helper"),
            P("helper", None),
            P(),
        ),
        out_specs=P("owner", None, "helper", None),
        check_vma=False,
    )
```

```python
import functools

import jax
import jax.numpy as jnp
from jax import lax
from jax.experimental import pallas as pl
from jax.experimental.pallas import tpu as pltpu
from jax.sharding import PartitionSpec as P

HEAD = 64
LANES = 128
F32 = jnp.float32
BF16 = jnp.bfloat16
VMEM_BYTES = 24 * 1024 * 1024
EARLY_WEIGHT = 3 * 10**9
LATE_WEIGHT = 10**11

VMEM = pl.BlockSpec(memory_space=pltpu.VMEM)
HBM = pl.BlockSpec(memory_space=pltpu.HBM)
ANY = pl.BlockSpec(memory_space=pl.ANY)


def owner_swaps(slot_count, owner_count):
    near = (slot_count - 1) // 2
    swaps = [(owner_count // 2, 0)]
    for k in range(near, 1, -1):
        swaps += [(k, 1), (k, 0)]
    return swaps + [(1, 0), (1, 1)]


def swap_target(owner, swap, owner_count):
    distance, colour = swap
    step = distance & -distance
    if isinstance(owner, int):
        up = (owner // step) % 2 == colour
        return (owner + (distance if up else owner_count - distance)) % owner_count
    up = jnp.bitwise_and(lax.shift_right_logical(owner, step.bit_length() - 1), 1) == colour
    return lax.rem(owner + jnp.where(up, distance, owner_count - distance), owner_count)


def nn(left, right):
    return lax.dot_general(left, right, (((1,), (0,)), ((), ())), preferred_element_type=F32)


def nt(left, right):
    return lax.dot_general(left, right, (((1,), (1,)), ((), ())), preferred_element_type=F32)


def norm_core(values):
    row_mean = jnp.mean(values, -1, keepdims=True)
    centred = values - row_mean
    row_var = jnp.mean(centred * centred, -1, keepdims=True)
    return centred * lax.rsqrt(row_var + 1e-05)


def head_stack(queries):
    head_of = lax.broadcasted_iota(jnp.int32, queries.shape, 1) // HEAD
    zero = jnp.zeros((), queries.dtype)
    return jnp.concatenate(
        [jnp.where(head_of == h, queries, zero) for h in range(queries.shape[1] // HEAD)], 0
    ).astype(BF16)


def attend(stacked, keys_t, values_t):
    column_n = keys_t.shape[0]
    head_n = column_n // HEAD
    row_n = stacked.shape[0] // head_n
    scores = nn(stacked, keys_t)
    powers = jnp.exp(scores - jnp.max(scores, -1, keepdims=True))
    weights = (powers * (1.0 / jnp.sum(powers, -1, keepdims=True))).astype(BF16)
    spread = nt(weights, values_t)
    head_of = lax.broadcasted_iota(jnp.int32, (row_n, column_n), 1) // HEAD
    context = spread[(head_n - 1) * row_n :]
    for h in range(head_n - 1):
        context = jnp.where(head_of == h, spread[h * row_n : (h + 1) * row_n], context)
    return context


def pack(block):
    row_n = block.shape[0]
    tail = block[:, LANES:]
    return jnp.concatenate(
        [block[:, :LANES], jnp.concatenate([tail[: row_n // 2], tail[row_n // 2 :]], 1)], 0
    ).astype(BF16)


def joined_image(partners, owner, image_n):
    low = owner * image_n
    found = jnp.int32(0)
    for image in range(1, image_n):
        for slot in range(partners.shape[1]):
            gap = partners[image, slot] - low
            found = jnp.where(jnp.logical_and(gap >= 0, gap < image_n), jnp.int32(image), found)
    return found


def own_images_kernel(swaps, owner_n, states, gains, self_t, cross_t, partners, weight, *rest):
    outs, rest = rest[: len(swaps)], rest[len(swaps) :]
    context_out, table, weight_out, states_v, gains_v, self_v, cross_v, partners_s, held, sems = rest
    image_n, patch_n, width = states.shape
    columns = self_t.shape[1]
    copies = [
        pltpu.make_async_copy(states, states_v, sems.at[0]),
        pltpu.make_async_copy(gains, gains_v, sems.at[1]),
        pltpu.make_async_copy(cross_t.at[pl.ds(1, 2)], cross_v, sems.at[2]),
        pltpu.make_async_copy(partners, partners_s, sems.at[3]),
        pltpu.make_async_copy(self_t, self_v, sems.at[4]),
        pltpu.make_async_copy(weight, weight_out, sems.at[5]),
    ]
    for copy in copies:
        copy.start()
    copies[0].wait()
    rows = norm_core(states_v[...].reshape(image_n * patch_n, width).astype(F32))
    copies[1].wait()
    normed = (rows * gains_v[2:3, :]).astype(BF16)
    copies[2].wait()
    projected = nt(cross_v[...].reshape(2 * columns, width), normed).astype(BF16)
    for image in range(image_n):
        held[image] = projected[:, image * patch_n : (image + 1) * patch_n]
    copies[3].wait()
    me = lax.axis_index("owner")
    for at, (out, swap) in enumerate(zip(outs, swaps)):
        image = joined_image(partners_s, swap_target(me, swap, owner_n), image_n)
        out[...] = held[image]
        table[at : at + 1, :] = jnp.full((1, LANES), image, jnp.int32)
    normed = (rows * gains_v[0:1, :]).astype(BF16)
    copies[4].wait()
    queries = nt(normed, self_v[0]).astype(BF16).astype(F32) * HEAD ** (-0.5)
    key_value = nt(self_v[1:3].reshape(2 * columns, width), normed).astype(BF16)
    contexts = []
    for image in range(image_n):
        span = slice(image * patch_n, (image + 1) * patch_n)
        contexts.append(
            attend(head_stack(queries[span]), key_value[:columns, span], key_value[columns:, span])
        )
    context_out[...] = pack(jnp.concatenate(contexts, 0))
    copies[5].wait()


def unpack(block):
    row_n = block.shape[0] * 2 // 3
    tail = block[row_n:, :]
    return jnp.concatenate(
        [block[:row_n, :], jnp.concatenate([tail[:, :HEAD], tail[:, HEAD:]], 0)], 1
    )


def partial_kernel(states, own, got, own_weight, got_weight, cross_out, base, sent, weight_v, sems):
    row_all = base.shape[0]
    copies = [
        pltpu.make_async_copy(got_weight, weight_v, sems.at[0]),
        pltpu.make_async_copy(cross_out, sent.at[pl.ds(row_all, cross_out.shape[0])], sems.at[1]),
    ]
    for copy in copies:
        copy.start()
    part = nn(unpack(own[...]), own_weight[...])
    base[...] = states[...].reshape(part.shape).astype(F32)
    copies[0].wait()
    part = part + nn(unpack(got[...]), weight_v[...])
    sent[:row_all, :] = part.astype(BF16)
    base[...] += part
    copies[1].wait()


def query_kernel(helper_n, base, got, gains, proj_t, *rest):
    own_rows, queries_out, weight_out, mixed_ref, sem = rest[-5:]
    copy = pltpu.make_async_copy(got.at[pl.ds(base.shape[0], weight_out.shape[0])], weight_out, sem)
    copy.start()
    mixed = base[...] + got[: base.shape[0], :].astype(F32)
    image_n, row_n, width = own_rows.shape
    patch_n = row_n * helper_n
    mixed_ref[...] = mixed.reshape(image_n, patch_n, width)
    normed = (norm_core(mixed) * gains[1:2, :]).astype(BF16)
    queries = nt(normed, proj_t[0]).astype(BF16).astype(F32) * HEAD ** (-0.5)
    queries_out[...] = queries.reshape(queries_out.shape)
    start = pl.multiple_of(lax.axis_index("helper") * row_n, row_n)
    own_rows[...] = mixed_ref[:, pl.ds(start, row_n), :]
    copy.wait()


def hand_on_kernel(weight, waited, out, sem):
    del waited
    copy = pltpu.make_async_copy(weight, out, sem)
    copy.start()
    copy.wait()


def cross_pairs(places, helper_n, queries, table, arrived, put):
    for at, (place, block) in enumerate(zip(places, arrived)):
        chosen = queries[0]
        for image in range(1, queries.shape[0]):
            chosen = jnp.where(table[place : place + 1, 0:1] == image, queries[image], chosen)
        columns = block.shape[0] // 2
        context = attend(head_stack(chosen), block[:columns, :], block[columns:, :])
        row_n = context.shape[0] // helper_n
        for helper in range(helper_n):
            put(at, helper, pack(context[helper * row_n : (helper + 1) * row_n]))


def cross_kernel(places, helper_n, queries, table, *rest):
    *arrived, out = rest

    def put(at, helper, rows):
        out[helper, at] = rows

    cross_pairs(places, helper_n, queries, table, arrived, put)


def last_cross_kernel(places, helper_n, queries, table, before, *rest):
    arrived, (*outs, held) = rest[: len(places)], rest[len(places) :]
    first = before.shape[1]
    helper = lax.axis_index("helper")
    for k, out in enumerate(outs):
        out[:first] = before[jnp.bitwise_xor(helper, k)]

    def put(at, helper, rows):
        held[helper, at] = rows

    cross_pairs(places, helper_n, queries, table, arrived, put)
    for k, out in enumerate(outs):
        out[first:] = held[jnp.bitwise_xor(helper, k)]


def side_rows(block):
    row_n = block.shape[1] * 2 // 3
    main, tail = block[:, :row_n, :], block[:, row_n:, :]
    tail = jnp.concatenate([tail[:, :, :HEAD], tail[:, :, HEAD:]], 1)
    return jnp.concatenate([main.reshape(-1, LANES), tail.reshape(-1, HEAD)], 1)


def out_kernel(swaps, owner_n, helper_n, partners, own_rows, *rest):
    sides, rest = rest[:helper_n], rest[helper_n:]
    weights, rest = rest[:helper_n], rest[helper_n:]
    out, term_ref, partners_s, sem = rest
    copy = pltpu.make_async_copy(partners, partners_s, sem)
    copy.start()
    image_n, row_n, width = own_rows.shape
    terms = None
    for side, weight in zip(sides, weights):
        part = nn(side_rows(side[...]), weight[...])
        terms = part if terms is None else terms + part
    term_ref[...] = terms.reshape(len(swaps), row_n, width)
    copy.wait()
    me = lax.axis_index("owner")
    lows = [swap_target(me, swap, owner_n) * image_n for swap in swaps]
    for image in range(image_n):
        for slot in range(partners.shape[1]):
            partner = partners_s[image, slot]
            which = jnp.int32(0)
            for at, low in enumerate(lows):
                gap = partner - low
                which = jnp.where(jnp.logical_and(gap >= 0, gap < image_n), jnp.int32(at), which)
            value = (own_rows[image] + term_ref[which]).astype(BF16)
            out[image, slot] = jnp.where(partner >= 0, value, jnp.zeros_like(value))


def local(owner_n, helper_n, states, partners, self_proj, self_out, cross_proj, cross_out, gains):
    image_n, patch_n, width = states.shape
    slot_n = partners.shape[1]
    columns = self_proj.shape[2]
    row_n = patch_n // helper_n
    row_all = image_n * patch_n
    swaps = owner_swaps(slot_n, owner_n)
    pair_n = len(swaps)
    self_proj_t = jnp.swapaxes(self_proj, 1, 2)
    cross_proj_t = jnp.swapaxes(cross_proj, 1, 2)
    chip_hop, core_hop = helper_n // 2, 1

    def across(value, k):
        return lax.ppermute(value, "helper", [(j, j ^ k) for j in range(helper_n)])

    def exchange(value, swap):
        return lax.ppermute(value, "owner", [(o, swap_target(o, swap, owner_n)) for o in range(owner_n)])

    def call(name, kernel, out_shape, in_specs, scratch, *operands, flops=1):
        with jax.named_scope(name):
            return pl.pallas_call(
                kernel,
                out_shape=out_shape,
                in_specs=in_specs,
                out_specs=jax.tree.map(lambda _: VMEM, out_shape),
                scratch_shapes=scratch,
                compiler_params=pltpu.CompilerParams(vmem_limit_bytes=VMEM_BYTES),
                cost_estimate=pl.CostEstimate(flops=flops, bytes_accessed=1, transcendentals=0),
            )(*operands)

    shape = jax.ShapeDtypeStruct
    dma = pltpu.SemaphoreType.DMA
    index_table = pltpu.SMEM(partners.shape, jnp.int32)
    block = shape((2 * columns, patch_n), BF16)

    partners_h = pltpu.with_memory_space_constraint(partners, pltpu.HBM)
    self_out_got = across(self_out, chip_hop)
    *outgoing, context, table, cross_out_own = call(
        "own_images",
        functools.partial(own_images_kernel, swaps, owner_n),
        [block] * pair_n
        + [
            shape((row_all * columns // LANES, LANES), BF16),
            shape((pair_n, LANES), jnp.int32),
            shape(cross_out.shape, BF16),
        ],
        [HBM] * 6,
        [
            pltpu.VMEM(states.shape, BF16),
            pltpu.VMEM(gains.shape, F32),
            pltpu.VMEM((3, columns, width), BF16),
            pltpu.VMEM((2, columns, width), BF16),
            index_table,
            pltpu.VMEM((image_n, 2 * columns, patch_n), BF16),
            dma((6,)),
        ],
        *[pltpu.with_memory_space_constraint(x, pltpu.HBM) for x in (states, gains, self_proj_t, cross_proj_t)],
        partners_h,
        pltpu.with_memory_space_constraint(cross_out, pltpu.HBM),
    )
    context_got = across(context, chip_hop)
    arrived = [exchange(value, swap) for value, swap in zip(outgoing, swaps)]
    late = [at for at, (_, colour) in enumerate(swaps) if colour]
    early = [at for at in range(pair_n) if at not in late]
    cross_out_sent = call(
        "cross_output_rows",
        hand_on_kernel,
        shape(cross_out.shape, BF16),
        [ANY, ANY],
        [dma],
        cross_out_own, context_got,
    )
    cross_out_got = across(cross_out_sent, chip_hop)

    base, sent = call(
        "self_output_share",
        partial_kernel,
        [shape((row_all, width), F32), shape((row_all + columns, width), BF16)],
        [VMEM] * 4 + [ANY, ANY],
        [pltpu.VMEM(self_out.shape, BF16), dma((2,))],
        states, context, context_got, self_out, self_out_got, cross_out_own,
    )
    made_shapes = [
        shape((image_n, row_n, width), F32),
        shape((image_n, patch_n, columns), F32),
        shape(cross_out.shape, BF16),
    ]

    def mixing(base, sent, gains, cross_proj_t, *waited):
        made = call(
            "mixed_and_queries",
            functools.partial(query_kernel, helper_n),
            made_shapes,
            [VMEM] * 4 + [ANY] * len(waited),
            [pltpu.VMEM((image_n, patch_n, width), F32), dma],
            base, across(sent, core_hop), gains, cross_proj_t, *waited,
        )
        return tuple(made)

    def no_images(*operands):
        return tuple(jnp.zeros(made.shape, made.dtype) for made in made_shapes)

    own_rows, queries, cross_out_core = lax.cond(
        lax.axis_index("owner") < owner_n, mixing, no_images,
        base, sent, gains, cross_proj_t, *[arrived[at] for at in early],
    )
    packed = columns * row_n // LANES
    early_sides = call(
        "early_cross_attention",
        functools.partial(cross_kernel, early, helper_n),
        shape((helper_n, len(early), packed, LANES), BF16),
        [VMEM] * (2 + len(early)),
        [],
        queries, table, *[arrived[at] for at in early],
        flops=EARLY_WEIGHT,
    )
    sides = call(
        "late_cross_attention",
        functools.partial(last_cross_kernel, late, helper_n),
        [shape((pair_n, packed, LANES), BF16)] * helper_n,
        [VMEM] * (3 + len(late)),
        [pltpu.VMEM((helper_n, len(late), packed, LANES), BF16)],
        queries, table, early_sides, *[arrived[at] for at in late],
        flops=LATE_WEIGHT,
    )
    sides = [sides[0]] + [across(sides[k], k) for k in range(1, helper_n)]
    weights = {0: cross_out_own, core_hop: cross_out_core, chip_hop: cross_out_got}
    weights[chip_hop ^ core_hop] = across(cross_out_got, core_hop)
    return call(
        "pair_output",
        functools.partial(out_kernel, [swaps[at] for at in early + late], owner_n, helper_n),
        shape((image_n, slot_n, row_n, width), BF16),
        [HBM] + [VMEM] * (1 + 2 * helper_n),
        [pltpu.VMEM((pair_n, row_n, width), F32), index_table, dma],
        partners_h, own_rows, *sides, *[weights[k] for k in range(helper_n)],
    )


def solution(mesh):
    return jax.shard_map(
        functools.partial(local, mesh.shape["owner"], mesh.shape["helper"]),
        mesh=mesh,
        in_specs=(
            P("owner", None, None),
            P("owner", None),
            P(None, None, "helper"),
            P("helper", None),
            P(None, None, "helper"),
            P("helper", None),
            P(),
        ),
        out_specs=P("owner", None, "helper", None),
        check_vma=False,
    )
```

```python
import functools

import jax
import jax.numpy as jnp
from jax import lax
from jax.experimental import pallas as pl
from jax.experimental.pallas import tpu as pltpu
from jax.sharding import PartitionSpec as P

HEAD = 64
LANES = 128
F32 = jnp.float32
BF16 = jnp.bfloat16
VMEM_BYTES = 24 * 1024 * 1024
EARLY_WEIGHT = 1
LATE_WEIGHT = 10**11

VMEM = pl.BlockSpec(memory_space=pltpu.VMEM)
HBM = pl.BlockSpec(memory_space=pltpu.HBM)
ANY = pl.BlockSpec(memory_space=pl.ANY)


def owner_swaps(slot_count, owner_count):
    near = (slot_count - 1) // 2
    swaps = [(owner_count // 2, 0)]
    for k in range(near, 1, -1):
        swaps += [(k, 1), (k, 0)]
    return swaps + [(1, 0), (1, 1)]


def swap_target(owner, swap, owner_count):
    distance, colour = swap
    step = distance & -distance
    if isinstance(owner, int):
        up = (owner // step) % 2 == colour
        return (owner + (distance if up else owner_count - distance)) % owner_count
    up = jnp.bitwise_and(lax.shift_right_logical(owner, step.bit_length() - 1), 1) == colour
    return lax.rem(owner + jnp.where(up, distance, owner_count - distance), owner_count)


def nn(left, right):
    return lax.dot_general(left, right, (((1,), (0,)), ((), ())), preferred_element_type=F32)


def nt(left, right):
    return lax.dot_general(left, right, (((1,), (1,)), ((), ())), preferred_element_type=F32)


def norm_core(values):
    row_mean = jnp.mean(values, -1, keepdims=True)
    centred = values - row_mean
    row_var = jnp.mean(centred * centred, -1, keepdims=True)
    return centred * lax.rsqrt(row_var + 1e-05)


def head_stack(queries):
    head_of = lax.broadcasted_iota(jnp.int32, queries.shape, 1) // HEAD
    zero = jnp.zeros((), queries.dtype)
    return jnp.concatenate(
        [jnp.where(head_of == h, queries, zero) for h in range(queries.shape[1] // HEAD)], 0
    ).astype(BF16)


def attend(stacked, keys_t, values_t):
    column_n = keys_t.shape[0]
    head_n = column_n // HEAD
    row_n = stacked.shape[0] // head_n
    scores = nn(stacked, keys_t)
    powers = jnp.exp(scores - jnp.max(scores, -1, keepdims=True))
    weights = (powers * (1.0 / jnp.sum(powers, -1, keepdims=True))).astype(BF16)
    spread = nt(weights, values_t)
    head_of = lax.broadcasted_iota(jnp.int32, (row_n, column_n), 1) // HEAD
    context = spread[(head_n - 1) * row_n :]
    for h in range(head_n - 1):
        context = jnp.where(head_of == h, spread[h * row_n : (h + 1) * row_n], context)
    return context


def pack(block):
    row_n = block.shape[0]
    tail = block[:, LANES:]
    return jnp.concatenate(
        [block[:, :LANES], jnp.concatenate([tail[: row_n // 2], tail[row_n // 2 :]], 1)], 0
    ).astype(BF16)


def joined_image(partners, owner, image_n):
    low = owner * image_n
    found = jnp.int32(0)
    for image in range(1, image_n):
        for slot in range(partners.shape[1]):
            gap = partners[image, slot] - low
            found = jnp.where(jnp.logical_and(gap >= 0, gap < image_n), jnp.int32(image), found)
    return found


def own_images_kernel(swaps, owner_n, states, gains, self_t, cross_t, partners, weight, *rest):
    outs, rest = rest[: len(swaps)], rest[len(swaps) :]
    context_out, table, weight_out, states_v, gains_v, self_v, cross_v, partners_s, held, sems = rest
    image_n, patch_n, width = states.shape
    columns = self_t.shape[1]
    copies = [
        pltpu.make_async_copy(states, states_v, sems.at[0]),
        pltpu.make_async_copy(gains, gains_v, sems.at[1]),
        pltpu.make_async_copy(cross_t.at[pl.ds(1, 2)], cross_v, sems.at[2]),
        pltpu.make_async_copy(partners, partners_s, sems.at[3]),
        pltpu.make_async_copy(self_t, self_v, sems.at[4]),
        pltpu.make_async_copy(weight, weight_out, sems.at[5]),
    ]
    for copy in copies:
        copy.start()
    copies[0].wait()
    rows = norm_core(states_v[...].reshape(image_n * patch_n, width).astype(F32))
    copies[1].wait()
    normed = (rows * gains_v[2:3, :]).astype(BF16)
    copies[2].wait()
    projected = nt(cross_v[...].reshape(2 * columns, width), normed).astype(BF16)
    for image in range(image_n):
        held[image] = projected[:, image * patch_n : (image + 1) * patch_n]
    copies[3].wait()
    me = lax.axis_index("owner")
    for at, (out, swap) in enumerate(zip(outs, swaps)):
        image = joined_image(partners_s, swap_target(me, swap, owner_n), image_n)
        out[...] = held[image]
        table[at : at + 1, :] = jnp.full((1, LANES), image, jnp.int32)
    normed = (rows * gains_v[0:1, :]).astype(BF16)
    copies[4].wait()
    queries = nt(normed, self_v[0]).astype(BF16).astype(F32) * HEAD ** (-0.5)
    key_value = nt(self_v[1:3].reshape(2 * columns, width), normed).astype(BF16)
    contexts = []
    for image in range(image_n):
        span = slice(image * patch_n, (image + 1) * patch_n)
        contexts.append(
            attend(head_stack(queries[span]), key_value[:columns, span], key_value[columns:, span])
        )
    context_out[...] = pack(jnp.concatenate(contexts, 0))
    copies[5].wait()


def unpack(block):
    row_n = block.shape[0] * 2 // 3
    tail = block[row_n:, :]
    return jnp.concatenate(
        [block[:row_n, :], jnp.concatenate([tail[:, :HEAD], tail[:, HEAD:]], 0)], 1
    )


def partial_kernel(states, own, got, own_weight, got_weight, cross_out, *rest):
    base, sent, sem = rest[-3:]
    row_all = base.shape[0]
    copy = pltpu.make_async_copy(cross_out, sent.at[pl.ds(row_all, cross_out.shape[0])], sem)
    copy.start()
    rows = jnp.concatenate([unpack(own[...]), unpack(got[...])], 1)
    part = nn(rows, jnp.concatenate([own_weight[...], got_weight[...]], 0))
    sent[:row_all, :] = part.astype(BF16)
    base[...] = states[...].reshape(part.shape).astype(F32) + part
    copy.wait()


def query_kernel(helper_n, base, got, gains, proj_t, own_rows, queries_out, mixed_ref):
    mixed = base[...] + got[: base.shape[0], :].astype(F32)
    image_n, row_n, width = own_rows.shape
    patch_n = row_n * helper_n
    mixed_ref[...] = mixed.reshape(image_n, patch_n, width)
    normed = (norm_core(mixed) * gains[1:2, :]).astype(BF16)
    queries = nt(normed, proj_t[0]).astype(BF16).astype(F32) * HEAD ** (-0.5)
    queries_out[...] = queries.reshape(queries_out.shape)
    start = pl.multiple_of(lax.axis_index("helper") * row_n, row_n)
    own_rows[...] = mixed_ref[:, pl.ds(start, row_n), :]


def hand_on_kernel(weight, waited, out, sem):
    del waited
    copy = pltpu.make_async_copy(weight, out, sem)
    copy.start()
    copy.wait()


def cross_pairs(places, helper_n, queries, table, arrived, put):
    for at, (place, block) in enumerate(zip(places, arrived)):
        chosen = queries[0]
        for image in range(1, queries.shape[0]):
            chosen = jnp.where(table[place : place + 1, 0:1] == image, queries[image], chosen)
        columns = block.shape[0] // 2
        context = attend(head_stack(chosen), block[:columns, :], block[columns:, :])
        row_n = context.shape[0] // helper_n
        for helper in range(helper_n):
            put(at, helper, pack(context[helper * row_n : (helper + 1) * row_n]))


def cross_kernel(places, helper_n, queries, table, *rest):
    *arrived, out = rest

    def put(at, helper, rows):
        out[helper, at] = rows

    cross_pairs(places, helper_n, queries, table, arrived, put)


def last_cross_kernel(places, helper_n, queries, table, before, *rest):
    arrived, (*outs, held) = rest[: len(places)], rest[len(places) :]
    first = before.shape[1]
    helper = lax.axis_index("helper")
    for k, out in enumerate(outs):
        out[:first] = before[jnp.bitwise_xor(helper, k)]

    def put(at, helper, rows):
        held[helper, at] = rows

    cross_pairs(places, helper_n, queries, table, arrived, put)
    for k, out in enumerate(outs):
        out[first:] = held[jnp.bitwise_xor(helper, k)]


def side_rows(block):
    row_n = block.shape[1] * 2 // 3
    main, tail = block[:, :row_n, :], block[:, row_n:, :]
    tail = jnp.concatenate([tail[:, :, :HEAD], tail[:, :, HEAD:]], 1)
    return jnp.concatenate([main.reshape(-1, LANES), tail.reshape(-1, HEAD)], 1)


def out_kernel(swaps, owner_n, helper_n, partners, own_rows, *rest):
    sides, rest = rest[:helper_n], rest[helper_n:]
    weights, rest = rest[:helper_n], rest[helper_n:]
    out, term_ref, partners_s, sem = rest
    copy = pltpu.make_async_copy(partners, partners_s, sem)
    copy.start()
    image_n, row_n, width = own_rows.shape
    columns = HEAD + LANES
    terms = None
    for side, weight in zip(sides, weights):
        part = nn(side_rows(side[...]), weight[weight.shape[0] - columns :, :])
        terms = part if terms is None else terms + part
    term_ref[...] = terms.reshape(len(swaps), row_n, width)
    copy.wait()
    me = lax.axis_index("owner")
    lows = [swap_target(me, swap, owner_n) * image_n for swap in swaps]
    for image in range(image_n):
        for slot in range(partners.shape[1]):
            partner = partners_s[image, slot]
            which = jnp.int32(0)
            for at, low in enumerate(lows):
                gap = partner - low
                which = jnp.where(jnp.logical_and(gap >= 0, gap < image_n), jnp.int32(at), which)
            value = (own_rows[image] + term_ref[which]).astype(BF16)
            out[image, slot] = jnp.where(partner >= 0, value, jnp.zeros_like(value))


def local(owner_n, helper_n, states, partners, self_proj, self_out, cross_proj, cross_out, gains):
    image_n, patch_n, width = states.shape
    slot_n = partners.shape[1]
    columns = self_proj.shape[2]
    row_n = patch_n // helper_n
    row_all = image_n * patch_n
    swaps = owner_swaps(slot_n, owner_n)
    pair_n = len(swaps)
    self_proj_t = jnp.swapaxes(self_proj, 1, 2)
    cross_proj_t = jnp.swapaxes(cross_proj, 1, 2)
    chip_hop, core_hop = helper_n // 2, 1

    def across(value, k):
        return lax.ppermute(value, "helper", [(j, j ^ k) for j in range(helper_n)])

    def exchange(value, swap):
        return lax.ppermute(value, "owner", [(o, swap_target(o, swap, owner_n)) for o in range(owner_n)])

    def call(name, kernel, out_shape, in_specs, scratch, *operands, flops=1):
        with jax.named_scope(name):
            return pl.pallas_call(
                kernel,
                out_shape=out_shape,
                in_specs=in_specs,
                out_specs=jax.tree.map(lambda _: VMEM, out_shape),
                scratch_shapes=scratch,
                compiler_params=pltpu.CompilerParams(vmem_limit_bytes=VMEM_BYTES),
                cost_estimate=pl.CostEstimate(flops=flops, bytes_accessed=1, transcendentals=0),
            )(*operands)

    shape = jax.ShapeDtypeStruct
    dma = pltpu.SemaphoreType.DMA
    index_table = pltpu.SMEM(partners.shape, jnp.int32)
    block = shape((2 * columns, patch_n), BF16)

    partners_h = pltpu.with_memory_space_constraint(partners, pltpu.HBM)
    self_out_got = across(self_out, chip_hop)
    *outgoing, context, table, cross_out_own = call(
        "own_images",
        functools.partial(own_images_kernel, swaps, owner_n),
        [block] * pair_n
        + [
            shape((row_all * columns // LANES, LANES), BF16),
            shape((pair_n, LANES), jnp.int32),
            shape(cross_out.shape, BF16),
        ],
        [HBM] * 6,
        [
            pltpu.VMEM(states.shape, BF16),
            pltpu.VMEM(gains.shape, F32),
            pltpu.VMEM((3, columns, width), BF16),
            pltpu.VMEM((2, columns, width), BF16),
            index_table,
            pltpu.VMEM((image_n, 2 * columns, patch_n), BF16),
            dma((6,)),
        ],
        *[pltpu.with_memory_space_constraint(x, pltpu.HBM) for x in (states, gains, self_proj_t, cross_proj_t)],
        partners_h,
        pltpu.with_memory_space_constraint(cross_out, pltpu.HBM),
    )
    context_got = across(context, chip_hop)
    arrived = [exchange(value, swap) for value, swap in zip(outgoing, swaps)]
    late = [at for at, (_, colour) in enumerate(swaps) if colour]
    early = [at for at in range(pair_n) if at not in late]
    cross_out_sent = call(
        "cross_output_rows",
        hand_on_kernel,
        shape(cross_out.shape, BF16),
        [ANY, ANY],
        [dma],
        cross_out_own, context_got,
    )
    cross_out_got = across(cross_out_sent, chip_hop)

    base, sent = call(
        "self_output_share",
        partial_kernel,
        [shape((row_all, width), F32), shape((row_all + columns, width), BF16)],
        [VMEM] * 5 + [ANY] * (1 + len(early)),
        [dma],
        states, context, context_got, self_out, self_out_got, cross_out_own, *[arrived[at] for at in early],
    )
    got = across(sent, core_hop)
    own_rows, queries = call(
        "mixed_and_queries",
        functools.partial(query_kernel, helper_n),
        [shape((image_n, row_n, width), F32), shape((image_n, patch_n, columns), F32)],
        [VMEM] * 4,
        [pltpu.VMEM((image_n, patch_n, width), F32)],
        base, got, gains, cross_proj_t,
    )
    packed = columns * row_n // LANES
    early_sides = call(
        "early_cross_attention",
        functools.partial(cross_kernel, early, helper_n),
        shape((helper_n, len(early), packed, LANES), BF16),
        [VMEM] * (2 + len(early)),
        [],
        queries, table, *[arrived[at] for at in early],
        flops=EARLY_WEIGHT,
    )
    sides = call(
        "late_cross_attention",
        functools.partial(last_cross_kernel, late, helper_n),
        [shape((pair_n, packed, LANES), BF16)] * helper_n,
        [VMEM] * (3 + len(late)),
        [pltpu.VMEM((helper_n, len(late), packed, LANES), BF16)],
        queries, table, early_sides, *[arrived[at] for at in late],
        flops=LATE_WEIGHT,
    )
    sides = [sides[0]] + [across(sides[k], k) for k in range(1, helper_n)]
    weights = {0: cross_out_own, core_hop: got, chip_hop: cross_out_got}
    cross_out_far = call(
        "cross_output_far_rows",
        hand_on_kernel,
        shape(cross_out.shape, BF16),
        [ANY, ANY],
        [dma],
        cross_out_got, early_sides,
    )
    weights[chip_hop ^ core_hop] = across(cross_out_far, core_hop)
    return call(
        "pair_output",
        functools.partial(out_kernel, [swaps[at] for at in early + late], owner_n, helper_n),
        shape((image_n, slot_n, row_n, width), BF16),
        [HBM] + [VMEM] * (1 + 2 * helper_n),
        [pltpu.VMEM((pair_n, row_n, width), F32), index_table, dma],
        partners_h, own_rows, *sides, *[weights[k] for k in range(helper_n)],
    )


def solution(mesh):
    return jax.shard_map(
        functools.partial(local, mesh.shape["owner"], mesh.shape["helper"]),
        mesh=mesh,
        in_specs=(
            P("owner", None, None),
            P("owner", None),
            P(None, None, "helper"),
            P("helper", None),
            P(None, None, "helper"),
            P("helper", None),
            P(),
        ),
        out_specs=P("owner", None, "helper", None),
        check_vma=False,
    )
```

```python
import functools

import jax
import jax.numpy as jnp
from jax import lax
from jax.experimental import pallas as pl
from jax.experimental.pallas import tpu as pltpu
from jax.sharding import PartitionSpec as P

HEAD = 64
LANES = 128
F32 = jnp.float32
BF16 = jnp.bfloat16
VMEM_BYTES = 24 * 1024 * 1024
EARLY_WEIGHT = 10**11
LATE_WEIGHT = 10**11

VMEM = pl.BlockSpec(memory_space=pltpu.VMEM)
HBM = pl.BlockSpec(memory_space=pltpu.HBM)
ANY = pl.BlockSpec(memory_space=pl.ANY)


def owner_swaps(slot_count, owner_count):
    near = (slot_count - 1) // 2
    swaps = [(owner_count // 2, 0)]
    for k in range(near, 1, -1):
        swaps += [(k, 1), (k, 0)]
    return swaps + [(1, 0), (1, 1)]


def swap_target(owner, swap, owner_count):
    distance, colour = swap
    step = distance & -distance
    if isinstance(owner, int):
        up = (owner // step) % 2 == colour
        return (owner + (distance if up else owner_count - distance)) % owner_count
    up = jnp.bitwise_and(lax.shift_right_logical(owner, step.bit_length() - 1), 1) == colour
    return lax.rem(owner + jnp.where(up, distance, owner_count - distance), owner_count)


def nn(left, right):
    return lax.dot_general(left, right, (((1,), (0,)), ((), ())), preferred_element_type=F32)


def nt(left, right):
    return lax.dot_general(left, right, (((1,), (1,)), ((), ())), preferred_element_type=F32)


def norm_core(values):
    row_mean = jnp.mean(values, -1, keepdims=True)
    centred = values - row_mean
    row_var = jnp.mean(centred * centred, -1, keepdims=True)
    return centred * lax.rsqrt(row_var + 1e-05)


def head_stack(queries):
    head_of = lax.broadcasted_iota(jnp.int32, queries.shape, 1) // HEAD
    zero = jnp.zeros((), queries.dtype)
    return jnp.concatenate(
        [jnp.where(head_of == h, queries, zero) for h in range(queries.shape[1] // HEAD)], 0
    ).astype(BF16)


def attend(stacked, keys_t, values_t):
    column_n = keys_t.shape[0]
    head_n = column_n // HEAD
    row_n = stacked.shape[0] // head_n
    scores = nn(stacked, keys_t)
    powers = jnp.exp(scores - jnp.max(scores, -1, keepdims=True))
    weights = (powers * (1.0 / jnp.sum(powers, -1, keepdims=True))).astype(BF16)
    spread = nt(weights, values_t)
    head_of = lax.broadcasted_iota(jnp.int32, (row_n, column_n), 1) // HEAD
    context = spread[(head_n - 1) * row_n :]
    for h in range(head_n - 1):
        context = jnp.where(head_of == h, spread[h * row_n : (h + 1) * row_n], context)
    return context


def pack(block):
    row_n = block.shape[0]
    tail = block[:, LANES:]
    return jnp.concatenate(
        [block[:, :LANES], jnp.concatenate([tail[: row_n // 2], tail[row_n // 2 :]], 1)], 0
    ).astype(BF16)


def joined_image(partners, owner, image_n):
    low = owner * image_n
    found = jnp.int32(0)
    for image in range(1, image_n):
        for slot in range(partners.shape[1]):
            gap = partners[image, slot] - low
            found = jnp.where(jnp.logical_and(gap >= 0, gap < image_n), jnp.int32(image), found)
    return found


def own_images_kernel(swaps, owner_n, states, gains, self_t, cross_t, partners, weight, *rest):
    outs, rest = rest[: len(swaps)], rest[len(swaps) :]
    context_out, table, weight_out, states_v, gains_v, self_v, cross_v, partners_s, held, sems = rest
    image_n, patch_n, width = states.shape
    columns = self_t.shape[1]
    copies = [
        pltpu.make_async_copy(states, states_v, sems.at[0]),
        pltpu.make_async_copy(gains, gains_v, sems.at[1]),
        pltpu.make_async_copy(cross_t.at[pl.ds(1, 2)], cross_v, sems.at[2]),
        pltpu.make_async_copy(partners, partners_s, sems.at[3]),
        pltpu.make_async_copy(self_t, self_v, sems.at[4]),
        pltpu.make_async_copy(weight, weight_out, sems.at[5]),
    ]
    for copy in copies:
        copy.start()
    copies[0].wait()
    rows = norm_core(states_v[...].reshape(image_n * patch_n, width).astype(F32))
    copies[1].wait()
    normed = (rows * gains_v[2:3, :]).astype(BF16)
    copies[2].wait()
    projected = nt(cross_v[...].reshape(2 * columns, width), normed).astype(BF16)
    for image in range(image_n):
        held[image] = projected[:, image * patch_n : (image + 1) * patch_n]
    copies[3].wait()
    me = lax.axis_index("owner")
    for at, (out, swap) in enumerate(zip(outs, swaps)):
        image = joined_image(partners_s, swap_target(me, swap, owner_n), image_n)
        out[...] = held[image]
        table[at : at + 1, :] = jnp.full((1, LANES), image, jnp.int32)
    normed = (rows * gains_v[0:1, :]).astype(BF16)
    copies[4].wait()
    queries = nt(normed, self_v[0]).astype(BF16).astype(F32) * HEAD ** (-0.5)
    key_value = nt(self_v[1:3].reshape(2 * columns, width), normed).astype(BF16)
    contexts = []
    for image in range(image_n):
        span = slice(image * patch_n, (image + 1) * patch_n)
        contexts.append(
            attend(head_stack(queries[span]), key_value[:columns, span], key_value[columns:, span])
        )
    context_out[...] = pack(jnp.concatenate(contexts, 0))
    copies[5].wait()


def unpack(block):
    row_n = block.shape[0] * 2 // 3
    tail = block[row_n:, :]
    return jnp.concatenate(
        [block[:row_n, :], jnp.concatenate([tail[:, :HEAD], tail[:, HEAD:]], 0)], 1
    )


def partial_kernel(states, own, got, own_weight, got_weight, cross_out, base, sent, sem):
    row_all = base.shape[0]
    copy = pltpu.make_async_copy(cross_out, sent.at[pl.ds(row_all, cross_out.shape[0])], sem)
    copy.start()
    rows = jnp.concatenate([unpack(own[...]), unpack(got[...])], 1)
    part = nn(rows, jnp.concatenate([own_weight[...], got_weight[...]], 0))
    sent[:row_all, :] = part.astype(BF16)
    base[...] = states[...].reshape(part.shape).astype(F32) + part
    copy.wait()


def query_kernel(helper_n, base, got, gains, proj_t, own_rows, queries_out, weight_out, mixed_ref, sem):
    copy = pltpu.make_async_copy(got.at[pl.ds(base.shape[0], weight_out.shape[0])], weight_out, sem)
    copy.start()
    mixed = base[...] + got[: base.shape[0], :].astype(F32)
    image_n, row_n, width = own_rows.shape
    patch_n = row_n * helper_n
    mixed_ref[...] = mixed.reshape(image_n, patch_n, width)
    normed = (norm_core(mixed) * gains[1:2, :]).astype(BF16)
    queries = nt(normed, proj_t[0]).astype(BF16).astype(F32) * HEAD ** (-0.5)
    queries_out[...] = queries.reshape(queries_out.shape)
    start = pl.multiple_of(lax.axis_index("helper") * row_n, row_n)
    own_rows[...] = mixed_ref[:, pl.ds(start, row_n), :]
    copy.wait()


def hand_on_kernel(weight, *rest):
    out, sem = rest[-2:]
    copy = pltpu.make_async_copy(weight, out, sem)
    copy.start()
    copy.wait()


def cross_pairs(places, helper_n, queries, table, arrived, put):
    for at, (place, block) in enumerate(zip(places, arrived)):
        chosen = queries[0]
        for image in range(1, queries.shape[0]):
            chosen = jnp.where(table[place : place + 1, 0:1] == image, queries[image], chosen)
        columns = block.shape[0] // 2
        context = attend(head_stack(chosen), block[:columns, :], block[columns:, :])
        row_n = context.shape[0] // helper_n
        for helper in range(helper_n):
            put(at, helper, pack(context[helper * row_n : (helper + 1) * row_n]))


def cross_kernel(places, helper_n, queries, table, *rest):
    *arrived, out = rest

    def put(at, helper, rows):
        out[helper, at] = rows

    cross_pairs(places, helper_n, queries, table, arrived, put)


def last_cross_kernel(places, helper_n, queries, table, before, *rest):
    arrived, (*outs, held) = rest[: len(places)], rest[len(places) :]
    first = before.shape[1]
    helper = lax.axis_index("helper")
    for k, out in enumerate(outs):
        out[:first] = before[jnp.bitwise_xor(helper, k)]

    def put(at, helper, rows):
        held[helper, at] = rows

    cross_pairs(places, helper_n, queries, table, arrived, put)
    for k, out in enumerate(outs):
        out[first:] = held[jnp.bitwise_xor(helper, k)]


def side_rows(block):
    row_n = block.shape[1] * 2 // 3
    main, tail = block[:, :row_n, :], block[:, row_n:, :]
    tail = jnp.concatenate([tail[:, :, :HEAD], tail[:, :, HEAD:]], 1)
    return jnp.concatenate([main.reshape(-1, LANES), tail.reshape(-1, HEAD)], 1)


def out_kernel(swaps, owner_n, helper_n, partners, own_rows, *rest):
    sides, rest = rest[:helper_n], rest[helper_n:]
    weights, rest = rest[:helper_n], rest[helper_n:]
    out, term_ref, partners_s, sem = rest
    copy = pltpu.make_async_copy(partners, partners_s, sem)
    copy.start()
    image_n, row_n, width = own_rows.shape
    terms = None
    for side, weight in zip(sides, weights):
        part = nn(side_rows(side[...]), weight[...])
        terms = part if terms is None else terms + part
    term_ref[...] = terms.reshape(len(swaps), row_n, width)
    copy.wait()
    me = lax.axis_index("owner")
    lows = [swap_target(me, swap, owner_n) * image_n for swap in swaps]
    for image in range(image_n):
        for slot in range(partners.shape[1]):
            partner = partners_s[image, slot]
            which = jnp.int32(0)
            for at, low in enumerate(lows):
                gap = partner - low
                which = jnp.where(jnp.logical_and(gap >= 0, gap < image_n), jnp.int32(at), which)
            value = (own_rows[image] + term_ref[which]).astype(BF16)
            out[image, slot] = jnp.where(partner >= 0, value, jnp.zeros_like(value))


def local(owner_n, helper_n, states, partners, self_proj, self_out, cross_proj, cross_out, gains):
    image_n, patch_n, width = states.shape
    slot_n = partners.shape[1]
    columns = self_proj.shape[2]
    row_n = patch_n // helper_n
    row_all = image_n * patch_n
    swaps = owner_swaps(slot_n, owner_n)
    pair_n = len(swaps)
    self_proj_t = jnp.swapaxes(self_proj, 1, 2)
    cross_proj_t = jnp.swapaxes(cross_proj, 1, 2)
    chip_hop, core_hop = helper_n // 2, 1

    def across(value, k):
        return lax.ppermute(value, "helper", [(j, j ^ k) for j in range(helper_n)])

    def exchange(value, swap):
        return lax.ppermute(value, "owner", [(o, swap_target(o, swap, owner_n)) for o in range(owner_n)])

    def call(name, kernel, out_shape, in_specs, scratch, *operands, flops=1):
        with jax.named_scope(name):
            return pl.pallas_call(
                kernel,
                out_shape=out_shape,
                in_specs=in_specs,
                out_specs=jax.tree.map(lambda _: VMEM, out_shape),
                scratch_shapes=scratch,
                compiler_params=pltpu.CompilerParams(vmem_limit_bytes=VMEM_BYTES),
                cost_estimate=pl.CostEstimate(flops=flops, bytes_accessed=1, transcendentals=0),
            )(*operands)

    shape = jax.ShapeDtypeStruct
    dma = pltpu.SemaphoreType.DMA
    index_table = pltpu.SMEM(partners.shape, jnp.int32)
    block = shape((2 * columns, patch_n), BF16)

    partners_h = pltpu.with_memory_space_constraint(partners, pltpu.HBM)
    self_out_got = across(self_out, chip_hop)
    *outgoing, context, table, cross_out_own = call(
        "own_images",
        functools.partial(own_images_kernel, swaps, owner_n),
        [block] * pair_n
        + [
            shape((row_all * columns // LANES, LANES), BF16),
            shape((pair_n, LANES), jnp.int32),
            shape(cross_out.shape, BF16),
        ],
        [HBM] * 6,
        [
            pltpu.VMEM(states.shape, BF16),
            pltpu.VMEM(gains.shape, F32),
            pltpu.VMEM((3, columns, width), BF16),
            pltpu.VMEM((2, columns, width), BF16),
            index_table,
            pltpu.VMEM((image_n, 2 * columns, patch_n), BF16),
            dma((6,)),
        ],
        *[pltpu.with_memory_space_constraint(x, pltpu.HBM) for x in (states, gains, self_proj_t, cross_proj_t)],
        partners_h,
        pltpu.with_memory_space_constraint(cross_out, pltpu.HBM),
    )
    context_got = across(context, chip_hop)
    arrived = [exchange(value, swap) for value, swap in zip(outgoing, swaps)]
    near = (slot_n - 1) // 2
    late = [at for at, (_, colour) in enumerate(swaps) if colour]
    early = [at for at in range(pair_n) if at not in late]
    short = [2 * near - 2, 2 * near - 1]
    before = [context_got, self_out_got] + [arrived[at] for at in short]
    cross_out_sent = call(
        "cross_output_rows",
        hand_on_kernel,
        shape(cross_out.shape, BF16),
        [ANY] * (1 + len(before)),
        [dma],
        cross_out_own, *before,
    )
    cross_out_got = across(cross_out_sent, chip_hop)

    made_shapes = [
        shape((image_n, row_n, width), F32),
        shape((image_n, patch_n, columns), F32),
        shape(cross_out.shape, BF16),
    ]

    def mixing(states, gains, cross_proj_t, context, context_got, self_out, self_out_got, cross_out):
        base, sent = call(
            "self_output_share",
            partial_kernel,
            [shape((row_all, width), F32), shape((row_all + columns, width), BF16)],
            [VMEM] * 5 + [ANY],
            [dma],
            states, context, context_got, self_out, self_out_got, cross_out,
        )
        made = call(
            "mixed_and_queries",
            functools.partial(query_kernel, helper_n),
            made_shapes,
            [VMEM] * 4,
            [pltpu.VMEM((image_n, patch_n, width), F32), dma],
            base, across(sent, core_hop), gains, cross_proj_t,
        )
        return tuple(made)

    def no_images(*operands):
        return tuple(jnp.zeros(made.shape, made.dtype) for made in made_shapes)

    own_rows, queries, cross_out_core = lax.cond(
        lax.axis_index("owner") < owner_n, mixing, no_images,
        states, gains, cross_proj_t, context, context_got, self_out, self_out_got, cross_out_own,
    )
    packed = columns * row_n // LANES
    early_sides = call(
        "early_cross_attention",
        functools.partial(cross_kernel, early, helper_n),
        shape((helper_n, len(early), packed, LANES), BF16),
        [VMEM] * (2 + len(early)),
        [],
        queries, table, *[arrived[at] for at in early],
        flops=EARLY_WEIGHT,
    )
    sides = call(
        "late_cross_attention",
        functools.partial(last_cross_kernel, late, helper_n),
        [shape((pair_n, packed, LANES), BF16)] * helper_n,
        [VMEM] * (3 + len(late)),
        [pltpu.VMEM((helper_n, len(late), packed, LANES), BF16)],
        queries, table, early_sides, *[arrived[at] for at in late],
        flops=LATE_WEIGHT,
    )
    sides = [sides[0]] + [across(sides[k], k) for k in range(1, helper_n)]
    weights = {0: cross_out_own, core_hop: cross_out_core, chip_hop: cross_out_got}
    weights[chip_hop ^ core_hop] = across(cross_out_got, core_hop)
    return call(
        "pair_output",
        functools.partial(out_kernel, [swaps[at] for at in early + late], owner_n, helper_n),
        shape((image_n, slot_n, row_n, width), BF16),
        [HBM] + [VMEM] * (1 + 2 * helper_n),
        [pltpu.VMEM((pair_n, row_n, width), F32), index_table, dma],
        partners_h, own_rows, *sides, *[weights[k] for k in range(helper_n)],
    )


def solution(mesh):
    return jax.shard_map(
        functools.partial(local, mesh.shape["owner"], mesh.shape["helper"]),
        mesh=mesh,
        in_specs=(
            P("owner", None, None),
            P("owner", None),
            P(None, None, "helper"),
            P("helper", None),
            P(None, None, "helper"),
            P("helper", None),
            P(),
        ),
        out_specs=P("owner", None, "helper", None),
        check_vma=False,
    )
```

```python
import functools

import jax
import jax.numpy as jnp
from jax import lax
from jax.experimental import pallas as pl
from jax.experimental.pallas import tpu as pltpu
from jax.sharding import PartitionSpec as P

HEAD = 64
LANES = 128
F32 = jnp.float32
BF16 = jnp.bfloat16
VMEM_BYTES = 24 * 1024 * 1024
EARLY_WEIGHT = 10**11
LATE_WEIGHT = 10**11

VMEM = pl.BlockSpec(memory_space=pltpu.VMEM)
HBM = pl.BlockSpec(memory_space=pltpu.HBM)
ANY = pl.BlockSpec(memory_space=pl.ANY)


def owner_swaps(slot_count, owner_count):
    near = (slot_count - 1) // 2
    swaps = [(owner_count // 2, 0)]
    for k in range(near, 1, -1):
        swaps += [(k, 1), (k, 0)]
    return swaps + [(1, 0), (1, 1)]


def swap_target(owner, swap, owner_count):
    distance, colour = swap
    step = distance & -distance
    if isinstance(owner, int):
        up = (owner // step) % 2 == colour
        return (owner + (distance if up else owner_count - distance)) % owner_count
    up = jnp.bitwise_and(lax.shift_right_logical(owner, step.bit_length() - 1), 1) == colour
    return lax.rem(owner + jnp.where(up, distance, owner_count - distance), owner_count)


def nn(left, right):
    return lax.dot_general(left, right, (((1,), (0,)), ((), ())), preferred_element_type=F32)


def nt(left, right):
    return lax.dot_general(left, right, (((1,), (1,)), ((), ())), preferred_element_type=F32)


def norm_core(values):
    row_mean = jnp.mean(values, -1, keepdims=True)
    centred = values - row_mean
    row_var = jnp.mean(centred * centred, -1, keepdims=True)
    return centred * lax.rsqrt(row_var + 1e-05)


def head_stack(queries):
    head_of = lax.broadcasted_iota(jnp.int32, queries.shape, 1) // HEAD
    zero = jnp.zeros((), queries.dtype)
    return jnp.concatenate(
        [jnp.where(head_of == h, queries, zero) for h in range(queries.shape[1] // HEAD)], 0
    ).astype(BF16)


def attend(stacked, keys_t, values_t):
    column_n = keys_t.shape[0]
    head_n = column_n // HEAD
    row_n = stacked.shape[0] // head_n
    scores = nn(stacked, keys_t)
    powers = jnp.exp(scores - jnp.max(scores, -1, keepdims=True))
    weights = (powers * (1.0 / jnp.sum(powers, -1, keepdims=True))).astype(BF16)
    spread = nt(weights, values_t)
    head_of = lax.broadcasted_iota(jnp.int32, (row_n, column_n), 1) // HEAD
    context = spread[(head_n - 1) * row_n :]
    for h in range(head_n - 1):
        context = jnp.where(head_of == h, spread[h * row_n : (h + 1) * row_n], context)
    return context


def pack(block):
    row_n = block.shape[0]
    tail = block[:, LANES:]
    return jnp.concatenate(
        [block[:, :LANES], jnp.concatenate([tail[: row_n // 2], tail[row_n // 2 :]], 1)], 0
    ).astype(BF16)


def joined_image(partners, owner, image_n):
    low = owner * image_n
    found = jnp.int32(0)
    for image in range(1, image_n):
        for slot in range(partners.shape[1]):
            gap = partners[image, slot] - low
            found = jnp.where(jnp.logical_and(gap >= 0, gap < image_n), jnp.int32(image), found)
    return found


def own_images_kernel(swaps, owner_n, states, gains, self_t, cross_t, partners, weight, *rest):
    outs, rest = rest[: len(swaps)], rest[len(swaps) :]
    context_out, table, weight_out, query_weight_out, states_v, gains_v, self_v, cross_v, partners_s, held, sems = rest
    image_n, patch_n, width = states.shape
    columns = self_t.shape[1]
    copies = [
        pltpu.make_async_copy(states, states_v, sems.at[0]),
        pltpu.make_async_copy(gains, gains_v, sems.at[1]),
        pltpu.make_async_copy(cross_t.at[pl.ds(1, 2)], cross_v, sems.at[2]),
        pltpu.make_async_copy(partners, partners_s, sems.at[3]),
        pltpu.make_async_copy(self_t, self_v, sems.at[4]),
        pltpu.make_async_copy(weight, weight_out, sems.at[5]),
        pltpu.make_async_copy(cross_t.at[0], query_weight_out, sems.at[6]),
    ]
    for copy in copies:
        copy.start()
    copies[0].wait()
    rows = norm_core(states_v[...].reshape(image_n * patch_n, width).astype(F32))
    copies[1].wait()
    normed = (rows * gains_v[2:3, :]).astype(BF16)
    copies[2].wait()
    projected = nt(cross_v[...].reshape(2 * columns, width), normed).astype(BF16)
    for image in range(image_n):
        held[image] = projected[:, image * patch_n : (image + 1) * patch_n]
    copies[3].wait()
    me = lax.axis_index("owner")
    for at, (out, swap) in enumerate(zip(outs, swaps)):
        image = joined_image(partners_s, swap_target(me, swap, owner_n), image_n)
        out[...] = held[image]
        table[at : at + 1, :] = jnp.full((1, LANES), image, jnp.int32)
    normed = (rows * gains_v[0:1, :]).astype(BF16)
    copies[4].wait()
    queries = nt(normed, self_v[0]).astype(BF16).astype(F32) * HEAD ** (-0.5)
    key_value = nt(self_v[1:3].reshape(2 * columns, width), normed).astype(BF16)
    contexts = []
    for image in range(image_n):
        span = slice(image * patch_n, (image + 1) * patch_n)
        contexts.append(
            attend(head_stack(queries[span]), key_value[:columns, span], key_value[columns:, span])
        )
    context_out[...] = pack(jnp.concatenate(contexts, 0))
    copies[5].wait()
    copies[6].wait()


def unpack(block):
    row_n = block.shape[0] * 2 // 3
    tail = block[row_n:, :]
    return jnp.concatenate(
        [block[:row_n, :], jnp.concatenate([tail[:, :HEAD], tail[:, HEAD:]], 0)], 1
    )


def partial_kernel(states, own, got, own_weight, got_weight, base, sent):
    rows = jnp.concatenate([unpack(own[...]), unpack(got[...])], 1)
    part = nn(rows, jnp.concatenate([own_weight[...], got_weight[...]], 0))
    sent[...] = part.astype(BF16)
    base[...] = states[...].reshape(part.shape).astype(F32) + part


def query_kernel(helper_n, base, got, gains, weight, own_rows, queries_out, mixed_ref):
    mixed = base[...] + got[...].astype(F32)
    image_n, row_n, width = own_rows.shape
    patch_n = row_n * helper_n
    mixed_ref[...] = mixed.reshape(image_n, patch_n, width)
    normed = (norm_core(mixed) * gains[1:2, :]).astype(BF16)
    queries = nt(normed, weight[...]).astype(BF16).astype(F32) * HEAD ** (-0.5)
    queries_out[...] = queries.reshape(queries_out.shape).astype(BF16)
    start = pl.multiple_of(lax.axis_index("helper") * row_n, row_n)
    own_rows[...] = mixed_ref[:, pl.ds(start, row_n), :]


def hand_on_kernel(*refs):
    del refs


def both_kernel(own, got, waited, out, sems):
    del waited
    row_n = own.shape[0]
    copies = [
        pltpu.make_async_copy(own, out.at[pl.ds(0, row_n)], sems.at[0]),
        pltpu.make_async_copy(got, out.at[pl.ds(row_n, row_n)], sems.at[1]),
    ]
    for copy in copies:
        copy.start()
    for copy in copies:
        copy.wait()


def cross_pairs(places, helper_n, queries, table, arrived, put):
    for at, (place, block) in enumerate(zip(places, arrived)):
        chosen = queries[0].astype(F32)
        for image in range(1, queries.shape[0]):
            chosen = jnp.where(table[place : place + 1, 0:1] == image, queries[image].astype(F32), chosen)
        columns = block.shape[0] // 2
        context = attend(head_stack(chosen), block[:columns, :], block[columns:, :])
        row_n = context.shape[0] // helper_n
        for helper in range(helper_n):
            put(at, helper, pack(context[helper * row_n : (helper + 1) * row_n]))


def cross_kernel(places, helper_n, queries, table, *rest):
    *arrived, out = rest

    def put(at, helper, rows):
        out[helper, at] = rows

    cross_pairs(places, helper_n, queries, table, arrived, put)


def last_cross_kernel(places, helper_n, queries, table, before, *rest):
    arrived, (*outs, held) = rest[: len(places)], rest[len(places) :]
    first = before.shape[1]
    helper = lax.axis_index("helper")
    for k, out in enumerate(outs):
        out[:first] = before[jnp.bitwise_xor(helper, k)]

    def put(at, helper, rows):
        held[helper, at] = rows

    cross_pairs(places, helper_n, queries, table, arrived, put)
    for k, out in enumerate(outs):
        out[first:] = held[jnp.bitwise_xor(helper, k)]


def side_rows(block):
    row_n = block.shape[1] * 2 // 3
    main, tail = block[:, :row_n, :], block[:, row_n:, :]
    tail = jnp.concatenate([tail[:, :, :HEAD], tail[:, :, HEAD:]], 1)
    return jnp.concatenate([main.reshape(-1, LANES), tail.reshape(-1, HEAD)], 1)


def out_kernel(swaps, owner_n, partners, own_rows, own_weights, core_weights, *rest):
    *sides, out, term_ref, partners_s, sem = rest
    copy = pltpu.make_async_copy(partners, partners_s, sem)
    copy.start()
    image_n, row_n, width = own_rows.shape
    half = len(sides) // 2
    rows = [side_rows(side[...]) for side in sides]
    terms = nn(jnp.concatenate(rows[:half], 1), own_weights[...])
    terms = terms + nn(jnp.concatenate(rows[half:], 1), core_weights[...])
    term_ref[...] = terms.reshape(len(swaps), row_n, width)
    copy.wait()
    me = lax.axis_index("owner")
    lows = [swap_target(me, swap, owner_n) * image_n for swap in swaps]
    for image in range(image_n):
        for slot in range(partners.shape[1]):
            partner = partners_s[image, slot]
            which = jnp.int32(0)
            for at, low in enumerate(lows):
                gap = partner - low
                which = jnp.where(jnp.logical_and(gap >= 0, gap < image_n), jnp.int32(at), which)
            value = (own_rows[image] + term_ref[which]).astype(BF16)
            out[image, slot] = jnp.where(partner >= 0, value, jnp.zeros_like(value))


def local(owner_n, helper_n, states, partners, self_proj, self_out, cross_proj, cross_out, gains):
    image_n, patch_n, width = states.shape
    slot_n = partners.shape[1]
    columns = self_proj.shape[2]
    row_n = patch_n // helper_n
    row_all = image_n * patch_n
    swaps = owner_swaps(slot_n, owner_n)
    pair_n = len(swaps)
    self_proj_t = jnp.swapaxes(self_proj, 1, 2)
    cross_proj_t = jnp.swapaxes(cross_proj, 1, 2)
    chip_hop, core_hop = helper_n // 2, 1

    def across(value, k):
        return lax.ppermute(value, "helper", [(j, j ^ k) for j in range(helper_n)])

    def exchange(value, swap):
        return lax.ppermute(value, "owner", [(o, swap_target(o, swap, owner_n)) for o in range(owner_n)])

    def call(name, kernel, out_shape, in_specs, scratch, *operands, flops=1):
        with jax.named_scope(name):
            return pl.pallas_call(
                kernel,
                out_shape=out_shape,
                in_specs=in_specs,
                out_specs=jax.tree.map(lambda _: VMEM, out_shape),
                scratch_shapes=scratch,
                compiler_params=pltpu.CompilerParams(vmem_limit_bytes=VMEM_BYTES),
                cost_estimate=pl.CostEstimate(flops=flops, bytes_accessed=1, transcendentals=0),
            )(*operands)

    shape = jax.ShapeDtypeStruct
    dma = pltpu.SemaphoreType.DMA
    index_table = pltpu.SMEM(partners.shape, jnp.int32)
    block = shape((2 * columns, patch_n), BF16)

    partners_h = pltpu.with_memory_space_constraint(partners, pltpu.HBM)
    self_out_got = across(self_out, chip_hop)
    *outgoing, context, table, cross_out_own, query_weight = call(
        "own_images",
        functools.partial(own_images_kernel, swaps, owner_n),
        [block] * pair_n
        + [
            shape((row_all * columns // LANES, LANES), BF16),
            shape((pair_n, LANES), jnp.int32),
            shape(cross_out.shape, BF16),
            shape((columns, width), BF16),
        ],
        [HBM] * 6,
        [
            pltpu.VMEM(states.shape, BF16),
            pltpu.VMEM(gains.shape, F32),
            pltpu.VMEM((3, columns, width), BF16),
            pltpu.VMEM((2, columns, width), BF16),
            index_table,
            pltpu.VMEM((image_n, 2 * columns, patch_n), BF16),
            dma((7,)),
        ],
        *[pltpu.with_memory_space_constraint(x, pltpu.HBM) for x in (states, gains, self_proj_t, cross_proj_t)],
        partners_h,
        pltpu.with_memory_space_constraint(cross_out, pltpu.HBM),
    )
    context_got = across(context, chip_hop)
    arrived = [exchange(value, swap) for value, swap in zip(outgoing, swaps)]
    near = (slot_n - 1) // 2
    late = [at for at, (_, colour) in enumerate(swaps) if colour]
    early = [at for at in range(pair_n) if at not in late]
    short = [2 * near - 2, 2 * near - 1]
    before = [context_got, self_out_got] + [arrived[at] for at in short]
    cross_out_own = pl.pallas_call(
        hand_on_kernel,
        out_shape=shape(cross_out.shape, BF16),
        in_specs=[ANY] * (1 + len(before)),
        out_specs=ANY,
        input_output_aliases={0: 0},
        name="cross_output_rows",
    )(cross_out_own, *before)
    cross_out_got = across(cross_out_own, chip_hop)

    made_shapes = [
        shape((image_n, row_n, width), F32),
        shape((image_n, patch_n, columns), BF16),
    ]

    def mixing(states, gains, query_weight, context, context_got, self_out, self_out_got):
        base, sent = call(
            "self_output_share",
            partial_kernel,
            [shape((row_all, width), F32), shape((row_all, width), BF16)],
            [VMEM] * 5,
            [],
            states, context, context_got, self_out, self_out_got,
        )
        made = call(
            "mixed_and_queries",
            functools.partial(query_kernel, helper_n),
            made_shapes,
            [VMEM] * 4,
            [pltpu.VMEM((image_n, patch_n, width), F32)],
            base, across(sent, core_hop), gains, query_weight,
        )
        return tuple(made)

    def no_images(*operands):
        return tuple(jnp.zeros(made.shape, made.dtype) for made in made_shapes)

    own_rows, queries = lax.cond(
        lax.axis_index("owner") < owner_n, mixing, no_images,
        states, gains, query_weight, context, context_got, self_out, self_out_got,
    )
    packed = columns * row_n // LANES
    early_sides = call(
        "early_cross_attention",
        functools.partial(cross_kernel, early, helper_n),
        shape((helper_n, len(early), packed, LANES), BF16),
        [VMEM] * (2 + len(early)),
        [],
        queries, table, *[arrived[at] for at in early],
        flops=EARLY_WEIGHT,
    )
    sides = call(
        "late_cross_attention",
        functools.partial(last_cross_kernel, late, helper_n),
        [shape((pair_n, packed, LANES), BF16)] * helper_n,
        [VMEM] * (3 + len(late)),
        [pltpu.VMEM((helper_n, len(late), packed, LANES), BF16)],
        queries, table, early_sides, *[arrived[at] for at in late],
        flops=LATE_WEIGHT,
    )
    sides = [sides[0]] + [across(sides[k], k) for k in range(1, helper_n)]
    cross_out_both = call(
        "cross_output_both_rows",
        both_kernel,
        shape((2 * columns, width), BF16),
        [ANY] * 3,
        [dma((2,))],
        cross_out_own, cross_out_got, early_sides,
    )
    cross_out_core = across(cross_out_both, core_hop)
    return call(
        "pair_output",
        functools.partial(out_kernel, [swaps[at] for at in early + late], owner_n),
        shape((image_n, slot_n, row_n, width), BF16),
        [HBM] + [VMEM] * (3 + helper_n),
        [pltpu.VMEM((pair_n, row_n, width), F32), index_table, dma],
        partners_h, own_rows, cross_out_both, cross_out_core,
        *[sides[k] for k in (0, chip_hop, core_hop, chip_hop ^ core_hop)],
    )


def solution(mesh):
    return jax.shard_map(
        functools.partial(local, mesh.shape["owner"], mesh.shape["helper"]),
        mesh=mesh,
        in_specs=(
            P("owner", None, None),
            P("owner", None),
            P(None, None, "helper"),
            P("helper", None),
            P(None, None, "helper"),
            P("helper", None),
            P(),
        ),
        out_specs=P("owner", None, "helper", None),
        check_vma=False,
    )
```

```python
import functools

import jax
import jax.numpy as jnp
from jax import lax
from jax.experimental import pallas as pl
from jax.experimental.pallas import tpu as pltpu
from jax.sharding import PartitionSpec as P

HEAD = 64
LANES = 128
F32 = jnp.float32
BF16 = jnp.bfloat16
VMEM_BYTES = 24 * 1024 * 1024
EARLY_WEIGHT = 1
LATE_WEIGHT = 10**11

VMEM = pl.BlockSpec(memory_space=pltpu.VMEM)
HBM = pl.BlockSpec(memory_space=pltpu.HBM)
ANY = pl.BlockSpec(memory_space=pl.ANY)


def owner_swaps(slot_count, owner_count):
    near = (slot_count - 1) // 2
    swaps = [(owner_count // 2, 0)]
    for k in range(near, 1, -1):
        swaps += [(k, 1), (k, 0)]
    return swaps + [(1, 0), (1, 1)]


def swap_target(owner, swap, owner_count):
    distance, colour = swap
    step = distance & -distance
    if isinstance(owner, int):
        up = (owner // step) % 2 == colour
        return (owner + (distance if up else owner_count - distance)) % owner_count
    up = jnp.bitwise_and(lax.shift_right_logical(owner, step.bit_length() - 1), 1) == colour
    return lax.rem(owner + jnp.where(up, distance, owner_count - distance), owner_count)


def nn(left, right):
    return lax.dot_general(left, right, (((1,), (0,)), ((), ())), preferred_element_type=F32)


def nt(left, right):
    return lax.dot_general(left, right, (((1,), (1,)), ((), ())), preferred_element_type=F32)


def norm_core(values):
    row_mean = jnp.mean(values, -1, keepdims=True)
    centred = values - row_mean
    row_var = jnp.mean(centred * centred, -1, keepdims=True)
    return centred * lax.rsqrt(row_var + 1e-05)


def head_stack(queries):
    head_of = lax.broadcasted_iota(jnp.int32, queries.shape, 1) // HEAD
    zero = jnp.zeros((), queries.dtype)
    return jnp.concatenate(
        [jnp.where(head_of == h, queries, zero) for h in range(queries.shape[1] // HEAD)], 0
    ).astype(BF16)


def attend(stacked, keys_t, values_t):
    column_n = keys_t.shape[0]
    head_n = column_n // HEAD
    row_n = stacked.shape[0] // head_n
    scores = nn(stacked, keys_t)
    powers = jnp.exp(scores - jnp.max(scores, -1, keepdims=True))
    weights = (powers * (1.0 / jnp.sum(powers, -1, keepdims=True))).astype(BF16)
    spread = nt(weights, values_t)
    head_of = lax.broadcasted_iota(jnp.int32, (row_n, column_n), 1) // HEAD
    context = spread[(head_n - 1) * row_n :]
    for h in range(head_n - 1):
        context = jnp.where(head_of == h, spread[h * row_n : (h + 1) * row_n], context)
    return context


def pack(block):
    row_n = block.shape[0]
    tail = block[:, LANES:]
    return jnp.concatenate(
        [block[:, :LANES], jnp.concatenate([tail[: row_n // 2], tail[row_n // 2 :]], 1)], 0
    ).astype(BF16)


def joined_image(partners, owner, image_n):
    low = owner * image_n
    found = jnp.int32(0)
    for image in range(1, image_n):
        for slot in range(partners.shape[1]):
            gap = partners[image, slot] - low
            found = jnp.where(jnp.logical_and(gap >= 0, gap < image_n), jnp.int32(image), found)
    return found


def own_images_kernel(swaps, owner_n, states, gains, self_t, cross_t, partners, *rest):
    outs, rest = rest[: len(swaps)], rest[len(swaps) :]
    context_out, table, query_weight_out, states_v, gains_v, self_v, cross_v, partners_s, held, sems = rest
    image_n, patch_n, width = states.shape
    columns = self_t.shape[1]
    copies = [
        pltpu.make_async_copy(states, states_v, sems.at[0]),
        pltpu.make_async_copy(gains, gains_v, sems.at[1]),
        pltpu.make_async_copy(cross_t.at[pl.ds(1, 2)], cross_v, sems.at[2]),
        pltpu.make_async_copy(partners, partners_s, sems.at[3]),
        pltpu.make_async_copy(self_t, self_v, sems.at[4]),
        pltpu.make_async_copy(cross_t.at[0], query_weight_out, sems.at[5]),
    ]
    for copy in copies:
        copy.start()
    copies[0].wait()
    rows = norm_core(states_v[...].reshape(image_n * patch_n, width).astype(F32))
    copies[1].wait()
    normed = (rows * gains_v[2:3, :]).astype(BF16)
    copies[2].wait()
    projected = nt(cross_v[...].reshape(2 * columns, width), normed).astype(BF16)
    for image in range(image_n):
        held[image] = projected[:, image * patch_n : (image + 1) * patch_n]
    copies[3].wait()
    me = lax.axis_index("owner")
    for at, (out, swap) in enumerate(zip(outs, swaps)):
        image = joined_image(partners_s, swap_target(me, swap, owner_n), image_n)
        out[...] = held[image]
        table[at : at + 1, :] = jnp.full((1, LANES), image, jnp.int32)
    normed = (rows * gains_v[0:1, :]).astype(BF16)
    copies[4].wait()
    queries = nt(normed, self_v[0]).astype(BF16).astype(F32) * HEAD ** (-0.5)
    key_value = nt(self_v[1:3].reshape(2 * columns, width), normed).astype(BF16)
    contexts = []
    for image in range(image_n):
        span = slice(image * patch_n, (image + 1) * patch_n)
        contexts.append(
            attend(head_stack(queries[span]), key_value[:columns, span], key_value[columns:, span])
        )
    context_out[...] = pack(jnp.concatenate(contexts, 0))
    copies[5].wait()


def unpack(block):
    row_n = block.shape[0] * 2 // 3
    tail = block[row_n:, :]
    return jnp.concatenate(
        [block[:row_n, :], jnp.concatenate([tail[:, :HEAD], tail[:, HEAD:]], 0)], 1
    )


def partial_kernel(states, own, got, own_weight, got_weight, base, sent):
    rows = jnp.concatenate([unpack(own[...]), unpack(got[...])], 1)
    part = nn(rows, jnp.concatenate([own_weight[...], got_weight[...]], 0))
    sent[...] = part.astype(BF16)
    base[...] = states[...].reshape(part.shape).astype(F32) + part


def query_kernel(helper_n, base, got, gains, weight, own_rows, queries_out, mixed_ref):
    mixed = base[...] + got[...].astype(F32)
    image_n, row_n, width = own_rows.shape
    patch_n = row_n * helper_n
    mixed_ref[...] = mixed.reshape(image_n, patch_n, width)
    normed = (norm_core(mixed) * gains[1:2, :]).astype(BF16)
    queries = nt(normed, weight[...]).astype(BF16).astype(F32) * HEAD ** (-0.5)
    queries_out[...] = queries.reshape(queries_out.shape).astype(BF16)
    start = pl.multiple_of(lax.axis_index("helper") * row_n, row_n)
    own_rows[...] = mixed_ref[:, pl.ds(start, row_n), :]


def hand_on_kernel(value, *rest):
    out = rest[-1]
    out[...] = value[...]


def both_kernel(own, got, waited, out, sems):
    del waited
    row_n = own.shape[0]
    copies = [
        pltpu.make_async_copy(own, out.at[pl.ds(0, row_n)], sems.at[0]),
        pltpu.make_async_copy(got, out.at[pl.ds(row_n, row_n)], sems.at[1]),
    ]
    for copy in copies:
        copy.start()
    for copy in copies:
        copy.wait()


def cross_pairs(places, helper_n, queries, table, arrived, put):
    for at, (place, block) in enumerate(zip(places, arrived)):
        chosen = queries[0].astype(F32)
        for image in range(1, queries.shape[0]):
            chosen = jnp.where(table[place : place + 1, 0:1] == image, queries[image].astype(F32), chosen)
        columns = block.shape[0] // 2
        context = attend(head_stack(chosen), block[:columns, :], block[columns:, :])
        row_n = context.shape[0] // helper_n
        for helper in range(helper_n):
            put(at, helper, pack(context[helper * row_n : (helper + 1) * row_n]))


def cross_kernel(places, helper_n, queries, table, *rest):
    *arrived, out = rest

    def put(at, helper, rows):
        out[helper, at] = rows

    cross_pairs(places, helper_n, queries, table, arrived, put)


def last_cross_kernel(places, helper_n, queries, table, before, *rest):
    arrived, (*outs, held) = rest[: len(places)], rest[len(places) :]
    first = before.shape[1]
    helper = lax.axis_index("helper")
    for k, out in enumerate(outs):
        out[:first] = before[jnp.bitwise_xor(helper, k)]

    def put(at, helper, rows):
        held[helper, at] = rows

    cross_pairs(places, helper_n, queries, table, arrived, put)
    for k, out in enumerate(outs):
        out[first:] = held[jnp.bitwise_xor(helper, k)]


def side_rows(block):
    row_n = block.shape[1] * 2 // 3
    main, tail = block[:, :row_n, :], block[:, row_n:, :]
    tail = jnp.concatenate([tail[:, :, :HEAD], tail[:, :, HEAD:]], 1)
    return jnp.concatenate([main.reshape(-1, LANES), tail.reshape(-1, HEAD)], 1)


def out_kernel(swaps, owner_n, partners, own_rows, own_weights, core_weights, *rest):
    *sides, out, term_ref, partners_s, sem = rest
    copy = pltpu.make_async_copy(partners, partners_s, sem)
    copy.start()
    image_n, row_n, width = own_rows.shape
    half = len(sides) // 2
    rows = [side_rows(side[...]) for side in sides]
    terms = nn(jnp.concatenate(rows[:half], 1), own_weights[...])
    terms = terms + nn(jnp.concatenate(rows[half:], 1), core_weights[...])
    term_ref[...] = terms.reshape(len(swaps), row_n, width)
    copy.wait()
    me = lax.axis_index("owner")
    lows = [swap_target(me, swap, owner_n) * image_n for swap in swaps]
    for image in range(image_n):
        for slot in range(partners.shape[1]):
            partner = partners_s[image, slot]
            which = jnp.int32(0)
            for at, low in enumerate(lows):
                gap = partner - low
                which = jnp.where(jnp.logical_and(gap >= 0, gap < image_n), jnp.int32(at), which)
            value = (own_rows[image] + term_ref[which]).astype(BF16)
            out[image, slot] = jnp.where(partner >= 0, value, jnp.zeros_like(value))


def local(owner_n, helper_n, states, partners, self_proj, self_out, cross_proj, cross_out, gains):
    image_n, patch_n, width = states.shape
    slot_n = partners.shape[1]
    columns = self_proj.shape[2]
    row_n = patch_n // helper_n
    row_all = image_n * patch_n
    swaps = owner_swaps(slot_n, owner_n)
    pair_n = len(swaps)
    self_proj_t = jnp.swapaxes(self_proj, 1, 2)
    cross_proj_t = jnp.swapaxes(cross_proj, 1, 2)
    chip_hop, core_hop = helper_n // 2, 1

    def across(value, k):
        return lax.ppermute(value, "helper", [(j, j ^ k) for j in range(helper_n)])

    def exchange(value, swap):
        return lax.ppermute(value, "owner", [(o, swap_target(o, swap, owner_n)) for o in range(owner_n)])

    def call(name, kernel, out_shape, in_specs, scratch, *operands, flops=1):
        with jax.named_scope(name):
            return pl.pallas_call(
                kernel,
                out_shape=out_shape,
                in_specs=in_specs,
                out_specs=jax.tree.map(lambda _: VMEM, out_shape),
                scratch_shapes=scratch,
                compiler_params=pltpu.CompilerParams(vmem_limit_bytes=VMEM_BYTES),
                cost_estimate=pl.CostEstimate(flops=flops, bytes_accessed=1, transcendentals=0),
            )(*operands)

    shape = jax.ShapeDtypeStruct
    dma = pltpu.SemaphoreType.DMA
    index_table = pltpu.SMEM(partners.shape, jnp.int32)
    block = shape((2 * columns, patch_n), BF16)

    partners_h = pltpu.with_memory_space_constraint(partners, pltpu.HBM)
    self_out_got = across(self_out, chip_hop)
    cross_out_got = across(cross_out, chip_hop)
    *outgoing, context, table, query_weight = call(
        "own_images",
        functools.partial(own_images_kernel, swaps, owner_n),
        [block] * pair_n
        + [
            shape((row_all * columns // LANES, LANES), BF16),
            shape((pair_n, LANES), jnp.int32),
            shape((columns, width), BF16),
        ],
        [HBM] * 5,
        [
            pltpu.VMEM(states.shape, BF16),
            pltpu.VMEM(gains.shape, F32),
            pltpu.VMEM((3, columns, width), BF16),
            pltpu.VMEM((2, columns, width), BF16),
            index_table,
            pltpu.VMEM((image_n, 2 * columns, patch_n), BF16),
            dma((6,)),
        ],
        *[pltpu.with_memory_space_constraint(x, pltpu.HBM) for x in (states, gains, self_proj_t, cross_proj_t)],
        partners_h,
    )
    arrived = [exchange(value, swap) for value, swap in zip(outgoing, swaps)]
    context_got = across(context, chip_hop)
    near = (slot_n - 1) // 2
    late = [at for at, (_, colour) in enumerate(swaps) if colour]
    early = [at for at in range(pair_n) if at not in late]
    short = [2 * near - 2, 2 * near - 1]
    before = [arrived[at] for at in short] + [self_out_got]
    gains_then = call(
        "gains",
        hand_on_kernel,
        shape(gains.shape, F32),
        [VMEM] + [ANY] * len(before),
        [],
        gains, *before,
    )

    made_shapes = [
        shape((image_n, row_n, width), F32),
        shape((image_n, patch_n, columns), BF16),
    ]

    def mixing(states, gains, query_weight, context, context_got, self_out, self_out_got):
        base, sent = call(
            "self_output_share",
            partial_kernel,
            [shape((row_all, width), F32), shape((row_all, width), BF16)],
            [VMEM] * 5,
            [],
            states, context, context_got, self_out, self_out_got,
        )
        made = call(
            "mixed_and_queries",
            functools.partial(query_kernel, helper_n),
            made_shapes,
            [VMEM] * 4,
            [pltpu.VMEM((image_n, patch_n, width), F32)],
            base, across(sent, core_hop), gains, query_weight,
        )
        return tuple(made)

    def no_images(*operands):
        return tuple(jnp.zeros(made.shape, made.dtype) for made in made_shapes)

    own_rows, queries = lax.cond(
        lax.axis_index("owner") < owner_n, mixing, no_images,
        states, gains_then, query_weight, context, context_got, self_out, self_out_got,
    )
    packed = columns * row_n // LANES
    early_sides = call(
        "early_cross_attention",
        functools.partial(cross_kernel, early, helper_n),
        shape((helper_n, len(early), packed, LANES), BF16),
        [VMEM] * (2 + len(early)),
        [],
        queries, table, *[arrived[at] for at in early],
        flops=EARLY_WEIGHT,
    )
    sides = call(
        "late_cross_attention",
        functools.partial(last_cross_kernel, late, helper_n),
        [shape((pair_n, packed, LANES), BF16)] * helper_n,
        [VMEM] * (3 + len(late)),
        [pltpu.VMEM((helper_n, len(late), packed, LANES), BF16)],
        queries, table, early_sides, *[arrived[at] for at in late],
        flops=LATE_WEIGHT,
    )
    sides = [sides[0]] + [across(sides[k], k) for k in range(1, helper_n)]
    cross_out_both = call(
        "cross_output_both_rows",
        both_kernel,
        shape((2 * columns, width), BF16),
        [VMEM, ANY, ANY],
        [dma((2,))],
        cross_out, cross_out_got, early_sides,
    )
    cross_out_core = across(cross_out_both, core_hop)
    return call(
        "pair_output",
        functools.partial(out_kernel, [swaps[at] for at in early + late], owner_n),
        shape((image_n, slot_n, row_n, width), BF16),
        [HBM] + [VMEM] * (3 + helper_n),
        [pltpu.VMEM((pair_n, row_n, width), F32), index_table, dma],
        partners_h, own_rows, cross_out_both, cross_out_core,
        *[sides[k] for k in (0, chip_hop, core_hop, chip_hop ^ core_hop)],
    )


def solution(mesh):
    return jax.shard_map(
        functools.partial(local, mesh.shape["owner"], mesh.shape["helper"]),
        mesh=mesh,
        in_specs=(
            P("owner", None, None),
            P("owner", None),
            P(None, None, "helper"),
            P("helper", None),
            P(None, None, "helper"),
            P("helper", None),
            P(),
        ),
        out_specs=P("owner", None, "helper", None),
        check_vma=False,
    )
```

```python
import functools

import jax
import jax.numpy as jnp
from jax import lax
from jax.experimental import pallas as pl
from jax.experimental.pallas import tpu as pltpu
from jax.sharding import PartitionSpec as P

HEAD = 64
LANES = 128
F32 = jnp.float32
BF16 = jnp.bfloat16
VMEM_BYTES = 24 * 1024 * 1024
EARLY_WEIGHT = 1
LATE_WEIGHT = 10**11

VMEM = pl.BlockSpec(memory_space=pltpu.VMEM)
HBM = pl.BlockSpec(memory_space=pltpu.HBM)
ANY = pl.BlockSpec(memory_space=pl.ANY)


def owner_swaps(slot_count, owner_count):
    near = (slot_count - 1) // 2
    swaps = [(owner_count // 2, 0)]
    for k in range(near, 1, -1):
        swaps += [(k, 1), (k, 0)]
    return swaps + [(1, 0), (1, 1)]


def swap_target(owner, swap, owner_count):
    distance, colour = swap
    step = distance & -distance
    if isinstance(owner, int):
        up = (owner // step) % 2 == colour
        return (owner + (distance if up else owner_count - distance)) % owner_count
    up = jnp.bitwise_and(lax.shift_right_logical(owner, step.bit_length() - 1), 1) == colour
    return lax.rem(owner + jnp.where(up, distance, owner_count - distance), owner_count)


def nn(left, right):
    return lax.dot_general(left, right, (((1,), (0,)), ((), ())), preferred_element_type=F32)


def nt(left, right):
    return lax.dot_general(left, right, (((1,), (1,)), ((), ())), preferred_element_type=F32)


def norm_core(values):
    row_mean = jnp.mean(values, -1, keepdims=True)
    centred = values - row_mean
    row_var = jnp.mean(centred * centred, -1, keepdims=True)
    return centred * lax.rsqrt(row_var + 1e-05)


def head_stack(queries):
    head_of = lax.broadcasted_iota(jnp.int32, queries.shape, 1) // HEAD
    zero = jnp.zeros((), queries.dtype)
    return jnp.concatenate(
        [jnp.where(head_of == h, queries, zero) for h in range(queries.shape[1] // HEAD)], 0
    ).astype(BF16)


def attend(stacked, keys_t, values_t):
    column_n = keys_t.shape[0]
    head_n = column_n // HEAD
    row_n = stacked.shape[0] // head_n
    scores = nn(stacked, keys_t)
    powers = jnp.exp(scores - jnp.max(scores, -1, keepdims=True))
    weights = (powers * (1.0 / jnp.sum(powers, -1, keepdims=True))).astype(BF16)
    spread = nt(weights, values_t)
    head_of = lax.broadcasted_iota(jnp.int32, (row_n, column_n), 1) // HEAD
    context = spread[(head_n - 1) * row_n :]
    for h in range(head_n - 1):
        context = jnp.where(head_of == h, spread[h * row_n : (h + 1) * row_n], context)
    return context


def pack(block):
    row_n = block.shape[0]
    tail = block[:, LANES:]
    return jnp.concatenate(
        [block[:, :LANES], jnp.concatenate([tail[: row_n // 2], tail[row_n // 2 :]], 1)], 0
    ).astype(BF16)


def joined_image(partners, owner, image_n):
    low = owner * image_n
    found = jnp.int32(0)
    for image in range(1, image_n):
        for slot in range(partners.shape[1]):
            gap = partners[image, slot] - low
            found = jnp.where(jnp.logical_and(gap >= 0, gap < image_n), jnp.int32(image), found)
    return found


def own_images_kernel(swaps, owner_n, states, gains, self_t, cross_t, partners, weight, *rest):
    outs, rest = rest[: len(swaps)], rest[len(swaps) :]
    context_out, table, query_weight_out, weight_out, states_v, gains_v, self_v, cross_v, partners_s, held, sems = rest
    image_n, patch_n, width = states.shape
    columns = self_t.shape[1]
    copies = [
        pltpu.make_async_copy(states, states_v, sems.at[0]),
        pltpu.make_async_copy(gains, gains_v, sems.at[1]),
        pltpu.make_async_copy(cross_t.at[pl.ds(1, 2)], cross_v, sems.at[2]),
        pltpu.make_async_copy(partners, partners_s, sems.at[3]),
        pltpu.make_async_copy(self_t, self_v, sems.at[4]),
        pltpu.make_async_copy(cross_t.at[0], query_weight_out, sems.at[5]),
        pltpu.make_async_copy(weight, weight_out, sems.at[6]),
    ]
    for copy in copies:
        copy.start()
    copies[0].wait()
    rows = norm_core(states_v[...].reshape(image_n * patch_n, width).astype(F32))
    copies[1].wait()
    normed = (rows * gains_v[2:3, :]).astype(BF16)
    copies[2].wait()
    projected = nt(cross_v[...].reshape(2 * columns, width), normed).astype(BF16)
    for image in range(image_n):
        held[image] = projected[:, image * patch_n : (image + 1) * patch_n]
    copies[3].wait()
    me = lax.axis_index("owner")
    for at, (out, swap) in enumerate(zip(outs, swaps)):
        image = joined_image(partners_s, swap_target(me, swap, owner_n), image_n)
        out[...] = held[image]
        table[at : at + 1, :] = jnp.full((1, LANES), image, jnp.int32)
    normed = (rows * gains_v[0:1, :]).astype(BF16)
    copies[4].wait()
    queries = nt(normed, self_v[0]).astype(BF16).astype(F32) * HEAD ** (-0.5)
    key_value = nt(self_v[1:3].reshape(2 * columns, width), normed).astype(BF16)
    contexts = []
    for image in range(image_n):
        span = slice(image * patch_n, (image + 1) * patch_n)
        contexts.append(
            attend(head_stack(queries[span]), key_value[:columns, span], key_value[columns:, span])
        )
    context_out[...] = pack(jnp.concatenate(contexts, 0))
    copies[5].wait()
    copies[6].wait()


def unpack(block):
    row_n = block.shape[0] * 2 // 3
    tail = block[row_n:, :]
    return jnp.concatenate(
        [block[:row_n, :], jnp.concatenate([tail[:, :HEAD], tail[:, HEAD:]], 0)], 1
    )


def partial_kernel(states, own, got, own_weight, got_weight, base, sent):
    rows = jnp.concatenate([unpack(own[...]), unpack(got[...])], 1)
    part = nn(rows, jnp.concatenate([own_weight[...], got_weight[...]], 0))
    sent[...] = part.astype(BF16)
    base[...] = states[...].reshape(part.shape).astype(F32) + part


def query_kernel(helper_n, base, got, gains, weight, own_rows, queries_out, mixed_ref):
    mixed = base[...] + got[...].astype(F32)
    image_n, row_n, width = own_rows.shape
    patch_n = row_n * helper_n
    mixed_ref[...] = mixed.reshape(image_n, patch_n, width)
    normed = (norm_core(mixed) * gains[1:2, :]).astype(BF16)
    queries = nt(normed, weight[...]).astype(BF16).astype(F32) * HEAD ** (-0.5)
    queries_out[...] = queries.reshape(queries_out.shape).astype(BF16)
    start = pl.multiple_of(lax.axis_index("helper") * row_n, row_n)
    own_rows[...] = mixed_ref[:, pl.ds(start, row_n), :]


def hand_on_kernel(value, *rest):
    out = rest[-1]
    out[...] = value[...]


def both_kernel(own, got, waited, out, sems):
    del waited
    row_n = own.shape[0]
    copies = [
        pltpu.make_async_copy(own, out.at[pl.ds(0, row_n)], sems.at[0]),
        pltpu.make_async_copy(got, out.at[pl.ds(row_n, row_n)], sems.at[1]),
    ]
    for copy in copies:
        copy.start()
    for copy in copies:
        copy.wait()


def cross_pairs(places, helper_n, queries, table, arrived, put):
    for at, (place, block) in enumerate(zip(places, arrived)):
        chosen = queries[0].astype(F32)
        for image in range(1, queries.shape[0]):
            chosen = jnp.where(table[place : place + 1, 0:1] == image, queries[image].astype(F32), chosen)
        columns = block.shape[0] // 2
        context = attend(head_stack(chosen), block[:columns, :], block[columns:, :])
        row_n = context.shape[0] // helper_n
        for helper in range(helper_n):
            put(at, helper, pack(context[helper * row_n : (helper + 1) * row_n]))


def cross_kernel(places, helper_n, queries, table, *rest):
    *arrived, out = rest

    def put(at, helper, rows):
        out[helper, at] = rows

    cross_pairs(places, helper_n, queries, table, arrived, put)


def last_cross_kernel(places, helper_n, queries, table, before, *rest):
    arrived, (*outs, held) = rest[: len(places)], rest[len(places) :]
    first = before.shape[1]
    helper = lax.axis_index("helper")
    for k, out in enumerate(outs):
        out[:first] = before[jnp.bitwise_xor(helper, k)]

    def put(at, helper, rows):
        held[helper, at] = rows

    cross_pairs(places, helper_n, queries, table, arrived, put)
    for k, out in enumerate(outs):
        out[first:] = held[jnp.bitwise_xor(helper, k)]


def side_rows(block):
    row_n = block.shape[1] * 2 // 3
    main, tail = block[:, :row_n, :], block[:, row_n:, :]
    tail = jnp.concatenate([tail[:, :, :HEAD], tail[:, :, HEAD:]], 1)
    return jnp.concatenate([main.reshape(-1, LANES), tail.reshape(-1, HEAD)], 1)


def out_kernel(swaps, owner_n, partners, own_rows, own_weights, core_weights, *rest):
    *sides, out, term_ref, out_v, partners_s, sems = rest
    copy = pltpu.make_async_copy(partners, partners_s, sems.at[0])
    copy.start()
    image_n, row_n, width = own_rows.shape
    rows = jnp.concatenate([side_rows(side[...]) for side in sides], 1)
    terms = nn(rows, jnp.concatenate([own_weights[...], core_weights[...]], 0))
    term_ref[...] = terms.reshape(len(swaps), row_n, width)
    copy.wait()
    me = lax.axis_index("owner")
    lows = [swap_target(me, swap, owner_n) * image_n for swap in swaps]
    sent = []
    for image in range(image_n):
        for slot in range(partners.shape[1]):
            partner = partners_s[image, slot]
            which = jnp.int32(0)
            for at, low in enumerate(lows):
                gap = partner - low
                which = jnp.where(jnp.logical_and(gap >= 0, gap < image_n), jnp.int32(at), which)
            value = (own_rows[image] + term_ref[which]).astype(BF16)
            out_v[image, slot] = jnp.where(partner >= 0, value, jnp.zeros_like(value))
        sent.append(pltpu.make_async_copy(out_v.at[image], out.at[image], sems.at[1 + image]))
        sent[-1].start()
    for copy in sent:
        copy.wait()


def local(owner_n, helper_n, states, partners, self_proj, self_out, cross_proj, cross_out, gains):
    image_n, patch_n, width = states.shape
    slot_n = partners.shape[1]
    columns = self_proj.shape[2]
    row_n = patch_n // helper_n
    row_all = image_n * patch_n
    swaps = owner_swaps(slot_n, owner_n)
    pair_n = len(swaps)
    self_proj_t = jnp.swapaxes(self_proj, 1, 2)
    cross_proj_t = jnp.swapaxes(cross_proj, 1, 2)
    chip_hop, core_hop = helper_n // 2, 1

    def across(value, k):
        return lax.ppermute(value, "helper", [(j, j ^ k) for j in range(helper_n)])

    def exchange(value, swap):
        return lax.ppermute(value, "owner", [(o, swap_target(o, swap, owner_n)) for o in range(owner_n)])

    def call(name, kernel, out_shape, in_specs, scratch, *operands, out_specs=None, flops=1):
        with jax.named_scope(name):
            return pl.pallas_call(
                kernel,
                out_shape=out_shape,
                in_specs=in_specs,
                out_specs=out_specs or jax.tree.map(lambda _: VMEM, out_shape),
                scratch_shapes=scratch,
                compiler_params=pltpu.CompilerParams(vmem_limit_bytes=VMEM_BYTES),
                cost_estimate=pl.CostEstimate(flops=flops, bytes_accessed=1, transcendentals=0),
            )(*operands)

    shape = jax.ShapeDtypeStruct
    dma = pltpu.SemaphoreType.DMA
    index_table = pltpu.SMEM(partners.shape, jnp.int32)
    block = shape((2 * columns, patch_n), BF16)

    partners_h = pltpu.with_memory_space_constraint(partners, pltpu.HBM)
    self_out_got = across(self_out, chip_hop)
    *outgoing, context, table, query_weight, cross_out_own = call(
        "own_images",
        functools.partial(own_images_kernel, swaps, owner_n),
        [block] * pair_n
        + [
            shape((row_all * columns // LANES, LANES), BF16),
            shape((pair_n, LANES), jnp.int32),
            shape((columns, width), BF16),
            shape(cross_out.shape, BF16),
        ],
        [HBM] * 6,
        [
            pltpu.VMEM(states.shape, BF16),
            pltpu.VMEM(gains.shape, F32),
            pltpu.VMEM((3, columns, width), BF16),
            pltpu.VMEM((2, columns, width), BF16),
            index_table,
            pltpu.VMEM((image_n, 2 * columns, patch_n), BF16),
            dma((7,)),
        ],
        *[pltpu.with_memory_space_constraint(x, pltpu.HBM) for x in (states, gains, self_proj_t, cross_proj_t)],
        partners_h,
        pltpu.with_memory_space_constraint(cross_out, pltpu.HBM),
    )
    cross_out_got = across(cross_out_own, chip_hop)
    arrived = [exchange(value, swap) for value, swap in zip(outgoing, swaps)]
    context_got = across(context, chip_hop)
    near = (slot_n - 1) // 2
    late = [at for at, (_, colour) in enumerate(swaps) if colour]
    early = [at for at in range(pair_n) if at not in late]
    short = [2 * near - 2, 2 * near - 1]
    before = [arrived[at] for at in short] + [self_out_got]
    gains_then = call(
        "gains",
        hand_on_kernel,
        shape(gains.shape, F32),
        [VMEM] + [ANY] * len(before),
        [],
        gains, *before,
    )

    made_shapes = [
        shape((image_n, row_n, width), F32),
        shape((image_n, patch_n, columns), BF16),
    ]

    def mixing(states, gains, query_weight, context, context_got, self_out, self_out_got):
        base, sent = call(
            "self_output_share",
            partial_kernel,
            [shape((row_all, width), F32), shape((row_all, width), BF16)],
            [VMEM] * 5,
            [],
            states, context, context_got, self_out, self_out_got,
        )
        made = call(
            "mixed_and_queries",
            functools.partial(query_kernel, helper_n),
            made_shapes,
            [VMEM] * 4,
            [pltpu.VMEM((image_n, patch_n, width), F32)],
            base, across(sent, core_hop), gains, query_weight,
        )
        return tuple(made)

    def no_images(*operands):
        return tuple(jnp.zeros(made.shape, made.dtype) for made in made_shapes)

    own_rows, queries = lax.cond(
        lax.axis_index("owner") < owner_n, mixing, no_images,
        states, gains_then, query_weight, context, context_got, self_out, self_out_got,
    )
    packed = columns * row_n // LANES
    early_sides = call(
        "early_cross_attention",
        functools.partial(cross_kernel, early, helper_n),
        shape((helper_n, len(early), packed, LANES), BF16),
        [VMEM] * (2 + len(early)),
        [],
        queries, table, *[arrived[at] for at in early],
        flops=EARLY_WEIGHT,
    )
    sides = call(
        "late_cross_attention",
        functools.partial(last_cross_kernel, late, helper_n),
        [shape((pair_n, packed, LANES), BF16)] * helper_n,
        [VMEM] * (3 + len(late)),
        [pltpu.VMEM((helper_n, len(late), packed, LANES), BF16)],
        queries, table, early_sides, *[arrived[at] for at in late],
        flops=LATE_WEIGHT,
    )
    sides = [sides[0]] + [across(sides[k], k) for k in range(1, helper_n)]
    cross_out_both = call(
        "cross_output_both_rows",
        both_kernel,
        shape((2 * columns, width), BF16),
        [VMEM, ANY, ANY],
        [dma((2,))],
        cross_out, cross_out_got, early_sides,
    )
    cross_out_core = across(cross_out_both, core_hop)
    return call(
        "pair_output",
        functools.partial(out_kernel, [swaps[at] for at in early + late], owner_n),
        shape((image_n, slot_n, row_n, width), BF16),
        [HBM] + [VMEM] * (3 + helper_n),
        [
            pltpu.VMEM((pair_n, row_n, width), F32),
            pltpu.VMEM((image_n, slot_n, row_n, width), BF16),
            index_table,
            dma((1 + image_n,)),
        ],
        partners_h, own_rows, cross_out_both, cross_out_core,
        *[sides[k] for k in (0, chip_hop, core_hop, chip_hop ^ core_hop)],
        out_specs=HBM,
    )


def solution(mesh):
    return jax.shard_map(
        functools.partial(local, mesh.shape["owner"], mesh.shape["helper"]),
        mesh=mesh,
        in_specs=(
            P("owner", None, None),
            P("owner", None),
            P(None, None, "helper"),
            P("helper", None),
            P(None, None, "helper"),
            P("helper", None),
            P(),
        ),
        out_specs=P("owner", None, "helper", None),
        check_vma=False,
    )
```

```python
import functools

import jax
import jax.numpy as jnp
from jax import lax
from jax.experimental import pallas as pl
from jax.experimental.pallas import tpu as pltpu
from jax.sharding import PartitionSpec as P

HEAD = 64
LANES = 128
F32 = jnp.float32
BF16 = jnp.bfloat16
VMEM_BYTES = 24 * 1024 * 1024
EARLY_WEIGHT = 3*10**9
LATE_WEIGHT = 10**11

VMEM = pl.BlockSpec(memory_space=pltpu.VMEM)
HBM = pl.BlockSpec(memory_space=pltpu.HBM)
ANY = pl.BlockSpec(memory_space=pl.ANY)


def owner_swaps(slot_count, owner_count):
    near = (slot_count - 1) // 2
    swaps = [(owner_count // 2, 0)]
    for k in range(near, 1, -1):
        swaps += [(k, 1), (k, 0)]
    return swaps + [(1, 0), (1, 1)]


def swap_target(owner, swap, owner_count):
    distance, colour = swap
    step = distance & -distance
    if isinstance(owner, int):
        up = (owner // step) % 2 == colour
        return (owner + (distance if up else owner_count - distance)) % owner_count
    up = jnp.bitwise_and(lax.shift_right_logical(owner, step.bit_length() - 1), 1) == colour
    return lax.rem(owner + jnp.where(up, distance, owner_count - distance), owner_count)


def nn(left, right):
    return lax.dot_general(left, right, (((1,), (0,)), ((), ())), preferred_element_type=F32)


def nt(left, right):
    return lax.dot_general(left, right, (((1,), (1,)), ((), ())), preferred_element_type=F32)


def norm_core(values):
    row_mean = jnp.mean(values, -1, keepdims=True)
    centred = values - row_mean
    row_var = jnp.mean(centred * centred, -1, keepdims=True)
    return centred * lax.rsqrt(row_var + 1e-05)


def head_stack(queries):
    head_of = lax.broadcasted_iota(jnp.int32, queries.shape, 1) // HEAD
    zero = jnp.zeros((), queries.dtype)
    return jnp.concatenate(
        [jnp.where(head_of == h, queries, zero) for h in range(queries.shape[1] // HEAD)], 0
    ).astype(BF16)


def attend(stacked, keys_t, values_t):
    column_n = keys_t.shape[0]
    head_n = column_n // HEAD
    row_n = stacked.shape[0] // head_n
    scores = nn(stacked, keys_t)
    powers = jnp.exp(scores - jnp.max(scores, -1, keepdims=True))
    weights = (powers * (1.0 / jnp.sum(powers, -1, keepdims=True))).astype(BF16)
    spread = nt(weights, values_t)
    head_of = lax.broadcasted_iota(jnp.int32, (row_n, column_n), 1) // HEAD
    context = spread[(head_n - 1) * row_n :]
    for h in range(head_n - 1):
        context = jnp.where(head_of == h, spread[h * row_n : (h + 1) * row_n], context)
    return context


def pack(block):
    row_n = block.shape[0]
    tail = block[:, LANES:]
    return jnp.concatenate(
        [block[:, :LANES], jnp.concatenate([tail[: row_n // 2], tail[row_n // 2 :]], 1)], 0
    ).astype(BF16)


def pair_place(partners, owner, image_n):
    low = owner * image_n
    found_image, found_slot = jnp.int32(0), jnp.int32(0)
    for image in range(image_n):
        for slot in range(partners.shape[1]):
            gap = partners[image, slot] - low
            hit = jnp.logical_and(gap >= 0, gap < image_n)
            found_image = jnp.where(hit, jnp.int32(image), found_image)
            found_slot = jnp.where(hit, jnp.int32(slot), found_slot)
    return found_image, found_slot


def live_count(partners, image):
    count = jnp.int32(0)
    for slot in range(partners.shape[1]):
        count = count + jnp.where(partners[image, slot] >= 0, jnp.int32(1), jnp.int32(0))
    return count


def own_images_kernel(swaps, owner_n, states, gains, self_t, cross_t, partners, weight, *rest):
    outs, rest = rest[: len(swaps)], rest[len(swaps) :]
    context_out, table, query_weight_out, weight_out, states_v, gains_v, self_v, cross_v, partners_s, held, sems = rest
    image_n, patch_n, width = states.shape
    columns = self_t.shape[1]
    copies = [
        pltpu.make_async_copy(states, states_v, sems.at[0]),
        pltpu.make_async_copy(gains, gains_v, sems.at[1]),
        pltpu.make_async_copy(cross_t.at[pl.ds(1, 2)], cross_v, sems.at[2]),
        pltpu.make_async_copy(partners, partners_s, sems.at[3]),
        pltpu.make_async_copy(self_t, self_v, sems.at[4]),
        pltpu.make_async_copy(cross_t.at[0], query_weight_out, sems.at[5]),
        pltpu.make_async_copy(weight, weight_out, sems.at[6]),
    ]
    for copy in copies:
        copy.start()
    copies[0].wait()
    rows = norm_core(states_v[...].reshape(image_n * patch_n, width).astype(F32))
    copies[1].wait()
    normed = (rows * gains_v[2:3, :]).astype(BF16)
    copies[2].wait()
    projected = nt(cross_v[...].reshape(2 * columns, width), normed).astype(BF16)
    for image in range(image_n):
        held[image] = projected[:, image * patch_n : (image + 1) * patch_n]
    copies[3].wait()
    me = lax.axis_index("owner")
    pair_n = len(swaps)
    for at, (out, swap) in enumerate(zip(outs, swaps)):
        image, slot = pair_place(partners_s, swap_target(me, swap, owner_n), image_n)
        out[...] = held[image]
        position = jnp.where(image == 0, slot, pair_n - 1 - slot)
        table[at : at + 1, :] = jnp.full((1, LANES), image, jnp.int32)
        table[pair_n + at : pair_n + at + 1, :] = jnp.full((1, LANES), position, jnp.int32)
    table[2 * pair_n :, :] = jnp.full((1, LANES), live_count(partners_s, 0), jnp.int32)
    normed = (rows * gains_v[0:1, :]).astype(BF16)
    copies[4].wait()
    queries = nt(normed, self_v[0]).astype(BF16).astype(F32) * HEAD ** (-0.5)
    key_value = nt(self_v[1:3].reshape(2 * columns, width), normed).astype(BF16)
    contexts = []
    for image in range(image_n):
        span = slice(image * patch_n, (image + 1) * patch_n)
        contexts.append(
            attend(head_stack(queries[span]), key_value[:columns, span], key_value[columns:, span])
        )
    context_out[...] = pack(jnp.concatenate(contexts, 0))
    copies[5].wait()
    copies[6].wait()


def unpack(block):
    row_n = block.shape[0] * 2 // 3
    tail = block[row_n:, :]
    return jnp.concatenate(
        [block[:row_n, :], jnp.concatenate([tail[:, :HEAD], tail[:, HEAD:]], 0)], 1
    )


def partial_kernel(states, own, got, own_weight, got_weight, base, sent):
    rows = jnp.concatenate([unpack(own[...]), unpack(got[...])], 1)
    part = nn(rows, jnp.concatenate([own_weight[...], got_weight[...]], 0))
    sent[...] = part.astype(BF16)
    base[...] = states[...].reshape(part.shape).astype(F32) + part


def query_kernel(helper_n, base, got, gains, weight, own_rows, queries_out, mixed_ref):
    mixed = base[...] + got[...].astype(F32)
    image_n, row_n, width = own_rows.shape
    patch_n = row_n * helper_n
    mixed_ref[...] = mixed.reshape(image_n, patch_n, width)
    normed = (norm_core(mixed) * gains[1:2, :]).astype(BF16)
    queries = nt(normed, weight[...]).astype(BF16).astype(F32) * HEAD ** (-0.5)
    queries_out[...] = queries.reshape(queries_out.shape).astype(BF16)
    start = pl.multiple_of(lax.axis_index("helper") * row_n, row_n)
    own_rows[...] = mixed_ref[:, pl.ds(start, row_n), :]


def hand_on_kernel(value, *rest):
    out = rest[-1]
    out[...] = value[...]


def both_kernel(own, got, waited, out, sems):
    del waited
    row_n = own.shape[0]
    copies = [
        pltpu.make_async_copy(own, out.at[pl.ds(0, row_n)], sems.at[0]),
        pltpu.make_async_copy(got, out.at[pl.ds(row_n, row_n)], sems.at[1]),
    ]
    for copy in copies:
        copy.start()
    for copy in copies:
        copy.wait()


def cross_pairs(places, helper_n, queries, table, arrived, put):
    for at, (place, block) in enumerate(zip(places, arrived)):
        chosen = queries[0].astype(F32)
        for image in range(1, queries.shape[0]):
            chosen = jnp.where(table[place : place + 1, 0:1] == image, queries[image].astype(F32), chosen)
        columns = block.shape[0] // 2
        context = attend(head_stack(chosen), block[:columns, :], block[columns:, :])
        row_n = context.shape[0] // helper_n
        for helper in range(helper_n):
            put(at, helper, pack(context[helper * row_n : (helper + 1) * row_n]))


def cross_kernel(places, helper_n, queries, table, *rest):
    *arrived, out = rest

    def put(at, helper, rows):
        out[helper, at] = rows

    cross_pairs(places, helper_n, queries, table, arrived, put)


def last_cross_kernel(places, helper_n, queries, table, before, *rest):
    arrived, (*outs, held) = rest[: len(places)], rest[len(places) :]
    first = before.shape[1]
    helper = lax.axis_index("helper")
    for k, out in enumerate(outs):
        out[:first] = before[jnp.bitwise_xor(helper, k)]

    def put(at, helper, rows):
        held[helper, at] = rows

    cross_pairs(places, helper_n, queries, table, arrived, put)
    for k, out in enumerate(outs):
        out[first:] = held[jnp.bitwise_xor(helper, k)]


def side_rows(block):
    row_n = block.shape[1] * 2 // 3
    main, tail = block[:, :row_n, :], block[:, row_n:, :]
    tail = jnp.concatenate([tail[:, :, :HEAD], tail[:, :, HEAD:]], 1)
    return jnp.concatenate([main.reshape(-1, LANES), tail.reshape(-1, HEAD)], 1)


def out_kernel(order, own_rows, table, own_weights, core_weights, *rest):
    *sides, out, out_v, sems = rest
    row_n, width = own_rows.shape[1:]
    pair_n = len(order)
    placed = []
    for side in sides:
        pairs = [side[at].astype(F32) for at in range(pair_n)]
        for position in range(pair_n):
            block = pairs[0]
            for at in range(1, pair_n):
                row = pair_n + order[at]
                block = jnp.where(table[row : row + 1, 0:1] == position, pairs[at], block)
            placed.append(block.astype(BF16)[None])
    rows = [
        side_rows(jnp.concatenate(placed[at * pair_n : (at + 1) * pair_n], 0)) for at in range(len(sides))
    ]
    half = len(sides) // 2
    terms = nn(jnp.concatenate(rows[:half], 1), own_weights[...])
    terms = terms + nn(jnp.concatenate(rows[half:], 1), core_weights[...])
    first_n = table[2 * pair_n :, 0:1]
    zero = jnp.zeros((row_n, width), F32)
    for position in range(pair_n):
        term = terms[position * row_n : (position + 1) * row_n]
        is_first = first_n > position
        out_v[0, position] = jnp.where(is_first, own_rows[0] + term, zero).astype(BF16)
        out_v[1, pair_n - 1 - position] = jnp.where(is_first, zero, own_rows[1] + term).astype(BF16)
    copies = [pltpu.make_async_copy(out_v.at[image], out.at[image], sems.at[image]) for image in range(2)]
    for copy in copies:
        copy.start()
    for copy in copies:
        copy.wait()


def local(owner_n, helper_n, states, partners, self_proj, self_out, cross_proj, cross_out, gains):
    image_n, patch_n, width = states.shape
    slot_n = partners.shape[1]
    columns = self_proj.shape[2]
    row_n = patch_n // helper_n
    row_all = image_n * patch_n
    swaps = owner_swaps(slot_n, owner_n)
    pair_n = len(swaps)
    self_proj_t = jnp.swapaxes(self_proj, 1, 2)
    cross_proj_t = jnp.swapaxes(cross_proj, 1, 2)
    chip_hop, core_hop = helper_n // 2, 1

    def across(value, k):
        return lax.ppermute(value, "helper", [(j, j ^ k) for j in range(helper_n)])

    def exchange(value, swap):
        return lax.ppermute(value, "owner", [(o, swap_target(o, swap, owner_n)) for o in range(owner_n)])

    def call(name, kernel, out_shape, in_specs, scratch, *operands, out_specs=None, flops=1):
        with jax.named_scope(name):
            return pl.pallas_call(
                kernel,
                out_shape=out_shape,
                in_specs=in_specs,
                out_specs=out_specs or jax.tree.map(lambda _: VMEM, out_shape),
                scratch_shapes=scratch,
                compiler_params=pltpu.CompilerParams(vmem_limit_bytes=VMEM_BYTES),
                cost_estimate=pl.CostEstimate(flops=flops, bytes_accessed=1, transcendentals=0),
            )(*operands)

    shape = jax.ShapeDtypeStruct
    dma = pltpu.SemaphoreType.DMA
    index_table = pltpu.SMEM(partners.shape, jnp.int32)
    block = shape((2 * columns, patch_n), BF16)

    partners_h = pltpu.with_memory_space_constraint(partners, pltpu.HBM)
    self_out_got = across(self_out, chip_hop)
    *outgoing, context, table, query_weight, cross_out_own = call(
        "own_images",
        functools.partial(own_images_kernel, swaps, owner_n),
        [block] * pair_n
        + [
            shape((row_all * columns // LANES, LANES), BF16),
            shape((2 * pair_n + 1, LANES), jnp.int32),
            shape((columns, width), BF16),
            shape(cross_out.shape, BF16),
        ],
        [HBM] * 6,
        [
            pltpu.VMEM(states.shape, BF16),
            pltpu.VMEM(gains.shape, F32),
            pltpu.VMEM((3, columns, width), BF16),
            pltpu.VMEM((2, columns, width), BF16),
            index_table,
            pltpu.VMEM((image_n, 2 * columns, patch_n), BF16),
            dma((7,)),
        ],
        *[pltpu.with_memory_space_constraint(x, pltpu.HBM) for x in (states, gains, self_proj_t, cross_proj_t)],
        partners_h,
        pltpu.with_memory_space_constraint(cross_out, pltpu.HBM),
    )
    arrived = [exchange(value, swap) for value, swap in zip(outgoing, swaps)]
    context_got = across(context, chip_hop)
    near = (slot_n - 1) // 2
    late = [at for at, (_, colour) in enumerate(swaps) if colour]
    early = [at for at in range(pair_n) if at not in late]
    short = [2 * near - 2, 2 * near - 1]
    cross_out_sent = call(
        "cross_output_rows",
        hand_on_kernel,
        shape(cross_out.shape, BF16),
        [VMEM] + [ANY] * len([arrived[short[0]]]),
        [],
        cross_out_own, *[arrived[short[0]]],
    )
    cross_out_got = across(cross_out_sent, chip_hop)
    before = [arrived[at] for at in short] + [self_out_got]
    gains_then = call(
        "gains",
        hand_on_kernel,
        shape(gains.shape, F32),
        [VMEM] + [ANY] * len(before),
        [],
        gains, *before,
    )

    made_shapes = [
        shape((image_n, row_n, width), F32),
        shape((image_n, patch_n, columns), BF16),
    ]

    def mixing(states, gains, query_weight, context, context_got, self_out, self_out_got):
        base, sent = call(
            "self_output_share",
            partial_kernel,
            [shape((row_all, width), F32), shape((row_all, width), BF16)],
            [VMEM] * 5,
            [],
            states, context, context_got, self_out, self_out_got,
        )
        made = call(
            "mixed_and_queries",
            functools.partial(query_kernel, helper_n),
            made_shapes,
            [VMEM] * 4,
            [pltpu.VMEM((image_n, patch_n, width), F32)],
            base, across(sent, core_hop), gains, query_weight,
        )
        return tuple(made)

    def no_images(*operands):
        return tuple(jnp.zeros(made.shape, made.dtype) for made in made_shapes)

    own_rows, queries = lax.cond(
        lax.axis_index("owner") < owner_n, mixing, no_images,
        states, gains_then, query_weight, context, context_got, self_out, self_out_got,
    )
    packed = columns * row_n // LANES
    early_sides = call(
        "early_cross_attention",
        functools.partial(cross_kernel, early, helper_n),
        shape((helper_n, len(early), packed, LANES), BF16),
        [VMEM] * (2 + len(early)),
        [],
        queries, table, *[arrived[at] for at in early],
        flops=EARLY_WEIGHT,
    )
    sides = call(
        "late_cross_attention",
        functools.partial(last_cross_kernel, late, helper_n),
        [shape((pair_n, packed, LANES), BF16)] * helper_n,
        [VMEM] * (3 + len(late)),
        [pltpu.VMEM((helper_n, len(late), packed, LANES), BF16)],
        queries, table, early_sides, *[arrived[at] for at in late],
        flops=LATE_WEIGHT,
    )
    sides = [sides[0]] + [across(sides[k], k) for k in range(1, helper_n)]
    cross_out_both = call(
        "cross_output_both_rows",
        both_kernel,
        shape((2 * columns, width), BF16),
        [VMEM, ANY, ANY],
        [dma((2,))],
        cross_out, cross_out_got, early_sides,
    )
    cross_out_core = across(cross_out_both, core_hop)
    return call(
        "pair_output",
        functools.partial(out_kernel, early + late),
        shape((image_n, slot_n, row_n, width), BF16),
        [VMEM] * (4 + helper_n),
        [pltpu.VMEM((image_n, slot_n, row_n, width), BF16), dma((image_n,))],
        own_rows, table, cross_out_both, cross_out_core,
        *[sides[k] for k in (0, chip_hop, core_hop, chip_hop ^ core_hop)],
        out_specs=HBM,
    )


def solution(mesh):
    return jax.shard_map(
        functools.partial(local, mesh.shape["owner"], mesh.shape["helper"]),
        mesh=mesh,
        in_specs=(
            P("owner", None, None),
            P("owner", None),
            P(None, None, "helper"),
            P("helper", None),
            P(None, None, "helper"),
            P("helper", None),
            P(),
        ),
        out_specs=P("owner", None, "helper", None),
        check_vma=False,
    )
```

```python
import functools

import jax
import jax.numpy as jnp
from jax import lax
from jax.experimental import pallas as pl
from jax.experimental.pallas import tpu as pltpu
from jax.sharding import PartitionSpec as P

HEAD = 64
LANES = 128
F32 = jnp.float32
BF16 = jnp.bfloat16
VMEM_BYTES = 24 * 1024 * 1024
EARLY_WEIGHT = 3 * 10**9
LATE_WEIGHT = 10**11

VMEM = pl.BlockSpec(memory_space=pltpu.VMEM)
HBM = pl.BlockSpec(memory_space=pltpu.HBM)
ANY = pl.BlockSpec(memory_space=pl.ANY)


def owner_swaps(slot_count, owner_count):
    near = (slot_count - 1) // 2
    swaps = [(owner_count // 2, 0)]
    for k in range(near, 1, -1):
        swaps += [(k, 1), (k, 0)]
    return swaps + [(1, 0), (1, 1)]


def swap_target(owner, swap, owner_count):
    distance, colour = swap
    step = distance & -distance
    if isinstance(owner, int):
        up = (owner // step) % 2 == colour
        return (owner + (distance if up else owner_count - distance)) % owner_count
    up = jnp.bitwise_and(lax.shift_right_logical(owner, step.bit_length() - 1), 1) == colour
    return lax.rem(owner + jnp.where(up, distance, owner_count - distance), owner_count)


def nn(left, right):
    return lax.dot_general(left, right, (((1,), (0,)), ((), ())), preferred_element_type=F32)


def nt(left, right):
    return lax.dot_general(left, right, (((1,), (1,)), ((), ())), preferred_element_type=F32)


def norm_core(values):
    row_mean = jnp.mean(values, -1, keepdims=True)
    centred = values - row_mean
    row_var = jnp.mean(centred * centred, -1, keepdims=True)
    return centred * lax.rsqrt(row_var + 1e-05)


def head_stack(queries):
    head_of = lax.broadcasted_iota(jnp.int32, queries.shape, 1) // HEAD
    zero = jnp.zeros((), queries.dtype)
    return jnp.concatenate(
        [jnp.where(head_of == h, queries, zero) for h in range(queries.shape[1] // HEAD)], 0
    ).astype(BF16)


def attend(stacked, keys_t, values_t):
    column_n = keys_t.shape[0]
    head_n = column_n // HEAD
    row_n = stacked.shape[0] // head_n
    scores = nn(stacked, keys_t)
    powers = jnp.exp(scores - jnp.max(scores, -1, keepdims=True))
    weights = (powers * (1.0 / jnp.sum(powers, -1, keepdims=True))).astype(BF16)
    spread = nt(weights, values_t)
    head_of = lax.broadcasted_iota(jnp.int32, (row_n, column_n), 1) // HEAD
    context = spread[(head_n - 1) * row_n :]
    for h in range(head_n - 1):
        context = jnp.where(head_of == h, spread[h * row_n : (h + 1) * row_n], context)
    return context


def pack(block):
    row_n = block.shape[0]
    tail = block[:, LANES:]
    return jnp.concatenate(
        [block[:, :LANES], jnp.concatenate([tail[: row_n // 2], tail[row_n // 2 :]], 1)], 0
    ).astype(BF16)


def pair_place(partners, owner, image_n):
    low = owner * image_n
    found_image, found_slot = jnp.int32(0), jnp.int32(0)
    for image in range(image_n):
        for slot in range(partners.shape[1]):
            gap = partners[image, slot] - low
            hit = jnp.logical_and(gap >= 0, gap < image_n)
            found_image = jnp.where(hit, jnp.int32(image), found_image)
            found_slot = jnp.where(hit, jnp.int32(slot), found_slot)
    return found_image, found_slot


def live_count(partners, image):
    count = jnp.int32(0)
    for slot in range(partners.shape[1]):
        count = count + jnp.where(partners[image, slot] >= 0, jnp.int32(1), jnp.int32(0))
    return count


def own_images_kernel(swaps, owner_n, states, gains, self_t, cross_t, partners, weight, *rest):
    outs, rest = rest[: len(swaps)], rest[len(swaps) :]
    context_out, table, query_weight_out, weight_out, states_v, gains_v, self_v, cross_v, partners_s, held, sems = rest
    image_n, patch_n, width = states.shape
    columns = self_t.shape[1]
    copies = [
        pltpu.make_async_copy(states, states_v, sems.at[0]),
        pltpu.make_async_copy(gains, gains_v, sems.at[1]),
        pltpu.make_async_copy(cross_t.at[pl.ds(1, 2)], cross_v, sems.at[2]),
        pltpu.make_async_copy(partners, partners_s, sems.at[3]),
        pltpu.make_async_copy(self_t, self_v, sems.at[4]),
        pltpu.make_async_copy(cross_t.at[0], query_weight_out, sems.at[5]),
        pltpu.make_async_copy(weight, weight_out, sems.at[6]),
    ]
    for copy in copies:
        copy.start()
    copies[0].wait()
    rows = norm_core(states_v[...].reshape(image_n * patch_n, width).astype(F32))
    for copy in copies[1:5]:
        copy.wait()
    normed = (rows * gains_v[2:3, :]).astype(BF16)
    projected = nt(cross_v[...].reshape(2 * columns, width), normed).astype(BF16)
    for image in range(image_n):
        held[image] = projected[:, image * patch_n : (image + 1) * patch_n]
    normed = (rows * gains_v[0:1, :]).astype(BF16)
    queries = nt(normed, self_v[0]).astype(BF16).astype(F32) * HEAD ** (-0.5)
    key_value = nt(self_v[1:3].reshape(2 * columns, width), normed).astype(BF16)
    contexts = []
    for image in range(image_n):
        span = slice(image * patch_n, (image + 1) * patch_n)
        contexts.append(
            attend(head_stack(queries[span]), key_value[:columns, span], key_value[columns:, span])
        )
    me = lax.axis_index("owner")
    pair_n = len(swaps)
    for at, (out, swap) in enumerate(zip(outs, swaps)):
        image, slot = pair_place(partners_s, swap_target(me, swap, owner_n), image_n)
        out[...] = held[image]
        position = jnp.where(image == 0, slot, pair_n - 1 - slot)
        table[at : at + 1, :] = jnp.full((1, LANES), image, jnp.int32)
        table[pair_n + at : pair_n + at + 1, :] = jnp.full((1, LANES), position, jnp.int32)
    table[2 * pair_n :, :] = jnp.full((1, LANES), live_count(partners_s, 0), jnp.int32)
    context_out[...] = pack(jnp.concatenate(contexts, 0))
    copies[5].wait()
    copies[6].wait()


def unpack(block):
    row_n = block.shape[0] * 2 // 3
    tail = block[row_n:, :]
    return jnp.concatenate(
        [block[:row_n, :], jnp.concatenate([tail[:, :HEAD], tail[:, HEAD:]], 0)], 1
    )


def partial_kernel(states, own, got, own_weight, got_weight, base, sent):
    rows = jnp.concatenate([unpack(own[...]), unpack(got[...])], 1)
    part = nn(rows, jnp.concatenate([own_weight[...], got_weight[...]], 0))
    sent[...] = part.astype(BF16)
    base[...] = states[...].reshape(part.shape).astype(F32) + part


def query_kernel(helper_n, base, got, gains, weight, own_rows, queries_out, mixed_ref):
    mixed = base[...] + got[...].astype(F32)
    image_n, row_n, width = own_rows.shape
    patch_n = row_n * helper_n
    mixed_ref[...] = mixed.reshape(image_n, patch_n, width)
    normed = (norm_core(mixed) * gains[1:2, :]).astype(BF16)
    queries = nt(normed, weight[...]).astype(BF16).astype(F32) * HEAD ** (-0.5)
    queries_out[...] = queries.reshape(queries_out.shape).astype(BF16)
    start = pl.multiple_of(lax.axis_index("helper") * row_n, row_n)
    own_rows[...] = mixed_ref[:, pl.ds(start, row_n), :]


def hand_on_kernel(value, *rest):
    out = rest[-1]
    out[...] = value[...]


def both_kernel(own, got, waited, out, sems):
    del waited
    row_n = own.shape[0]
    copies = [
        pltpu.make_async_copy(own, out.at[pl.ds(0, row_n)], sems.at[0]),
        pltpu.make_async_copy(got, out.at[pl.ds(row_n, row_n)], sems.at[1]),
    ]
    for copy in copies:
        copy.start()
    for copy in copies:
        copy.wait()


def cross_pairs(places, helper_n, queries, table, arrived, put):
    for at, (place, block) in enumerate(zip(places, arrived)):
        chosen = queries[0].astype(F32)
        for image in range(1, queries.shape[0]):
            chosen = jnp.where(table[place : place + 1, 0:1] == image, queries[image].astype(F32), chosen)
        columns = block.shape[0] // 2
        context = attend(head_stack(chosen), block[:columns, :], block[columns:, :])
        row_n = context.shape[0] // helper_n
        for helper in range(helper_n):
            put(at, helper, pack(context[helper * row_n : (helper + 1) * row_n]))


def cross_kernel(places, helper_n, queries, table, *rest):
    *arrived, out = rest

    def put(at, helper, rows):
        out[helper, at] = rows

    cross_pairs(places, helper_n, queries, table, arrived, put)


def last_cross_kernel(places, helper_n, queries, table, before, *rest):
    arrived, (*outs, held) = rest[: len(places)], rest[len(places) :]
    first = before.shape[1]
    helper = lax.axis_index("helper")
    for k, out in enumerate(outs):
        out[:first] = before[jnp.bitwise_xor(helper, k)]

    def put(at, helper, rows):
        held[helper, at] = rows

    cross_pairs(places, helper_n, queries, table, arrived, put)
    for k, out in enumerate(outs):
        out[first:] = held[jnp.bitwise_xor(helper, k)]


def side_rows(block):
    row_n = block.shape[1] * 2 // 3
    main, tail = block[:, :row_n, :], block[:, row_n:, :]
    tail = jnp.concatenate([tail[:, :, :HEAD], tail[:, :, HEAD:]], 1)
    return jnp.concatenate([main.reshape(-1, LANES), tail.reshape(-1, HEAD)], 1)


def out_kernel(order, own_rows, table, own_weights, core_weights, *rest):
    own, across_chip, across_both, across_core, out, out_v, sems = rest
    sides = [own, across_chip, across_core, across_both]
    row_n, width = own_rows.shape[1:]
    pair_n = len(order)
    placed = []
    for side in sides:
        pairs = [side[at].astype(F32) for at in range(pair_n)]
        for position in range(pair_n):
            block = pairs[0]
            for at in range(1, pair_n):
                row = pair_n + order[at]
                block = jnp.where(table[row : row + 1, 0:1] == position, pairs[at], block)
            placed.append(block.astype(BF16)[None])
    rows = [
        side_rows(jnp.concatenate(placed[at * pair_n : (at + 1) * pair_n], 0)) for at in range(len(sides))
    ]
    half = len(sides) // 2
    terms = nn(jnp.concatenate(rows[:half], 1), own_weights[...])
    terms = terms + nn(jnp.concatenate(rows[half:], 1), core_weights[...])
    first_n = table[2 * pair_n :, 0:1]
    zero = jnp.zeros((row_n, width), F32)
    for position in range(pair_n):
        term = terms[position * row_n : (position + 1) * row_n]
        is_first = first_n > position
        out_v[0, position] = jnp.where(is_first, own_rows[0] + term, zero).astype(BF16)
        out_v[1, pair_n - 1 - position] = jnp.where(is_first, zero, own_rows[1] + term).astype(BF16)
    copies = [pltpu.make_async_copy(out_v.at[image], out.at[image], sems.at[image]) for image in range(2)]
    for copy in copies:
        copy.start()
    for copy in copies:
        copy.wait()


def local(owner_n, helper_n, states, partners, self_proj, self_out, cross_proj, cross_out, gains):
    image_n, patch_n, width = states.shape
    slot_n = partners.shape[1]
    columns = self_proj.shape[2]
    row_n = patch_n // helper_n
    row_all = image_n * patch_n
    swaps = owner_swaps(slot_n, owner_n)
    pair_n = len(swaps)
    self_proj_t = jnp.swapaxes(self_proj, 1, 2)
    cross_proj_t = jnp.swapaxes(cross_proj, 1, 2)
    chip_hop, core_hop = helper_n // 2, 1

    def across(value, k):
        return lax.ppermute(value, "helper", [(j, j ^ k) for j in range(helper_n)])

    def exchange(value, swap):
        return lax.ppermute(value, "owner", [(o, swap_target(o, swap, owner_n)) for o in range(owner_n)])

    def call(name, kernel, out_shape, in_specs, scratch, *operands, out_specs=None, flops=1):
        with jax.named_scope(name):
            return pl.pallas_call(
                kernel,
                out_shape=out_shape,
                in_specs=in_specs,
                out_specs=out_specs or jax.tree.map(lambda _: VMEM, out_shape),
                scratch_shapes=scratch,
                compiler_params=pltpu.CompilerParams(vmem_limit_bytes=VMEM_BYTES),
                cost_estimate=pl.CostEstimate(flops=flops, bytes_accessed=1, transcendentals=0),
            )(*operands)

    shape = jax.ShapeDtypeStruct
    dma = pltpu.SemaphoreType.DMA
    index_table = pltpu.SMEM(partners.shape, jnp.int32)
    block = shape((2 * columns, patch_n), BF16)

    partners_h = pltpu.with_memory_space_constraint(partners, pltpu.HBM)
    self_out_got = across(self_out, chip_hop)
    *outgoing, context, table, query_weight, cross_out_own = call(
        "own_images",
        functools.partial(own_images_kernel, swaps, owner_n),
        [block] * pair_n
        + [
            shape((row_all * columns // LANES, LANES), BF16),
            shape((2 * pair_n + 1, LANES), jnp.int32),
            shape((columns, width), BF16),
            shape(cross_out.shape, BF16),
        ],
        [HBM] * 6,
        [
            pltpu.VMEM(states.shape, BF16),
            pltpu.VMEM(gains.shape, F32),
            pltpu.VMEM((3, columns, width), BF16),
            pltpu.VMEM((2, columns, width), BF16),
            index_table,
            pltpu.VMEM((image_n, 2 * columns, patch_n), BF16),
            dma((7,)),
        ],
        *[pltpu.with_memory_space_constraint(x, pltpu.HBM) for x in (states, gains, self_proj_t, cross_proj_t)],
        partners_h,
        pltpu.with_memory_space_constraint(cross_out, pltpu.HBM),
    )
    arrived = [exchange(value, swap) for value, swap in zip(outgoing, swaps)]
    context_got = across(context, chip_hop)
    near = (slot_n - 1) // 2
    late = [at for at, (_, colour) in enumerate(swaps) if colour]
    early = [at for at in range(pair_n) if at not in late]
    short = [2 * near - 2, 2 * near - 1]
    cross_out_sent = call(
        "cross_output_rows",
        hand_on_kernel,
        shape(cross_out.shape, BF16),
        [VMEM] + [ANY] * len([arrived[short[0]]]),
        [],
        cross_out_own, *[arrived[short[0]]],
    )
    cross_out_got = across(cross_out_sent, chip_hop)
    before = [arrived[at] for at in short] + [self_out_got, arrived[0]]
    gains_then = call(
        "gains",
        hand_on_kernel,
        shape(gains.shape, F32),
        [VMEM] + [ANY] * len(before),
        [],
        gains, *before,
    )

    made_shapes = [
        shape((image_n, row_n, width), F32),
        shape((image_n, patch_n, columns), BF16),
    ]

    def mixing(states, gains, query_weight, context, context_got, self_out, self_out_got):
        base, sent = call(
            "self_output_share",
            partial_kernel,
            [shape((row_all, width), F32), shape((row_all, width), BF16)],
            [VMEM] * 5,
            [],
            states, context, context_got, self_out, self_out_got,
        )
        made = call(
            "mixed_and_queries",
            functools.partial(query_kernel, helper_n),
            made_shapes,
            [VMEM] * 4,
            [pltpu.VMEM((image_n, patch_n, width), F32)],
            base, across(sent, core_hop), gains, query_weight,
        )
        return tuple(made)

    def no_images(*operands):
        return tuple(jnp.zeros(made.shape, made.dtype) for made in made_shapes)

    own_rows, queries = lax.cond(
        lax.axis_index("owner") < owner_n, mixing, no_images,
        states, gains_then, query_weight, context, context_got, self_out, self_out_got,
    )
    packed = columns * row_n // LANES
    early_sides = call(
        "early_cross_attention",
        functools.partial(cross_kernel, early, helper_n),
        shape((helper_n, len(early), packed, LANES), BF16),
        [VMEM] * (2 + len(early)),
        [],
        queries, table, *[arrived[at] for at in early],
        flops=EARLY_WEIGHT,
    )
    sides = call(
        "late_cross_attention",
        functools.partial(last_cross_kernel, late, helper_n),
        [shape((pair_n, packed, LANES), BF16)] * helper_n,
        [VMEM] * (3 + len(late)),
        [pltpu.VMEM((helper_n, len(late), packed, LANES), BF16)],
        queries, table, early_sides, *[arrived[at] for at in late],
        flops=LATE_WEIGHT,
    )
    sides = [sides[0]] + [across(sides[k], k) for k in range(1, helper_n)]
    cross_out_both = call(
        "cross_output_both_rows",
        both_kernel,
        shape((2 * columns, width), BF16),
        [VMEM, ANY, ANY],
        [dma((2,))],
        cross_out, cross_out_got, early_sides,
    )
    cross_out_core = across(cross_out_both, core_hop)
    return call(
        "pair_output",
        functools.partial(out_kernel, early + late),
        shape((image_n, slot_n, row_n, width), BF16),
        [VMEM] * (4 + helper_n),
        [pltpu.VMEM((image_n, slot_n, row_n, width), BF16), dma((image_n,))],
        own_rows, table, cross_out_both, cross_out_core,
        *[sides[k] for k in (0, chip_hop, chip_hop ^ core_hop, core_hop)],
        out_specs=HBM,
    )


def solution(mesh):
    return jax.shard_map(
        functools.partial(local, mesh.shape["owner"], mesh.shape["helper"]),
        mesh=mesh,
        in_specs=(
            P("owner", None, None),
            P("owner", None),
            P(None, None, "helper"),
            P("helper", None),
            P(None, None, "helper"),
            P("helper", None),
            P(),
        ),
        out_specs=P("owner", None, "helper", None),
        check_vma=False,
    )
```

```python
import functools

import jax
import jax.numpy as jnp
from jax import lax
from jax.experimental import pallas as pl
from jax.experimental.pallas import tpu as pltpu
from jax.sharding import PartitionSpec as P

HEAD = 64
LANES = 128
F32 = jnp.float32
BF16 = jnp.bfloat16
VMEM_BYTES = 24 * 1024 * 1024
EARLY_WEIGHT = 3 * 10**9
LATE_WEIGHT = 10**11

VMEM = pl.BlockSpec(memory_space=pltpu.VMEM)
HBM = pl.BlockSpec(memory_space=pltpu.HBM)
ANY = pl.BlockSpec(memory_space=pl.ANY)


def owner_swaps(slot_count, owner_count):
    near = (slot_count - 1) // 2
    swaps = [(owner_count // 2, 0)]
    for k in range(near, 1, -1):
        swaps += [(k, 1), (k, 0)]
    return swaps + [(1, 0), (1, 1)]


def swap_target(owner, swap, owner_count):
    distance, colour = swap
    step = distance & -distance
    if isinstance(owner, int):
        up = (owner // step) % 2 == colour
        return (owner + (distance if up else owner_count - distance)) % owner_count
    up = jnp.bitwise_and(lax.shift_right_logical(owner, step.bit_length() - 1), 1) == colour
    return lax.rem(owner + jnp.where(up, distance, owner_count - distance), owner_count)


def nn(left, right):
    return lax.dot_general(left, right, (((1,), (0,)), ((), ())), preferred_element_type=F32)


def nt(left, right):
    return lax.dot_general(left, right, (((1,), (1,)), ((), ())), preferred_element_type=F32)


def norm_core(values):
    row_mean = jnp.mean(values, -1, keepdims=True)
    centred = values - row_mean
    row_var = jnp.mean(centred * centred, -1, keepdims=True)
    return centred * lax.rsqrt(row_var + 1e-05)


def head_stack(queries):
    head_of = lax.broadcasted_iota(jnp.int32, queries.shape, 1) // HEAD
    zero = jnp.zeros((), queries.dtype)
    return jnp.concatenate(
        [jnp.where(head_of == h, queries, zero) for h in range(queries.shape[1] // HEAD)], 0
    ).astype(BF16)


def attend(stacked, keys_t, values_t):
    column_n = keys_t.shape[0]
    head_n = column_n // HEAD
    row_n = stacked.shape[0] // head_n
    scores = nn(stacked, keys_t)
    powers = jnp.exp(scores - jnp.max(scores, -1, keepdims=True))
    weights = (powers * (1.0 / jnp.sum(powers, -1, keepdims=True))).astype(BF16)
    spread = nt(weights, values_t)
    head_of = lax.broadcasted_iota(jnp.int32, (row_n, column_n), 1) // HEAD
    context = spread[(head_n - 1) * row_n :]
    for h in range(head_n - 1):
        context = jnp.where(head_of == h, spread[h * row_n : (h + 1) * row_n], context)
    return context


def pack(block):
    row_n = block.shape[0]
    tail = block[:, LANES:]
    return jnp.concatenate(
        [block[:, :LANES], jnp.concatenate([tail[: row_n // 2], tail[row_n // 2 :]], 1)], 0
    ).astype(BF16)


def pair_place(partners, owner, image_n):
    low = owner * image_n
    found_image, found_slot = jnp.int32(0), jnp.int32(0)
    for image in range(image_n):
        for slot in range(partners.shape[1]):
            gap = partners[image, slot] - low
            hit = jnp.logical_and(gap >= 0, gap < image_n)
            found_image = jnp.where(hit, jnp.int32(image), found_image)
            found_slot = jnp.where(hit, jnp.int32(slot), found_slot)
    return found_image, found_slot


def live_count(partners, image):
    count = jnp.int32(0)
    for slot in range(partners.shape[1]):
        count = count + jnp.where(partners[image, slot] >= 0, jnp.int32(1), jnp.int32(0))
    return count


def own_images_kernel(swaps, owner_n, states, gains, self_t, cross_t, partners, weight, *rest):
    outs, rest = rest[: len(swaps)], rest[len(swaps) :]
    context_out, table, query_weight_out, weight_out, states_v, gains_v, self_v, cross_v, partners_s, held, sems = rest
    image_n, patch_n, width = states.shape
    columns = self_t.shape[1]
    copies = [
        pltpu.make_async_copy(states, states_v, sems.at[0]),
        pltpu.make_async_copy(gains, gains_v, sems.at[1]),
        pltpu.make_async_copy(cross_t.at[pl.ds(1, 2)], cross_v, sems.at[2]),
        pltpu.make_async_copy(partners, partners_s, sems.at[3]),
        pltpu.make_async_copy(self_t, self_v, sems.at[4]),
        pltpu.make_async_copy(cross_t.at[0], query_weight_out, sems.at[5]),
        pltpu.make_async_copy(weight, weight_out, sems.at[6]),
    ]
    for copy in copies:
        copy.start()
    copies[0].wait()
    rows = norm_core(states_v[...].reshape(image_n * patch_n, width).astype(F32))
    for copy in copies[1:5]:
        copy.wait()
    normed = (rows * gains_v[2:3, :]).astype(BF16)
    projected = nt(cross_v[...].reshape(2 * columns, width), normed).astype(BF16)
    for image in range(image_n):
        held[image] = projected[:, image * patch_n : (image + 1) * patch_n]
    normed = (rows * gains_v[0:1, :]).astype(BF16)
    queries = nt(normed, self_v[0]).astype(BF16).astype(F32) * HEAD ** (-0.5)
    key_value = nt(self_v[1:3].reshape(2 * columns, width), normed).astype(BF16)
    contexts = []
    for image in range(image_n):
        span = slice(image * patch_n, (image + 1) * patch_n)
        contexts.append(
            attend(head_stack(queries[span]), key_value[:columns, span], key_value[columns:, span])
        )
    me = lax.axis_index("owner")
    pair_n = len(swaps)
    for at, (out, swap) in enumerate(zip(outs, swaps)):
        image, slot = pair_place(partners_s, swap_target(me, swap, owner_n), image_n)
        out[...] = held[image]
        position = jnp.where(image == 0, slot, pair_n - 1 - slot)
        table[at : at + 1, :] = jnp.full((1, LANES), image, jnp.int32)
        table[pair_n + at : pair_n + at + 1, :] = jnp.full((1, LANES), position, jnp.int32)
    table[2 * pair_n :, :] = jnp.full((1, LANES), live_count(partners_s, 0), jnp.int32)
    context_out[...] = pack(jnp.concatenate(contexts, 0))
    copies[5].wait()
    copies[6].wait()


def unpack(block):
    row_n = block.shape[0] * 2 // 3
    tail = block[row_n:, :]
    return jnp.concatenate(
        [block[:row_n, :], jnp.concatenate([tail[:, :HEAD], tail[:, HEAD:]], 0)], 1
    )


def partial_kernel(states, own, got, own_weight, got_weight, base, sent):
    rows = jnp.concatenate([unpack(own[...]), unpack(got[...])], 1)
    part = nn(rows, jnp.concatenate([own_weight[...], got_weight[...]], 0))
    sent[...] = part.astype(BF16)
    base[...] = states[...].reshape(part.shape).astype(F32) + part


def query_kernel(helper_n, base, got, gains, weight, own_rows, queries_out, mixed_ref):
    mixed = base[...] + got[...].astype(F32)
    image_n, row_n, width = own_rows.shape
    patch_n = row_n * helper_n
    mixed_ref[...] = mixed.reshape(image_n, patch_n, width)
    normed = (norm_core(mixed) * gains[1:2, :]).astype(BF16)
    queries = nt(normed, weight[...]).astype(BF16).astype(F32) * HEAD ** (-0.5)
    queries_out[...] = queries.reshape(queries_out.shape).astype(BF16)
    start = pl.multiple_of(lax.axis_index("helper") * row_n, row_n)
    own_rows[...] = mixed_ref[:, pl.ds(start, row_n), :]


def hand_on_kernel(value, *rest):
    out = rest[-1]
    out[...] = value[...]


def both_kernel(own, got, waited, out, sems):
    del waited
    row_n = own.shape[0]
    copies = [
        pltpu.make_async_copy(own, out.at[pl.ds(0, row_n)], sems.at[0]),
        pltpu.make_async_copy(got, out.at[pl.ds(row_n, row_n)], sems.at[1]),
    ]
    for copy in copies:
        copy.start()
    for copy in copies:
        copy.wait()


def cross_pairs(places, helper_n, queries, table, arrived, put):
    for at, (place, block) in enumerate(zip(places, arrived)):
        chosen = queries[0].astype(F32)
        for image in range(1, queries.shape[0]):
            chosen = jnp.where(table[place : place + 1, 0:1] == image, queries[image].astype(F32), chosen)
        columns = block.shape[0] // 2
        context = attend(head_stack(chosen), block[:columns, :], block[columns:, :])
        row_n = context.shape[0] // helper_n
        for helper in range(helper_n):
            put(at, helper, pack(context[helper * row_n : (helper + 1) * row_n]))


def cross_kernel(places, helper_n, queries, table, *rest):
    *arrived, out = rest

    def put(at, helper, rows):
        out[helper, at] = rows

    cross_pairs(places, helper_n, queries, table, arrived, put)


def last_cross_kernel(places, helper_n, queries, table, before, *rest):
    arrived, (*outs, held) = rest[: len(places)], rest[len(places) :]
    first = before.shape[1]
    helper = lax.axis_index("helper")
    for k, out in enumerate(outs):
        out[:first] = before[jnp.bitwise_xor(helper, k)]

    def put(at, helper, rows):
        held[helper, at] = rows

    cross_pairs(places, helper_n, queries, table, arrived, put)
    for k, out in enumerate(outs):
        out[first:] = held[jnp.bitwise_xor(helper, k)]


def side_rows(block):
    row_n = block.shape[1] * 2 // 3
    main, tail = block[:, :row_n, :], block[:, row_n:, :]
    tail = jnp.concatenate([tail[:, :, :HEAD], tail[:, :, HEAD:]], 1)
    return jnp.concatenate([main.reshape(-1, LANES), tail.reshape(-1, HEAD)], 1)


def out_kernel(order, own_rows, table, own_weights, core_weights, *rest):
    own, across_chip, across_both, across_core, out, out_v, sems = rest
    sides = [own, across_chip, across_core, across_both]
    row_n, width = own_rows.shape[1:]
    pair_n = len(order)
    placed = []
    for side in sides:
        pairs = [side[at].astype(F32) for at in range(pair_n)]
        for position in range(pair_n):
            block = pairs[0]
            for at in range(1, pair_n):
                row = pair_n + order[at]
                block = jnp.where(table[row : row + 1, 0:1] == position, pairs[at], block)
            placed.append(block.astype(BF16)[None])
    rows = [
        side_rows(jnp.concatenate(placed[at * pair_n : (at + 1) * pair_n], 0)) for at in range(len(sides))
    ]
    half = len(sides) // 2
    terms = nn(jnp.concatenate(rows[:half], 1), own_weights[...])
    terms = terms + nn(jnp.concatenate(rows[half:], 1), core_weights[...])
    first_n = table[2 * pair_n :, 0:1]
    zero = jnp.zeros((row_n, width), F32)
    for position in range(pair_n):
        term = terms[position * row_n : (position + 1) * row_n]
        is_first = first_n > position
        out_v[0, position] = jnp.where(is_first, own_rows[0] + term, zero).astype(BF16)
        out_v[1, pair_n - 1 - position] = jnp.where(is_first, zero, own_rows[1] + term).astype(BF16)
    copies = [pltpu.make_async_copy(out_v.at[image], out.at[image], sems.at[image]) for image in range(2)]
    for copy in copies:
        copy.start()
    for copy in copies:
        copy.wait()


def local(owner_n, helper_n, states, partners, self_proj, self_out, cross_proj, cross_out, gains):
    image_n, patch_n, width = states.shape
    slot_n = partners.shape[1]
    columns = self_proj.shape[2]
    row_n = patch_n // helper_n
    row_all = image_n * patch_n
    swaps = owner_swaps(slot_n, owner_n)
    pair_n = len(swaps)
    self_proj_t = jnp.swapaxes(self_proj, 1, 2)
    cross_proj_t = jnp.swapaxes(cross_proj, 1, 2)
    chip_hop, core_hop = helper_n // 2, 1

    def across(value, k):
        return lax.ppermute(value, "helper", [(j, j ^ k) for j in range(helper_n)])

    def exchange(value, swap):
        return lax.ppermute(value, "owner", [(o, swap_target(o, swap, owner_n)) for o in range(owner_n)])

    def call(name, kernel, out_shape, in_specs, scratch, *operands, out_specs=None, flops=1):
        with jax.named_scope(name):
            return pl.pallas_call(
                kernel,
                out_shape=out_shape,
                in_specs=in_specs,
                out_specs=out_specs or jax.tree.map(lambda _: VMEM, out_shape),
                scratch_shapes=scratch,
                compiler_params=pltpu.CompilerParams(vmem_limit_bytes=VMEM_BYTES),
                cost_estimate=pl.CostEstimate(flops=flops, bytes_accessed=1, transcendentals=0),
            )(*operands)

    shape = jax.ShapeDtypeStruct
    dma = pltpu.SemaphoreType.DMA
    index_table = pltpu.SMEM(partners.shape, jnp.int32)
    block = shape((2 * columns, patch_n), BF16)

    partners_h = pltpu.with_memory_space_constraint(partners, pltpu.HBM)
    self_out_got = across(self_out, chip_hop)
    *outgoing, context, table, query_weight, cross_out_own = call(
        "own_images",
        functools.partial(own_images_kernel, swaps, owner_n),
        [block] * pair_n
        + [
            shape((row_all * columns // LANES, LANES), BF16),
            shape((2 * pair_n + 1, LANES), jnp.int32),
            shape((columns, width), BF16),
            shape(cross_out.shape, BF16),
        ],
        [HBM] * 6,
        [
            pltpu.VMEM(states.shape, BF16),
            pltpu.VMEM(gains.shape, F32),
            pltpu.VMEM((3, columns, width), BF16),
            pltpu.VMEM((2, columns, width), BF16),
            index_table,
            pltpu.VMEM((image_n, 2 * columns, patch_n), BF16),
            dma((7,)),
        ],
        *[pltpu.with_memory_space_constraint(x, pltpu.HBM) for x in (states, gains, self_proj_t, cross_proj_t)],
        partners_h,
        pltpu.with_memory_space_constraint(cross_out, pltpu.HBM),
    )
    arrived = [exchange(value, swap) for value, swap in zip(outgoing, swaps)]
    context_got = across(context, chip_hop)
    near = (slot_n - 1) // 2
    late = [at for at, (_, colour) in enumerate(swaps) if colour]
    early = [at for at in range(pair_n) if at not in late]
    short = [2 * near - 2, 2 * near - 1]
    cross_out_sent = call(
        "cross_output_rows",
        hand_on_kernel,
        shape(cross_out.shape, BF16),
        [VMEM] + [ANY] * len([arrived[short[0]]]),
        [],
        cross_out_own, *[arrived[short[0]]],
    )
    cross_out_got = across(cross_out_sent, chip_hop)
    before = [arrived[at] for at in short] + [self_out_got]
    gains_then = call(
        "gains",
        hand_on_kernel,
        shape(gains.shape, F32),
        [VMEM] + [ANY] * len(before),
        [],
        gains, *before,
    )

    made_shapes = [
        shape((image_n, row_n, width), F32),
        shape((image_n, patch_n, columns), BF16),
    ]

    def mixing(states, gains, query_weight, context, context_got, self_out, self_out_got):
        base, sent = call(
            "self_output_share",
            partial_kernel,
            [shape((row_all, width), F32), shape((row_all, width), BF16)],
            [VMEM] * 5,
            [],
            states, context, context_got, self_out, self_out_got,
        )
        made = call(
            "mixed_and_queries",
            functools.partial(query_kernel, helper_n),
            made_shapes,
            [VMEM] * 4,
            [pltpu.VMEM((image_n, patch_n, width), F32)],
            base, across(sent, core_hop), gains, query_weight,
        )
        return tuple(made)

    def no_images(*operands):
        return tuple(jnp.zeros(made.shape, made.dtype) for made in made_shapes)

    own_rows, queries = lax.cond(
        lax.axis_index("owner") < owner_n, mixing, no_images,
        states, gains_then, query_weight, context, context_got, self_out, self_out_got,
    )
    packed = columns * row_n // LANES
    early_sides = call(
        "early_cross_attention",
        functools.partial(cross_kernel, early, helper_n),
        shape((helper_n, len(early), packed, LANES), BF16),
        [VMEM] * (2 + len(early)),
        [],
        queries, table, *[arrived[at] for at in early],
        flops=EARLY_WEIGHT,
    )
    sides = call(
        "late_cross_attention",
        functools.partial(last_cross_kernel, late, helper_n),
        [shape((pair_n, packed, LANES), BF16)] * helper_n,
        [VMEM] * (3 + len(late)),
        [pltpu.VMEM((helper_n, len(late), packed, LANES), BF16)],
        queries, table, early_sides, *[arrived[at] for at in late],
        flops=LATE_WEIGHT,
    )
    sides = [sides[0]] + [across(sides[k], k) for k in range(1, helper_n)]
    cross_out_both = call(
        "cross_output_both_rows",
        both_kernel,
        shape((2 * columns, width), BF16),
        [VMEM, ANY, ANY],
        [dma((2,))],
        cross_out, cross_out_got, early_sides,
    )
    cross_out_core = across(cross_out_both, core_hop)
    return call(
        "pair_output",
        functools.partial(out_kernel, early + late),
        shape((image_n, slot_n, row_n, width), BF16),
        [VMEM] * (4 + helper_n),
        [pltpu.VMEM((image_n, slot_n, row_n, width), BF16), dma((image_n,))],
        own_rows, table, cross_out_both, cross_out_core,
        *[sides[k] for k in (0, chip_hop, chip_hop ^ core_hop, core_hop)],
        out_specs=HBM,
    )


def solution(mesh):
    return jax.shard_map(
        functools.partial(local, mesh.shape["owner"], mesh.shape["helper"]),
        mesh=mesh,
        in_specs=(
            P("owner", None, None),
            P("owner", None),
            P(None, None, "helper"),
            P("helper", None),
            P(None, None, "helper"),
            P("helper", None),
            P(),
        ),
        out_specs=P("owner", None, "helper", None),
        check_vma=False,
    )
```

```python
import functools

import jax
import jax.numpy as jnp
from jax import lax
from jax.experimental import pallas as pl
from jax.experimental.pallas import tpu as pltpu
from jax.sharding import PartitionSpec as P

HEAD = 64
LANES = 128
F32 = jnp.float32
BF16 = jnp.bfloat16
VMEM_BYTES = 24 * 1024 * 1024
EARLY_WEIGHT = 3 * 10**9
LATE_WEIGHT = 10**11

VMEM = pl.BlockSpec(memory_space=pltpu.VMEM)
HBM = pl.BlockSpec(memory_space=pltpu.HBM)
ANY = pl.BlockSpec(memory_space=pl.ANY)


def owner_swaps(slot_count, owner_count):
    near = (slot_count - 1) // 2
    swaps = [(owner_count // 2, 0)]
    for k in range(near, 1, -1):
        swaps += [(k, 1), (k, 0)]
    return swaps + [(1, 0), (1, 1)]


def swap_target(owner, swap, owner_count):
    distance, colour = swap
    step = distance & -distance
    if isinstance(owner, int):
        up = (owner // step) % 2 == colour
        return (owner + (distance if up else owner_count - distance)) % owner_count
    up = jnp.bitwise_and(lax.shift_right_logical(owner, step.bit_length() - 1), 1) == colour
    return lax.rem(owner + jnp.where(up, distance, owner_count - distance), owner_count)


def nn(left, right):
    return lax.dot_general(left, right, (((1,), (0,)), ((), ())), preferred_element_type=F32)


def nt(left, right):
    return lax.dot_general(left, right, (((1,), (1,)), ((), ())), preferred_element_type=F32)


def norm_core(values):
    row_mean = jnp.mean(values, -1, keepdims=True)
    centred = values - row_mean
    row_var = jnp.mean(centred * centred, -1, keepdims=True)
    return centred * lax.rsqrt(row_var + 1e-05)


def head_stack(queries):
    head_of = lax.broadcasted_iota(jnp.int32, queries.shape, 1) // HEAD
    zero = jnp.zeros((), queries.dtype)
    return jnp.concatenate(
        [jnp.where(head_of == h, queries, zero) for h in range(queries.shape[1] // HEAD)], 0
    ).astype(BF16)


def attend(stacked, keys_t, values_t):
    column_n = keys_t.shape[0]
    head_n = column_n // HEAD
    row_n = stacked.shape[0] // head_n
    scores = nn(stacked, keys_t)
    weights = jnp.exp(scores - jnp.max(scores, -1, keepdims=True)).astype(BF16)
    spread = nt(weights, values_t)
    totals = nn(weights, jnp.ones((weights.shape[1], column_n), BF16))
    head_of = lax.broadcasted_iota(jnp.int32, (row_n, column_n), 1) // HEAD
    context, total = spread[(head_n - 1) * row_n :], totals[(head_n - 1) * row_n :]
    for h in range(head_n - 1):
        context = jnp.where(head_of == h, spread[h * row_n : (h + 1) * row_n], context)
        total = jnp.where(head_of == h, totals[h * row_n : (h + 1) * row_n], total)
    return context / total


def pack(block):
    row_n = block.shape[0]
    tail = block[:, LANES:]
    return jnp.concatenate(
        [block[:, :LANES], jnp.concatenate([tail[: row_n // 2], tail[row_n // 2 :]], 1)], 0
    ).astype(BF16)


def pair_place(partners, owner, image_n):
    low = owner * image_n
    found_image, found_slot = jnp.int32(0), jnp.int32(0)
    for image in range(image_n):
        for slot in range(partners.shape[1]):
            gap = partners[image, slot] - low
            hit = jnp.logical_and(gap >= 0, gap < image_n)
            found_image = jnp.where(hit, jnp.int32(image), found_image)
            found_slot = jnp.where(hit, jnp.int32(slot), found_slot)
    return found_image, found_slot


def live_count(partners, image):
    count = jnp.int32(0)
    for slot in range(partners.shape[1]):
        count = count + jnp.where(partners[image, slot] >= 0, jnp.int32(1), jnp.int32(0))
    return count


def own_images_kernel(swaps, owner_n, states, gains, self_t, cross_t, partners, weight, *rest):
    outs, rest = rest[: len(swaps)], rest[len(swaps) :]
    context_out, table, query_weight_out, weight_out, states_v, gains_v, self_v, cross_v, partners_s, held, sems = rest
    image_n, patch_n, width = states.shape
    columns = self_t.shape[1]
    copies = [
        pltpu.make_async_copy(states, states_v, sems.at[0]),
        pltpu.make_async_copy(gains, gains_v, sems.at[1]),
        pltpu.make_async_copy(cross_t.at[pl.ds(1, 2)], cross_v, sems.at[2]),
        pltpu.make_async_copy(partners, partners_s, sems.at[3]),
        pltpu.make_async_copy(self_t, self_v, sems.at[4]),
        pltpu.make_async_copy(cross_t.at[0], query_weight_out, sems.at[5]),
        pltpu.make_async_copy(weight, weight_out, sems.at[6]),
    ]
    for copy in copies:
        copy.start()
    copies[0].wait()
    rows = norm_core(states_v[...].reshape(image_n * patch_n, width).astype(F32))
    for copy in copies[1:5]:
        copy.wait()
    normed = (rows * gains_v[2:3, :]).astype(BF16)
    projected = nt(cross_v[...].reshape(2 * columns, width), normed).astype(BF16)
    for image in range(image_n):
        held[image] = projected[:, image * patch_n : (image + 1) * patch_n]
    normed = (rows * gains_v[0:1, :]).astype(BF16)
    queries = nt(normed, self_v[0]).astype(BF16).astype(F32) * HEAD ** (-0.5)
    key_value = nt(self_v[1:3].reshape(2 * columns, width), normed).astype(BF16)
    contexts = []
    for image in range(image_n):
        span = slice(image * patch_n, (image + 1) * patch_n)
        contexts.append(
            attend(head_stack(queries[span]), key_value[:columns, span], key_value[columns:, span])
        )
    me = lax.axis_index("owner")
    pair_n = len(swaps)
    for at, (out, swap) in enumerate(zip(outs, swaps)):
        image, slot = pair_place(partners_s, swap_target(me, swap, owner_n), image_n)
        out[...] = held[image]
        position = jnp.where(image == 0, slot, pair_n - 1 - slot)
        table[at : at + 1, :] = jnp.full((1, LANES), image, jnp.int32)
        table[pair_n + at : pair_n + at + 1, :] = jnp.full((1, LANES), position, jnp.int32)
    table[2 * pair_n :, :] = jnp.full((1, LANES), live_count(partners_s, 0), jnp.int32)
    context_out[...] = pack(jnp.concatenate(contexts, 0))
    copies[5].wait()
    copies[6].wait()


def unpack(block):
    row_n = block.shape[0] * 2 // 3
    tail = block[row_n:, :]
    return jnp.concatenate(
        [block[:row_n, :], jnp.concatenate([tail[:, :HEAD], tail[:, HEAD:]], 0)], 1
    )


def partial_kernel(states, own, got, own_weight, got_weight, base, sent):
    rows = jnp.concatenate([unpack(own[...]), unpack(got[...])], 1)
    part = nn(rows, jnp.concatenate([own_weight[...], got_weight[...]], 0))
    sent[...] = part.astype(BF16)
    base[...] = states[...].reshape(part.shape).astype(F32) + part


def query_kernel(helper_n, base, got, gains, weight, own_rows, queries_out, mixed_ref):
    mixed = base[...] + got[...].astype(F32)
    image_n, row_n, width = own_rows.shape
    patch_n = row_n * helper_n
    mixed_ref[...] = mixed.reshape(image_n, patch_n, width)
    normed = (norm_core(mixed) * gains[1:2, :]).astype(BF16)
    queries = nt(normed, weight[...]).astype(BF16).astype(F32) * HEAD ** (-0.5)
    queries_out[...] = queries.reshape(queries_out.shape).astype(BF16)
    start = pl.multiple_of(lax.axis_index("helper") * row_n, row_n)
    own_rows[...] = mixed_ref[:, pl.ds(start, row_n), :]


def hand_on_kernel(value, *rest):
    out = rest[-1]
    out[...] = value[...]


def both_kernel(own, got, waited, out, sems):
    del waited
    row_n = own.shape[0]
    copies = [
        pltpu.make_async_copy(own, out.at[pl.ds(0, row_n)], sems.at[0]),
        pltpu.make_async_copy(got, out.at[pl.ds(row_n, row_n)], sems.at[1]),
    ]
    for copy in copies:
        copy.start()
    for copy in copies:
        copy.wait()


def cross_pairs(places, helper_n, queries, table, arrived, put):
    for at, (place, block) in enumerate(zip(places, arrived)):
        chosen = queries[0].astype(F32)
        for image in range(1, queries.shape[0]):
            chosen = jnp.where(table[place : place + 1, 0:1] == image, queries[image].astype(F32), chosen)
        columns = block.shape[0] // 2
        context = attend(head_stack(chosen), block[:columns, :], block[columns:, :])
        row_n = context.shape[0] // helper_n
        for helper in range(helper_n):
            put(at, helper, pack(context[helper * row_n : (helper + 1) * row_n]))


def cross_kernel(places, helper_n, queries, table, *rest):
    *arrived, out = rest

    def put(at, helper, rows):
        out[helper, at] = rows

    cross_pairs(places, helper_n, queries, table, arrived, put)


def last_cross_kernel(places, helper_n, queries, table, before, *rest):
    arrived, (*outs, held) = rest[: len(places)], rest[len(places) :]
    first = before.shape[1]
    helper = lax.axis_index("helper")
    for k, out in enumerate(outs):
        out[:first] = before[jnp.bitwise_xor(helper, k)]

    def put(at, helper, rows):
        held[helper, at] = rows

    cross_pairs(places, helper_n, queries, table, arrived, put)
    for k, out in enumerate(outs):
        out[first:] = held[jnp.bitwise_xor(helper, k)]


def side_rows(block):
    row_n = block.shape[1] * 2 // 3
    main, tail = block[:, :row_n, :], block[:, row_n:, :]
    tail = jnp.concatenate([tail[:, :, :HEAD], tail[:, :, HEAD:]], 1)
    return jnp.concatenate([main.reshape(-1, LANES), tail.reshape(-1, HEAD)], 1)


def out_kernel(order, own_rows, table, own_weights, core_weights, *rest):
    own, across_chip, across_both, across_core, out, out_v, sems = rest
    sides = [own, across_chip, across_core, across_both]
    row_n, width = own_rows.shape[1:]
    pair_n = len(order)
    placed = []
    for side in sides:
        pairs = [side[at].astype(F32) for at in range(pair_n)]
        for position in range(pair_n):
            block = pairs[0]
            for at in range(1, pair_n):
                row = pair_n + order[at]
                block = jnp.where(table[row : row + 1, 0:1] == position, pairs[at], block)
            placed.append(block.astype(BF16)[None])
    rows = [
        side_rows(jnp.concatenate(placed[at * pair_n : (at + 1) * pair_n], 0)) for at in range(len(sides))
    ]
    half = len(sides) // 2
    terms = nn(jnp.concatenate(rows[:half], 1), own_weights[...])
    terms = terms + nn(jnp.concatenate(rows[half:], 1), core_weights[...])
    first_n = table[2 * pair_n :, 0:1]
    zero = jnp.zeros((row_n, width), F32)
    for position in range(pair_n):
        term = terms[position * row_n : (position + 1) * row_n]
        is_first = first_n > position
        out_v[0, position] = jnp.where(is_first, own_rows[0] + term, zero).astype(BF16)
        out_v[1, pair_n - 1 - position] = jnp.where(is_first, zero, own_rows[1] + term).astype(BF16)
    copies = [pltpu.make_async_copy(out_v.at[image], out.at[image], sems.at[image]) for image in range(2)]
    for copy in copies:
        copy.start()
    for copy in copies:
        copy.wait()


def local(owner_n, helper_n, states, partners, self_proj, self_out, cross_proj, cross_out, gains):
    image_n, patch_n, width = states.shape
    slot_n = partners.shape[1]
    columns = self_proj.shape[2]
    row_n = patch_n // helper_n
    row_all = image_n * patch_n
    swaps = owner_swaps(slot_n, owner_n)
    pair_n = len(swaps)
    self_proj_t = jnp.swapaxes(self_proj, 1, 2)
    cross_proj_t = jnp.swapaxes(cross_proj, 1, 2)
    chip_hop, core_hop = helper_n // 2, 1

    def across(value, k):
        return lax.ppermute(value, "helper", [(j, j ^ k) for j in range(helper_n)])

    def exchange(value, swap):
        return lax.ppermute(value, "owner", [(o, swap_target(o, swap, owner_n)) for o in range(owner_n)])

    def call(name, kernel, out_shape, in_specs, scratch, *operands, out_specs=None, flops=1):
        with jax.named_scope(name):
            return pl.pallas_call(
                kernel,
                out_shape=out_shape,
                in_specs=in_specs,
                out_specs=out_specs or jax.tree.map(lambda _: VMEM, out_shape),
                scratch_shapes=scratch,
                compiler_params=pltpu.CompilerParams(vmem_limit_bytes=VMEM_BYTES),
                cost_estimate=pl.CostEstimate(flops=flops, bytes_accessed=1, transcendentals=0),
            )(*operands)

    shape = jax.ShapeDtypeStruct
    dma = pltpu.SemaphoreType.DMA
    index_table = pltpu.SMEM(partners.shape, jnp.int32)
    block = shape((2 * columns, patch_n), BF16)

    partners_h = pltpu.with_memory_space_constraint(partners, pltpu.HBM)
    self_out_got = across(self_out, chip_hop)
    *outgoing, context, table, query_weight, cross_out_own = call(
        "own_images",
        functools.partial(own_images_kernel, swaps, owner_n),
        [block] * pair_n
        + [
            shape((row_all * columns // LANES, LANES), BF16),
            shape((2 * pair_n + 1, LANES), jnp.int32),
            shape((columns, width), BF16),
            shape(cross_out.shape, BF16),
        ],
        [HBM] * 6,
        [
            pltpu.VMEM(states.shape, BF16),
            pltpu.VMEM(gains.shape, F32),
            pltpu.VMEM((3, columns, width), BF16),
            pltpu.VMEM((2, columns, width), BF16),
            index_table,
            pltpu.VMEM((image_n, 2 * columns, patch_n), BF16),
            dma((7,)),
        ],
        *[pltpu.with_memory_space_constraint(x, pltpu.HBM) for x in (states, gains, self_proj_t, cross_proj_t)],
        partners_h,
        pltpu.with_memory_space_constraint(cross_out, pltpu.HBM),
    )
    arrived = [exchange(value, swap) for value, swap in zip(outgoing, swaps)]
    context_got = across(context, chip_hop)
    near = (slot_n - 1) // 2
    late = [at for at, (_, colour) in enumerate(swaps) if colour]
    early = [at for at in range(pair_n) if at not in late]
    short = [2 * near - 2, 2 * near - 1]
    cross_out_sent = call(
        "cross_output_rows",
        hand_on_kernel,
        shape(cross_out.shape, BF16),
        [VMEM] + [ANY] * len([arrived[short[1]]]),
        [],
        cross_out_own, *[arrived[short[1]]],
    )
    cross_out_got = across(cross_out_sent, chip_hop)
    before = [arrived[at] for at in short] + [self_out_got]
    gains_then = call(
        "gains",
        hand_on_kernel,
        shape(gains.shape, F32),
        [VMEM] + [ANY] * len(before),
        [],
        gains, *before,
    )

    made_shapes = [
        shape((image_n, row_n, width), F32),
        shape((image_n, patch_n, columns), BF16),
    ]

    def mixing(states, gains, query_weight, context, context_got, self_out, self_out_got):
        base, sent = call(
            "self_output_share",
            partial_kernel,
            [shape((row_all, width), F32), shape((row_all, width), BF16)],
            [VMEM] * 5,
            [],
            states, context, context_got, self_out, self_out_got,
        )
        made = call(
            "mixed_and_queries",
            functools.partial(query_kernel, helper_n),
            made_shapes,
            [VMEM] * 4,
            [pltpu.VMEM((image_n, patch_n, width), F32)],
            base, across(sent, core_hop), gains, query_weight,
        )
        return tuple(made)

    def no_images(*operands):
        return tuple(jnp.zeros(made.shape, made.dtype) for made in made_shapes)

    own_rows, queries = lax.cond(
        lax.axis_index("owner") < owner_n, mixing, no_images,
        states, gains_then, query_weight, context, context_got, self_out, self_out_got,
    )
    packed = columns * row_n // LANES
    early_sides = call(
        "early_cross_attention",
        functools.partial(cross_kernel, early, helper_n),
        shape((helper_n, len(early), packed, LANES), BF16),
        [VMEM] * (2 + len(early)),
        [],
        queries, table, *[arrived[at] for at in early],
        flops=EARLY_WEIGHT,
    )
    sides = call(
        "late_cross_attention",
        functools.partial(last_cross_kernel, late, helper_n),
        [shape((pair_n, packed, LANES), BF16)] * helper_n,
        [VMEM] * (3 + len(late)),
        [pltpu.VMEM((helper_n, len(late), packed, LANES), BF16)],
        queries, table, early_sides, *[arrived[at] for at in late],
        flops=LATE_WEIGHT,
    )
    sides = [sides[0]] + [across(sides[k], k) for k in range(1, helper_n)]
    cross_out_both = call(
        "cross_output_both_rows",
        both_kernel,
        shape((2 * columns, width), BF16),
        [VMEM, ANY, ANY],
        [dma((2,))],
        cross_out, cross_out_got, early_sides,
    )
    cross_out_core = across(cross_out_both, core_hop)
    return call(
        "pair_output",
        functools.partial(out_kernel, early + late),
        shape((image_n, slot_n, row_n, width), BF16),
        [VMEM] * (4 + helper_n),
        [pltpu.VMEM((image_n, slot_n, row_n, width), BF16), dma((image_n,))],
        own_rows, table, cross_out_both, cross_out_core,
        *[sides[k] for k in (0, chip_hop, chip_hop ^ core_hop, core_hop)],
        out_specs=HBM,
    )


def solution(mesh):
    return jax.shard_map(
        functools.partial(local, mesh.shape["owner"], mesh.shape["helper"]),
        mesh=mesh,
        in_specs=(
            P("owner", None, None),
            P("owner", None),
            P(None, None, "helper"),
            P("helper", None),
            P(None, None, "helper"),
            P("helper", None),
            P(),
        ),
        out_specs=P("owner", None, "helper", None),
        check_vma=False,
    )
```

```python
import functools

import jax
import jax.numpy as jnp
from jax import lax
from jax.experimental import pallas as pl
from jax.experimental.pallas import tpu as pltpu
from jax.sharding import PartitionSpec as P

HEAD = 64
LANES = 128
F32 = jnp.float32
BF16 = jnp.bfloat16
VMEM_BYTES = 24 * 1024 * 1024
EARLY_WEIGHT = 3 * 10**9
LATE_WEIGHT = 10**11

VMEM = pl.BlockSpec(memory_space=pltpu.VMEM)
HBM = pl.BlockSpec(memory_space=pltpu.HBM)
ANY = pl.BlockSpec(memory_space=pl.ANY)


def owner_swaps(slot_count, owner_count):
    near = (slot_count - 1) // 2
    swaps = [(owner_count // 2, 0)]
    for k in range(near, 1, -1):
        swaps += [(k, 1), (k, 0)]
    return swaps + [(1, 0), (1, 1)]


def swap_target(owner, swap, owner_count):
    distance, colour = swap
    step = distance & -distance
    if isinstance(owner, int):
        up = (owner // step) % 2 == colour
        return (owner + (distance if up else owner_count - distance)) % owner_count
    up = jnp.bitwise_and(lax.shift_right_logical(owner, step.bit_length() - 1), 1) == colour
    return lax.rem(owner + jnp.where(up, distance, owner_count - distance), owner_count)


def nn(left, right):
    return lax.dot_general(left, right, (((1,), (0,)), ((), ())), preferred_element_type=F32)


def nt(left, right):
    return lax.dot_general(left, right, (((1,), (1,)), ((), ())), preferred_element_type=F32)


def norm_core(values):
    row_mean = jnp.mean(values, -1, keepdims=True)
    centred = values - row_mean
    row_var = jnp.mean(centred * centred, -1, keepdims=True)
    return centred * lax.rsqrt(row_var + 1e-05)


def head_stack(queries):
    head_of = lax.broadcasted_iota(jnp.int32, queries.shape, 1) // HEAD
    zero = jnp.zeros((), queries.dtype)
    return jnp.concatenate(
        [jnp.where(head_of == h, queries, zero) for h in range(queries.shape[1] // HEAD)], 0
    ).astype(BF16)


def attend(stacked, keys_t, values_t):
    column_n = keys_t.shape[0]
    head_n = column_n // HEAD
    row_n = stacked.shape[0] // head_n
    scores = nn(stacked, keys_t)
    powers = jnp.exp(scores - jnp.max(scores, -1, keepdims=True))
    weights = (powers * (1.0 / jnp.sum(powers, -1, keepdims=True))).astype(BF16)
    spread = nt(weights, values_t)
    head_of = lax.broadcasted_iota(jnp.int32, (row_n, column_n), 1) // HEAD
    context = spread[(head_n - 1) * row_n :]
    for h in range(head_n - 1):
        context = jnp.where(head_of == h, spread[h * row_n : (h + 1) * row_n], context)
    return context


def pack(block):
    row_n = block.shape[0]
    tail = block[:, LANES:]
    return jnp.concatenate(
        [block[:, :LANES], jnp.concatenate([tail[: row_n // 2], tail[row_n // 2 :]], 1)], 0
    ).astype(BF16)


def pair_place(partners, owner, image_n):
    low = owner * image_n
    found_image, found_slot = jnp.int32(0), jnp.int32(0)
    for image in range(image_n):
        for slot in range(partners.shape[1]):
            gap = partners[image, slot] - low
            hit = jnp.logical_and(gap >= 0, gap < image_n)
            found_image = jnp.where(hit, jnp.int32(image), found_image)
            found_slot = jnp.where(hit, jnp.int32(slot), found_slot)
    return found_image, found_slot


def live_count(partners, image):
    count = jnp.int32(0)
    for slot in range(partners.shape[1]):
        count = count + jnp.where(partners[image, slot] >= 0, jnp.int32(1), jnp.int32(0))
    return count


def own_images_kernel(swaps, owner_n, states, gains, self_t, cross_t, partners, weight, *rest):
    outs, rest = rest[: len(swaps)], rest[len(swaps) :]
    context_out, table, query_weight_out, weight_out, states_v, gains_v, self_v, cross_v, partners_s, held, sems = rest
    image_n, patch_n, width = states.shape
    columns = self_t.shape[1]
    copies = [
        pltpu.make_async_copy(states, states_v, sems.at[0]),
        pltpu.make_async_copy(gains, gains_v, sems.at[1]),
        pltpu.make_async_copy(cross_t.at[pl.ds(1, 2)], cross_v, sems.at[2]),
        pltpu.make_async_copy(partners, partners_s, sems.at[3]),
        pltpu.make_async_copy(self_t, self_v, sems.at[4]),
        pltpu.make_async_copy(cross_t.at[0], query_weight_out, sems.at[5]),
        pltpu.make_async_copy(weight, weight_out, sems.at[6]),
    ]
    for copy in copies:
        copy.start()
    copies[0].wait()
    rows = norm_core(states_v[...].reshape(image_n * patch_n, width).astype(F32))
    for copy in copies[1:5]:
        copy.wait()
    normed = (rows * gains_v[2:3, :]).astype(BF16)
    projected = nt(cross_v[...].reshape(2 * columns, width), normed).astype(BF16)
    for image in range(image_n):
        held[image] = projected[:, image * patch_n : (image + 1) * patch_n]
    normed = (rows * gains_v[0:1, :]).astype(BF16)
    queries = nt(normed, self_v[0]).astype(BF16).astype(F32) * HEAD ** (-0.5)
    key_value = nt(self_v[1:3].reshape(2 * columns, width), normed).astype(BF16)
    contexts = []
    for image in range(image_n):
        span = slice(image * patch_n, (image + 1) * patch_n)
        contexts.append(
            attend(head_stack(queries[span]), key_value[:columns, span], key_value[columns:, span])
        )
    me = lax.axis_index("owner")
    pair_n = len(swaps)
    for at, (out, swap) in enumerate(zip(outs, swaps)):
        image, slot = pair_place(partners_s, swap_target(me, swap, owner_n), image_n)
        out[...] = held[image]
        position = jnp.where(image == 0, slot, pair_n - 1 - slot)
        table[at : at + 1, :] = jnp.full((1, LANES), image, jnp.int32)
        table[pair_n + at : pair_n + at + 1, :] = jnp.full((1, LANES), position, jnp.int32)
    table[2 * pair_n :, :] = jnp.full((1, LANES), live_count(partners_s, 0), jnp.int32)
    context_out[...] = pack(jnp.concatenate(contexts, 0))
    copies[5].wait()
    copies[6].wait()


def unpack(block):
    row_n = block.shape[0] * 2 // 3
    tail = block[row_n:, :]
    return jnp.concatenate(
        [block[:row_n, :], jnp.concatenate([tail[:, :HEAD], tail[:, HEAD:]], 0)], 1
    )


def partial_kernel(states, own, got, own_weight, got_weight, base, sent):
    rows = jnp.concatenate([unpack(own[...]), unpack(got[...])], 1)
    part = nn(rows, jnp.concatenate([own_weight[...], got_weight[...]], 0))
    sent[...] = part.astype(BF16)
    base[...] = states[...].reshape(part.shape).astype(F32) + part


def query_kernel(helper_n, base, got, gains, weight, own_rows, queries_out, mixed_ref):
    mixed = base[...] + got[...].astype(F32)
    image_n, row_n, width = own_rows.shape
    patch_n = row_n * helper_n
    mixed_ref[...] = mixed.reshape(image_n, patch_n, width)
    normed = (norm_core(mixed) * gains[1:2, :]).astype(BF16)
    queries = nt(normed, weight[...]).astype(BF16).astype(F32) * HEAD ** (-0.5)
    queries_out[...] = queries.reshape(queries_out.shape).astype(BF16)
    start = pl.multiple_of(lax.axis_index("helper") * row_n, row_n)
    own_rows[...] = mixed_ref[:, pl.ds(start, row_n), :]


def hand_on_kernel(value, *rest):
    out = rest[-1]
    out[...] = value[...]


def both_kernel(own, got, waited, out, sems):
    del waited
    row_n = own.shape[0]
    copies = [
        pltpu.make_async_copy(own, out.at[pl.ds(0, row_n)], sems.at[0]),
        pltpu.make_async_copy(got, out.at[pl.ds(row_n, row_n)], sems.at[1]),
    ]
    for copy in copies:
        copy.start()
    for copy in copies:
        copy.wait()


def cross_pairs(places, helper_n, queries, table, arrived, put):
    for at, (place, block) in enumerate(zip(places, arrived)):
        chosen = queries[0].astype(F32)
        for image in range(1, queries.shape[0]):
            chosen = jnp.where(table[place : place + 1, 0:1] == image, queries[image].astype(F32), chosen)
        columns = block.shape[0] // 2
        context = attend(head_stack(chosen), block[:columns, :], block[columns:, :])
        row_n = context.shape[0] // helper_n
        for helper in range(helper_n):
            put(at, helper, pack(context[helper * row_n : (helper + 1) * row_n]))


def cross_kernel(places, helper_n, queries, table, *rest):
    *arrived, out = rest

    def put(at, helper, rows):
        out[helper, at] = rows

    cross_pairs(places, helper_n, queries, table, arrived, put)


def last_cross_kernel(places, helper_n, queries, table, before, *rest):
    arrived, (*outs, held) = rest[: len(places)], rest[len(places) :]
    first = before.shape[1]
    helper = lax.axis_index("helper")
    for k, out in enumerate(outs):
        out[:first] = before[jnp.bitwise_xor(helper, k)]

    def put(at, helper, rows):
        held[helper, at] = rows

    cross_pairs(places, helper_n, queries, table, arrived, put)
    for k, out in enumerate(outs):
        out[first:] = held[jnp.bitwise_xor(helper, k)]


def side_rows(block):
    row_n = block.shape[1] * 2 // 3
    main, tail = block[:, :row_n, :], block[:, row_n:, :]
    tail = jnp.concatenate([tail[:, :, :HEAD], tail[:, :, HEAD:]], 1)
    return jnp.concatenate([main.reshape(-1, LANES), tail.reshape(-1, HEAD)], 1)


def out_kernel(order, own_rows, table, own_weights, core_weights, *rest):
    own, across_chip, across_both, across_core, out, out_v, sems = rest
    sides = [own, across_chip, across_core, across_both]
    row_n, width = own_rows.shape[1:]
    pair_n = len(order)
    placed = []
    for side in sides:
        pairs = [side[at].astype(F32) for at in range(pair_n)]
        for position in range(pair_n):
            block = pairs[0]
            for at in range(1, pair_n):
                row = pair_n + order[at]
                block = jnp.where(table[row : row + 1, 0:1] == position, pairs[at], block)
            placed.append(block.astype(BF16)[None])
    rows = [
        side_rows(jnp.concatenate(placed[at * pair_n : (at + 1) * pair_n], 0)) for at in range(len(sides))
    ]
    half = len(sides) // 2
    terms = nn(jnp.concatenate(rows[:half], 1), own_weights[...])
    terms = terms + nn(jnp.concatenate(rows[half:], 1), core_weights[...])
    first_n = table[2 * pair_n :, 0:1]
    zero = jnp.zeros((row_n, width), F32)
    for position in range(pair_n):
        term = terms[position * row_n : (position + 1) * row_n]
        is_first = first_n > position
        out_v[0, position] = jnp.where(is_first, own_rows[0] + term, zero).astype(BF16)
        out_v[1, pair_n - 1 - position] = jnp.where(is_first, zero, own_rows[1] + term).astype(BF16)
    copies = [pltpu.make_async_copy(out_v.at[image], out.at[image], sems.at[image]) for image in range(2)]
    for copy in copies:
        copy.start()
    for copy in copies:
        copy.wait()


def local(owner_n, helper_n, states, partners, self_proj, self_out, cross_proj, cross_out, gains):
    image_n, patch_n, width = states.shape
    slot_n = partners.shape[1]
    columns = self_proj.shape[2]
    row_n = patch_n // helper_n
    row_all = image_n * patch_n
    swaps = owner_swaps(slot_n, owner_n)
    pair_n = len(swaps)
    self_proj_t = jnp.swapaxes(self_proj, 1, 2)
    cross_proj_t = jnp.swapaxes(cross_proj, 1, 2)
    chip_hop, core_hop = helper_n // 2, 1

    def across(value, k):
        return lax.ppermute(value, "helper", [(j, j ^ k) for j in range(helper_n)])

    def exchange(value, swap):
        return lax.ppermute(value, "owner", [(o, swap_target(o, swap, owner_n)) for o in range(owner_n)])

    def call(name, kernel, out_shape, in_specs, scratch, *operands, out_specs=None, flops=1):
        with jax.named_scope(name):
            return pl.pallas_call(
                kernel,
                out_shape=out_shape,
                in_specs=in_specs,
                out_specs=out_specs or jax.tree.map(lambda _: VMEM, out_shape),
                scratch_shapes=scratch,
                compiler_params=pltpu.CompilerParams(vmem_limit_bytes=VMEM_BYTES),
                cost_estimate=pl.CostEstimate(flops=flops, bytes_accessed=1, transcendentals=0),
            )(*operands)

    shape = jax.ShapeDtypeStruct
    dma = pltpu.SemaphoreType.DMA
    index_table = pltpu.SMEM(partners.shape, jnp.int32)
    block = shape((2 * columns, patch_n), BF16)

    partners_h = pltpu.with_memory_space_constraint(partners, pltpu.HBM)
    self_out_got = across(self_out, chip_hop)
    *outgoing, context, table, query_weight, cross_out_own = call(
        "own_images",
        functools.partial(own_images_kernel, swaps, owner_n),
        [block] * pair_n
        + [
            shape((row_all * columns // LANES, LANES), BF16),
            shape((2 * pair_n + 1, LANES), jnp.int32),
            shape((columns, width), BF16),
            shape(cross_out.shape, BF16),
        ],
        [HBM] * 6,
        [
            pltpu.VMEM(states.shape, BF16),
            pltpu.VMEM(gains.shape, F32),
            pltpu.VMEM((3, columns, width), BF16),
            pltpu.VMEM((2, columns, width), BF16),
            index_table,
            pltpu.VMEM((image_n, 2 * columns, patch_n), BF16),
            dma((7,)),
        ],
        *[pltpu.with_memory_space_constraint(x, pltpu.HBM) for x in (states, gains, self_proj_t, cross_proj_t)],
        partners_h,
        pltpu.with_memory_space_constraint(cross_out, pltpu.HBM),
    )
    arrived = [exchange(value, swap) for value, swap in zip(outgoing, swaps)]
    context_got = across(context, chip_hop)
    near = (slot_n - 1) // 2
    late = [at for at, (_, colour) in enumerate(swaps) if colour]
    early = [at for at in range(pair_n) if at not in late]
    short = [2 * near - 2, 2 * near - 1]
    cross_out_sent = call(
        "cross_output_rows",
        hand_on_kernel,
        shape(cross_out.shape, BF16),
        [VMEM] + [ANY] * len([self_out_got]),
        [],
        cross_out_own, *[self_out_got],
    )
    cross_out_got = across(cross_out_sent, chip_hop)
    before = [arrived[at] for at in short] + [self_out_got]
    gains_then = call(
        "gains",
        hand_on_kernel,
        shape(gains.shape, F32),
        [VMEM] + [ANY] * len(before),
        [],
        gains, *before,
    )

    made_shapes = [
        shape((image_n, row_n, width), F32),
        shape((image_n, patch_n, columns), BF16),
    ]

    def mixing(states, gains, query_weight, context, context_got, self_out, self_out_got):
        base, sent = call(
            "self_output_share",
            partial_kernel,
            [shape((row_all, width), F32), shape((row_all, width), BF16)],
            [VMEM] * 5,
            [],
            states, context, context_got, self_out, self_out_got,
        )
        made = call(
            "mixed_and_queries",
            functools.partial(query_kernel, helper_n),
            made_shapes,
            [VMEM] * 4,
            [pltpu.VMEM((image_n, patch_n, width), F32)],
            base, across(sent, core_hop), gains, query_weight,
        )
        return tuple(made)

    def no_images(*operands):
        return tuple(jnp.zeros(made.shape, made.dtype) for made in made_shapes)

    own_rows, queries = lax.cond(
        lax.axis_index("owner") < owner_n, mixing, no_images,
        states, gains_then, query_weight, context, context_got, self_out, self_out_got,
    )
    packed = columns * row_n // LANES
    early_sides = call(
        "early_cross_attention",
        functools.partial(cross_kernel, early, helper_n),
        shape((helper_n, len(early), packed, LANES), BF16),
        [VMEM] * (2 + len(early)),
        [],
        queries, table, *[arrived[at] for at in early],
        flops=EARLY_WEIGHT,
    )
    sides = call(
        "late_cross_attention",
        functools.partial(last_cross_kernel, late, helper_n),
        [shape((pair_n, packed, LANES), BF16)] * helper_n,
        [VMEM] * (3 + len(late)),
        [pltpu.VMEM((helper_n, len(late), packed, LANES), BF16)],
        queries, table, early_sides, *[arrived[at] for at in late],
        flops=LATE_WEIGHT,
    )
    sides = [sides[0]] + [across(sides[k], k) for k in range(1, helper_n)]
    cross_out_both = call(
        "cross_output_both_rows",
        both_kernel,
        shape((2 * columns, width), BF16),
        [VMEM, ANY, ANY],
        [dma((2,))],
        cross_out, cross_out_got, early_sides,
    )
    cross_out_core = across(cross_out_both, core_hop)
    return call(
        "pair_output",
        functools.partial(out_kernel, early + late),
        shape((image_n, slot_n, row_n, width), BF16),
        [VMEM] * (4 + helper_n),
        [pltpu.VMEM((image_n, slot_n, row_n, width), BF16), dma((image_n,))],
        own_rows, table, cross_out_both, cross_out_core,
        *[sides[k] for k in (0, chip_hop, chip_hop ^ core_hop, core_hop)],
        out_specs=HBM,
    )


def solution(mesh):
    return jax.shard_map(
        functools.partial(local, mesh.shape["owner"], mesh.shape["helper"]),
        mesh=mesh,
        in_specs=(
            P("owner", None, None),
            P("owner", None),
            P(None, None, "helper"),
            P("helper", None),
            P(None, None, "helper"),
            P("helper", None),
            P(),
        ),
        out_specs=P("owner", None, "helper", None),
        check_vma=False,
    )
```

```python
import functools

import jax
import jax.numpy as jnp
from jax import lax
from jax.experimental import pallas as pl
from jax.experimental.pallas import tpu as pltpu
from jax.sharding import PartitionSpec as P

HEAD = 64
LANES = 128
F32 = jnp.float32
BF16 = jnp.bfloat16
VMEM_BYTES = 24 * 1024 * 1024
EARLY_WEIGHT = 3 * 10**9
LATE_WEIGHT = 10**11

VMEM = pl.BlockSpec(memory_space=pltpu.VMEM)
HBM = pl.BlockSpec(memory_space=pltpu.HBM)
ANY = pl.BlockSpec(memory_space=pl.ANY)


def owner_swaps(slot_count, owner_count):
    near = (slot_count - 1) // 2
    swaps = [(owner_count // 2, 0)]
    for k in range(near, 1, -1):
        swaps += [(k, 1), (k, 0)]
    return swaps + [(1, 0), (1, 1)]


def swap_target(owner, swap, owner_count):
    distance, colour = swap
    step = distance & -distance
    if isinstance(owner, int):
        up = (owner // step) % 2 == colour
        return (owner + (distance if up else owner_count - distance)) % owner_count
    up = jnp.bitwise_and(lax.shift_right_logical(owner, step.bit_length() - 1), 1) == colour
    return lax.rem(owner + jnp.where(up, distance, owner_count - distance), owner_count)


def nn(left, right):
    return lax.dot_general(left, right, (((1,), (0,)), ((), ())), preferred_element_type=F32)


def nt(left, right):
    return lax.dot_general(left, right, (((1,), (1,)), ((), ())), preferred_element_type=F32)


def norm_core(values):
    row_mean = jnp.mean(values, -1, keepdims=True)
    centred = values - row_mean
    row_var = jnp.mean(centred * centred, -1, keepdims=True)
    return centred * lax.rsqrt(row_var + 1e-05)


def head_stack(queries):
    head_of = lax.broadcasted_iota(jnp.int32, queries.shape, 1) // HEAD
    zero = jnp.zeros((), queries.dtype)
    return jnp.concatenate(
        [jnp.where(head_of == h, queries, zero) for h in range(queries.shape[1] // HEAD)], 0
    ).astype(BF16)


def attend(stacked, keys_t, values_t):
    column_n = keys_t.shape[0]
    head_n = column_n // HEAD
    row_n = stacked.shape[0] // head_n
    scores = nn(stacked, keys_t)
    powers = jnp.exp(scores - jnp.max(scores, -1, keepdims=True))
    weights = (powers * (1.0 / jnp.sum(powers, -1, keepdims=True))).astype(BF16)
    spread = nt(weights, values_t)
    head_of = lax.broadcasted_iota(jnp.int32, (row_n, column_n), 1) // HEAD
    context = spread[(head_n - 1) * row_n :]
    for h in range(head_n - 1):
        context = jnp.where(head_of == h, spread[h * row_n : (h + 1) * row_n], context)
    return context


def pack(block):
    row_n = block.shape[0]
    tail = block[:, LANES:]
    return jnp.concatenate(
        [block[:, :LANES], jnp.concatenate([tail[: row_n // 2], tail[row_n // 2 :]], 1)], 0
    ).astype(BF16)


def pair_place(partners, owner, image_n):
    low = owner * image_n
    found_image, found_slot = jnp.int32(0), jnp.int32(0)
    for image in range(image_n):
        for slot in range(partners.shape[1]):
            gap = partners[image, slot] - low
            hit = jnp.logical_and(gap >= 0, gap < image_n)
            found_image = jnp.where(hit, jnp.int32(image), found_image)
            found_slot = jnp.where(hit, jnp.int32(slot), found_slot)
    return found_image, found_slot


def live_count(partners, image):
    count = jnp.int32(0)
    for slot in range(partners.shape[1]):
        count = count + jnp.where(partners[image, slot] >= 0, jnp.int32(1), jnp.int32(0))
    return count


def own_images_kernel(swaps, owner_n, states, gains, self_t, cross_t, partners, weight, *rest):
    outs, rest = rest[: len(swaps)], rest[len(swaps) :]
    context_out, table, query_weight_out, weight_out, states_v, gains_v, self_v, cross_v, partners_s, held, sems = rest
    image_n, patch_n, width = states.shape
    columns = self_t.shape[1]
    copies = [
        pltpu.make_async_copy(states, states_v, sems.at[0]),
        pltpu.make_async_copy(gains, gains_v, sems.at[1]),
        pltpu.make_async_copy(cross_t.at[pl.ds(1, 2)], cross_v, sems.at[2]),
        pltpu.make_async_copy(partners, partners_s, sems.at[3]),
        pltpu.make_async_copy(self_t, self_v, sems.at[4]),
        pltpu.make_async_copy(cross_t.at[0], query_weight_out, sems.at[5]),
        pltpu.make_async_copy(weight, weight_out, sems.at[6]),
    ]
    for copy in copies:
        copy.start()
    copies[0].wait()
    rows = norm_core(states_v[...].reshape(image_n * patch_n, width).astype(F32))
    for copy in copies[1:5]:
        copy.wait()
    normed = (rows * gains_v[2:3, :]).astype(BF16)
    projected = nt(cross_v[...].reshape(2 * columns, width), normed).astype(BF16)
    for image in range(image_n):
        held[image] = projected[:, image * patch_n : (image + 1) * patch_n]
    normed = (rows * gains_v[0:1, :]).astype(BF16)
    queries = nt(normed, self_v[0]).astype(BF16).astype(F32) * HEAD ** (-0.5)
    key_value = nt(self_v[1:3].reshape(2 * columns, width), normed).astype(BF16)
    contexts = []
    for image in range(image_n):
        span = slice(image * patch_n, (image + 1) * patch_n)
        contexts.append(
            attend(head_stack(queries[span]), key_value[:columns, span], key_value[columns:, span])
        )
    me = lax.axis_index("owner")
    pair_n = len(swaps)
    for at, (out, swap) in enumerate(zip(outs, swaps)):
        image, slot = pair_place(partners_s, swap_target(me, swap, owner_n), image_n)
        out[...] = held[image]
        position = jnp.where(image == 0, slot, pair_n - 1 - slot)
        table[at : at + 1, :] = jnp.full((1, LANES), image, jnp.int32)
        table[pair_n + at : pair_n + at + 1, :] = jnp.full((1, LANES), position, jnp.int32)
    table[2 * pair_n :, :] = jnp.full((1, LANES), live_count(partners_s, 0), jnp.int32)
    context_out[...] = pack(jnp.concatenate(contexts, 0))
    copies[5].wait()
    copies[6].wait()


def unpack(block):
    row_n = block.shape[0] * 2 // 3
    tail = block[row_n:, :]
    return jnp.concatenate(
        [block[:row_n, :], jnp.concatenate([tail[:, :HEAD], tail[:, HEAD:]], 0)], 1
    )


def partial_kernel(states, own, got, own_weight, got_weight, base, sent):
    rows = jnp.concatenate([unpack(own[...]), unpack(got[...])], 1)
    part = nn(rows, jnp.concatenate([own_weight[...], got_weight[...]], 0))
    sent[...] = part.astype(BF16)
    base[...] = states[...].reshape(part.shape).astype(F32) + part


def query_kernel(helper_n, base, got, gains, weight, own_rows, queries_out, mixed_ref):
    mixed = base[...] + got[...].astype(F32)
    image_n, row_n, width = own_rows.shape
    patch_n = row_n * helper_n
    mixed_ref[...] = mixed.reshape(image_n, patch_n, width)
    normed = (norm_core(mixed) * gains[1:2, :]).astype(BF16)
    queries = nt(normed, weight[...]).astype(BF16).astype(F32) * HEAD ** (-0.5)
    queries_out[...] = queries.reshape(queries_out.shape).astype(BF16)
    start = pl.multiple_of(lax.axis_index("helper") * row_n, row_n)
    own_rows[...] = mixed_ref[:, pl.ds(start, row_n), :]


def hand_on_kernel(value, *rest):
    out = rest[-1]
    out[...] = value[...]


def both_kernel(own, got, waited, out, sems):
    del waited
    row_n = own.shape[0]
    copies = [
        pltpu.make_async_copy(own, out.at[pl.ds(0, row_n)], sems.at[0]),
        pltpu.make_async_copy(got, out.at[pl.ds(row_n, row_n)], sems.at[1]),
    ]
    for copy in copies:
        copy.start()
    for copy in copies:
        copy.wait()


def cross_pairs(places, helper_n, queries, table, arrived, put):
    for at, (place, block) in enumerate(zip(places, arrived)):
        chosen = queries[0].astype(F32)
        for image in range(1, queries.shape[0]):
            chosen = jnp.where(table[place : place + 1, 0:1] == image, queries[image].astype(F32), chosen)
        columns = block.shape[0] // 2
        context = attend(head_stack(chosen), block[:columns, :], block[columns:, :])
        row_n = context.shape[0] // helper_n
        for helper in range(helper_n):
            put(at, helper, pack(context[helper * row_n : (helper + 1) * row_n]))


def cross_kernel(places, helper_n, queries, table, *rest):
    *arrived, out = rest

    def put(at, helper, rows):
        out[helper, at] = rows

    cross_pairs(places, helper_n, queries, table, arrived, put)


def last_cross_kernel(places, helper_n, queries, table, before, *rest):
    arrived, (*outs, held) = rest[: len(places)], rest[len(places) :]
    first = before.shape[1]
    helper = lax.axis_index("helper")
    for k, out in enumerate(outs):
        out[:first] = before[jnp.bitwise_xor(helper, k)]

    def put(at, helper, rows):
        held[helper, at] = rows

    cross_pairs(places, helper_n, queries, table, arrived, put)
    for k, out in enumerate(outs):
        out[first:] = held[jnp.bitwise_xor(helper, k)]


def side_rows(block):
    row_n = block.shape[1] * 2 // 3
    main, tail = block[:, :row_n, :], block[:, row_n:, :]
    tail = jnp.concatenate([tail[:, :, :HEAD], tail[:, :, HEAD:]], 1)
    return jnp.concatenate([main.reshape(-1, LANES), tail.reshape(-1, HEAD)], 1)


def placed_rows(sides, order, table):
    pair_n = len(order)
    rows = []
    for side in sides:
        pairs = [side[at].astype(F32) for at in range(pair_n)]
        placed = []
        for position in range(pair_n):
            block = pairs[0]
            for at in range(1, pair_n):
                row = pair_n + order[at]
                block = jnp.where(table[row : row + 1, 0:1] == position, pairs[at], block)
            placed.append(block.astype(BF16)[None])
        rows.append(side_rows(jnp.concatenate(placed, 0)))
    return jnp.concatenate(rows, 1)


def first_terms_kernel(order, table, weights, own, across_chip, terms):
    terms[...] = nn(placed_rows((own, across_chip), order, table), weights[...])


def out_kernel(order, own_rows, table, weights, first, across_both, across_core, out, out_v, sems):
    row_n, width = own_rows.shape[1:]
    pair_n = len(order)
    terms = first[...] + nn(placed_rows((across_core, across_both), order, table), weights[...])
    first_n = table[2 * pair_n :, 0:1]
    zero = jnp.zeros((row_n, width), F32)
    for position in range(pair_n):
        term = terms[position * row_n : (position + 1) * row_n]
        is_first = first_n > position
        out_v[0, position] = jnp.where(is_first, own_rows[0] + term, zero).astype(BF16)
        out_v[1, pair_n - 1 - position] = jnp.where(is_first, zero, own_rows[1] + term).astype(BF16)
    copies = [pltpu.make_async_copy(out_v.at[image], out.at[image], sems.at[image]) for image in range(2)]
    for copy in copies:
        copy.start()
    for copy in copies:
        copy.wait()


def local(owner_n, helper_n, states, partners, self_proj, self_out, cross_proj, cross_out, gains):
    image_n, patch_n, width = states.shape
    slot_n = partners.shape[1]
    columns = self_proj.shape[2]
    row_n = patch_n // helper_n
    row_all = image_n * patch_n
    swaps = owner_swaps(slot_n, owner_n)
    pair_n = len(swaps)
    self_proj_t = jnp.swapaxes(self_proj, 1, 2)
    cross_proj_t = jnp.swapaxes(cross_proj, 1, 2)
    chip_hop, core_hop = helper_n // 2, 1

    def across(value, k):
        return lax.ppermute(value, "helper", [(j, j ^ k) for j in range(helper_n)])

    def exchange(value, swap):
        return lax.ppermute(value, "owner", [(o, swap_target(o, swap, owner_n)) for o in range(owner_n)])

    def call(name, kernel, out_shape, in_specs, scratch, *operands, out_specs=None, flops=1):
        with jax.named_scope(name):
            return pl.pallas_call(
                kernel,
                out_shape=out_shape,
                in_specs=in_specs,
                out_specs=out_specs or jax.tree.map(lambda _: VMEM, out_shape),
                scratch_shapes=scratch,
                compiler_params=pltpu.CompilerParams(vmem_limit_bytes=VMEM_BYTES),
                cost_estimate=pl.CostEstimate(flops=flops, bytes_accessed=1, transcendentals=0),
            )(*operands)

    shape = jax.ShapeDtypeStruct
    dma = pltpu.SemaphoreType.DMA
    index_table = pltpu.SMEM(partners.shape, jnp.int32)
    block = shape((2 * columns, patch_n), BF16)

    partners_h = pltpu.with_memory_space_constraint(partners, pltpu.HBM)
    self_out_got = across(self_out, chip_hop)
    *outgoing, context, table, query_weight, cross_out_own = call(
        "own_images",
        functools.partial(own_images_kernel, swaps, owner_n),
        [block] * pair_n
        + [
            shape((row_all * columns // LANES, LANES), BF16),
            shape((2 * pair_n + 1, LANES), jnp.int32),
            shape((columns, width), BF16),
            shape(cross_out.shape, BF16),
        ],
        [HBM] * 6,
        [
            pltpu.VMEM(states.shape, BF16),
            pltpu.VMEM(gains.shape, F32),
            pltpu.VMEM((3, columns, width), BF16),
            pltpu.VMEM((2, columns, width), BF16),
            index_table,
            pltpu.VMEM((image_n, 2 * columns, patch_n), BF16),
            dma((7,)),
        ],
        *[pltpu.with_memory_space_constraint(x, pltpu.HBM) for x in (states, gains, self_proj_t, cross_proj_t)],
        partners_h,
        pltpu.with_memory_space_constraint(cross_out, pltpu.HBM),
    )
    arrived = [exchange(value, swap) for value, swap in zip(outgoing, swaps)]
    context_got = across(context, chip_hop)
    near = (slot_n - 1) // 2
    late = [at for at, (_, colour) in enumerate(swaps) if colour]
    early = [at for at in range(pair_n) if at not in late]
    short = [2 * near - 2, 2 * near - 1]
    cross_out_sent = call(
        "cross_output_rows",
        hand_on_kernel,
        shape(cross_out.shape, BF16),
        [VMEM] + [ANY] * len([arrived[short[0]]]),
        [],
        cross_out_own, *[arrived[short[0]]],
    )
    cross_out_got = across(cross_out_sent, chip_hop)
    before = [arrived[at] for at in short] + [self_out_got]
    gains_then = call(
        "gains",
        hand_on_kernel,
        shape(gains.shape, F32),
        [VMEM] + [ANY] * len(before),
        [],
        gains, *before,
    )

    made_shapes = [
        shape((image_n, row_n, width), F32),
        shape((image_n, patch_n, columns), BF16),
    ]

    def mixing(states, gains, query_weight, context, context_got, self_out, self_out_got):
        base, sent = call(
            "self_output_share",
            partial_kernel,
            [shape((row_all, width), F32), shape((row_all, width), BF16)],
            [VMEM] * 5,
            [],
            states, context, context_got, self_out, self_out_got,
        )
        made = call(
            "mixed_and_queries",
            functools.partial(query_kernel, helper_n),
            made_shapes,
            [VMEM] * 4,
            [pltpu.VMEM((image_n, patch_n, width), F32)],
            base, across(sent, core_hop), gains, query_weight,
        )
        return tuple(made)

    def no_images(*operands):
        return tuple(jnp.zeros(made.shape, made.dtype) for made in made_shapes)

    own_rows, queries = lax.cond(
        lax.axis_index("owner") < owner_n, mixing, no_images,
        states, gains_then, query_weight, context, context_got, self_out, self_out_got,
    )
    packed = columns * row_n // LANES
    early_sides = call(
        "early_cross_attention",
        functools.partial(cross_kernel, early, helper_n),
        shape((helper_n, len(early), packed, LANES), BF16),
        [VMEM] * (2 + len(early)),
        [],
        queries, table, *[arrived[at] for at in early],
        flops=EARLY_WEIGHT,
    )
    sides = call(
        "late_cross_attention",
        functools.partial(last_cross_kernel, late, helper_n),
        [shape((pair_n, packed, LANES), BF16)] * helper_n,
        [VMEM] * (3 + len(late)),
        [pltpu.VMEM((helper_n, len(late), packed, LANES), BF16)],
        queries, table, early_sides, *[arrived[at] for at in late],
        flops=LATE_WEIGHT,
    )
    sides = [sides[0]] + [across(sides[k], k) for k in range(1, helper_n)]
    cross_out_both = call(
        "cross_output_both_rows",
        both_kernel,
        shape((2 * columns, width), BF16),
        [VMEM, ANY, ANY],
        [dma((2,))],
        cross_out, cross_out_got, early_sides,
    )
    cross_out_core = across(cross_out_both, core_hop)
    order = early + late
    first_terms = call(
        "first_terms",
        functools.partial(first_terms_kernel, order),
        shape((pair_n * row_n, width), F32),
        [VMEM] * 4,
        [],
        table, cross_out_both, sides[0], sides[chip_hop],
    )
    return call(
        "pair_output",
        functools.partial(out_kernel, order),
        shape((image_n, slot_n, row_n, width), BF16),
        [VMEM] * 6,
        [pltpu.VMEM((image_n, slot_n, row_n, width), BF16), dma((image_n,))],
        own_rows, table, cross_out_core, first_terms, sides[chip_hop ^ core_hop], sides[core_hop],
        out_specs=HBM,
    )


def solution(mesh):
    return jax.shard_map(
        functools.partial(local, mesh.shape["owner"], mesh.shape["helper"]),
        mesh=mesh,
        in_specs=(
            P("owner", None, None),
            P("owner", None),
            P(None, None, "helper"),
            P("helper", None),
            P(None, None, "helper"),
            P("helper", None),
            P(),
        ),
        out_specs=P("owner", None, "helper", None),
        check_vma=False,
    )
```

```python
import functools

import jax
import jax.numpy as jnp
from jax import lax
from jax.experimental import pallas as pl
from jax.experimental.pallas import tpu as pltpu
from jax.sharding import PartitionSpec as P

HEAD = 64
LANES = 128
F32 = jnp.float32
BF16 = jnp.bfloat16
VMEM_BYTES = 24 * 1024 * 1024
EARLY_WEIGHT = 3 * 10**9
LATE_WEIGHT = 10**11

VMEM = pl.BlockSpec(memory_space=pltpu.VMEM)
HBM = pl.BlockSpec(memory_space=pltpu.HBM)
ANY = pl.BlockSpec(memory_space=pl.ANY)


def owner_swaps(slot_count, owner_count):
    near = (slot_count - 1) // 2
    swaps = [(owner_count // 2, 0)]
    for k in range(near, 1, -1):
        swaps += [(k, 1), (k, 0)]
    return swaps + [(1, 0), (1, 1)]


def swap_target(owner, swap, owner_count):
    distance, colour = swap
    step = distance & -distance
    if isinstance(owner, int):
        up = (owner // step) % 2 == colour
        return (owner + (distance if up else owner_count - distance)) % owner_count
    up = jnp.bitwise_and(lax.shift_right_logical(owner, step.bit_length() - 1), 1) == colour
    return lax.rem(owner + jnp.where(up, distance, owner_count - distance), owner_count)


def nn(left, right):
    return lax.dot_general(left, right, (((1,), (0,)), ((), ())), preferred_element_type=F32)


def nt(left, right):
    return lax.dot_general(left, right, (((1,), (1,)), ((), ())), preferred_element_type=F32)


def norm_core(values):
    row_mean = jnp.mean(values, -1, keepdims=True)
    centred = values - row_mean
    row_var = jnp.mean(centred * centred, -1, keepdims=True)
    return centred * lax.rsqrt(row_var + 1e-05)


def head_stack(queries):
    head_of = lax.broadcasted_iota(jnp.int32, queries.shape, 1) // HEAD
    zero = jnp.zeros((), queries.dtype)
    return jnp.concatenate(
        [jnp.where(head_of == h, queries, zero) for h in range(queries.shape[1] // HEAD)], 0
    ).astype(BF16)


def attend(stacked, keys_t, values_t):
    column_n = keys_t.shape[0]
    head_n = column_n // HEAD
    row_n = stacked.shape[0] // head_n
    scores = nn(stacked, keys_t)
    powers = jnp.exp(scores - jnp.max(scores, -1, keepdims=True))
    weights = (powers * (1.0 / jnp.sum(powers, -1, keepdims=True))).astype(BF16)
    spread = nt(weights, values_t)
    head_of = lax.broadcasted_iota(jnp.int32, (row_n, column_n), 1) // HEAD
    context = spread[(head_n - 1) * row_n :]
    for h in range(head_n - 1):
        context = jnp.where(head_of == h, spread[h * row_n : (h + 1) * row_n], context)
    return context


def pack(block):
    row_n = block.shape[0]
    tail = block[:, LANES:]
    return jnp.concatenate(
        [block[:, :LANES], jnp.concatenate([tail[: row_n // 2], tail[row_n // 2 :]], 1)], 0
    ).astype(BF16)


def pair_place(partners, owner, image_n):
    low = owner * image_n
    found_image, found_slot = jnp.int32(0), jnp.int32(0)
    for image in range(image_n):
        for slot in range(partners.shape[1]):
            gap = partners[image, slot] - low
            hit = jnp.logical_and(gap >= 0, gap < image_n)
            found_image = jnp.where(hit, jnp.int32(image), found_image)
            found_slot = jnp.where(hit, jnp.int32(slot), found_slot)
    return found_image, found_slot


def live_count(partners, image):
    count = jnp.int32(0)
    for slot in range(partners.shape[1]):
        count = count + jnp.where(partners[image, slot] >= 0, jnp.int32(1), jnp.int32(0))
    return count


def own_images_kernel(swaps, owner_n, states, gains, self_t, cross_t, partners, weight, *rest):
    outs, rest = rest[: len(swaps)], rest[len(swaps) :]
    context_out, table, query_weight_out, weight_out, states_v, gains_v, self_v, cross_v, partners_s, held, sems = rest
    image_n, patch_n, width = states.shape
    columns = self_t.shape[1]
    copies = [
        pltpu.make_async_copy(states, states_v, sems.at[0]),
        pltpu.make_async_copy(gains, gains_v, sems.at[1]),
        pltpu.make_async_copy(cross_t.at[pl.ds(1, 2)], cross_v, sems.at[2]),
        pltpu.make_async_copy(partners, partners_s, sems.at[3]),
        pltpu.make_async_copy(self_t, self_v, sems.at[4]),
        pltpu.make_async_copy(cross_t.at[0], query_weight_out, sems.at[5]),
        pltpu.make_async_copy(weight, weight_out, sems.at[6]),
    ]
    for copy in copies:
        copy.start()
    copies[0].wait()
    rows = norm_core(states_v[...].reshape(image_n * patch_n, width).astype(F32))
    for copy in copies[1:5]:
        copy.wait()
    normed = (rows * gains_v[2:3, :]).astype(BF16)
    projected = nt(cross_v[...].reshape(2 * columns, width), normed).astype(BF16)
    for image in range(image_n):
        held[image] = projected[:, image * patch_n : (image + 1) * patch_n]
    normed = (rows * gains_v[0:1, :]).astype(BF16)
    queries = nt(normed, self_v[0]).astype(BF16).astype(F32) * HEAD ** (-0.5)
    key_value = nt(self_v[1:3].reshape(2 * columns, width), normed).astype(BF16)
    contexts = []
    for image in range(image_n):
        span = slice(image * patch_n, (image + 1) * patch_n)
        contexts.append(
            attend(head_stack(queries[span]), key_value[:columns, span], key_value[columns:, span])
        )
    me = lax.axis_index("owner")
    pair_n = len(swaps)
    for at, (out, swap) in enumerate(zip(outs, swaps)):
        image, slot = pair_place(partners_s, swap_target(me, swap, owner_n), image_n)
        out[...] = held[image]
        position = jnp.where(image == 0, slot, pair_n - 1 - slot)
        table[at : at + 1, :] = jnp.full((1, LANES), image, jnp.int32)
        table[pair_n + at : pair_n + at + 1, :] = jnp.full((1, LANES), position, jnp.int32)
    table[2 * pair_n :, :] = jnp.full((1, LANES), live_count(partners_s, 0), jnp.int32)
    context_out[...] = pack(jnp.concatenate(contexts, 0))
    copies[5].wait()
    copies[6].wait()


def unpack(block):
    row_n = block.shape[0] * 2 // 3
    tail = block[row_n:, :]
    return jnp.concatenate(
        [block[:row_n, :], jnp.concatenate([tail[:, :HEAD], tail[:, HEAD:]], 0)], 1
    )


def partial_kernel(states, own, got, own_weight, got_weight, base, sent):
    rows = jnp.concatenate([unpack(own[...]), unpack(got[...])], 1)
    part = nn(rows, jnp.concatenate([own_weight[...], got_weight[...]], 0))
    sent[...] = part.astype(BF16)
    base[...] = states[...].reshape(part.shape).astype(F32) + part


def query_kernel(helper_n, base, got, gains, weight, own_rows, queries_out, mixed_ref):
    mixed = base[...] + got[...].astype(F32)
    image_n, row_n, width = own_rows.shape
    patch_n = row_n * helper_n
    mixed_ref[...] = mixed.reshape(image_n, patch_n, width)
    normed = (norm_core(mixed) * gains[1:2, :]).astype(BF16)
    queries = nt(normed, weight[...]).astype(BF16).astype(F32) * HEAD ** (-0.5)
    queries_out[...] = queries.reshape(queries_out.shape).astype(BF16)
    start = pl.multiple_of(lax.axis_index("helper") * row_n, row_n)
    own_rows[...] = mixed_ref[:, pl.ds(start, row_n), :]


def hand_on_kernel(value, *rest):
    out = rest[-1]
    out[...] = value[...]


def both_kernel(own, got, waited, out, sems):
    del waited
    row_n = own.shape[0]
    copies = [
        pltpu.make_async_copy(own, out.at[pl.ds(0, row_n)], sems.at[0]),
        pltpu.make_async_copy(got, out.at[pl.ds(row_n, row_n)], sems.at[1]),
    ]
    for copy in copies:
        copy.start()
    for copy in copies:
        copy.wait()


def cross_pairs(places, helper_n, queries, table, arrived, put):
    for at, (place, block) in enumerate(zip(places, arrived)):
        chosen = queries[0].astype(F32)
        for image in range(1, queries.shape[0]):
            chosen = jnp.where(table[place : place + 1, 0:1] == image, queries[image].astype(F32), chosen)
        columns = block.shape[0] // 2
        context = attend(head_stack(chosen), block[:columns, :], block[columns:, :])
        row_n = context.shape[0] // helper_n
        for helper in range(helper_n):
            put(at, helper, pack(context[helper * row_n : (helper + 1) * row_n]))


def cross_kernel(places, helper_n, queries, table, *rest):
    *arrived, out = rest

    def put(at, helper, rows):
        out[helper, at] = rows

    cross_pairs(places, helper_n, queries, table, arrived, put)


def last_cross_kernel(places, helper_n, queries, table, before, *rest):
    arrived, (*outs, held) = rest[: len(places)], rest[len(places) :]
    first = before.shape[1]
    helper = lax.axis_index("helper")
    for k, out in enumerate(outs):
        out[:first] = before[jnp.bitwise_xor(helper, k)]

    def put(at, helper, rows):
        held[helper, at] = rows

    cross_pairs(places, helper_n, queries, table, arrived, put)
    for k, out in enumerate(outs):
        out[first:] = held[jnp.bitwise_xor(helper, k)]


def side_rows(block):
    row_n = block.shape[1] * 2 // 3
    main, tail = block[:, :row_n, :], block[:, row_n:, :]
    tail = jnp.concatenate([tail[:, :, :HEAD], tail[:, :, HEAD:]], 1)
    return jnp.concatenate([main.reshape(-1, LANES), tail.reshape(-1, HEAD)], 1)


def placed_rows(sides, order, table):
    pair_n = len(order)
    rows = []
    for side in sides:
        pairs = [side[at].astype(F32) for at in range(pair_n)]
        placed = []
        for position in range(pair_n):
            block = pairs[0]
            for at in range(1, pair_n):
                row = pair_n + order[at]
                block = jnp.where(table[row : row + 1, 0:1] == position, pairs[at], block)
            placed.append(block.astype(BF16)[None])
        rows.append(side_rows(jnp.concatenate(placed, 0)))
    return jnp.concatenate(rows, 1)


def first_terms_kernel(order, table, weights, own, across_chip, terms):
    terms[...] = nn(placed_rows((own, across_chip), order, table), weights[...])


def out_kernel(order, own_rows, table, weights, first, across_both, across_core, out, out_v, sems):
    row_n, width = own_rows.shape[1:]
    pair_n = len(order)
    terms = first[...] + nn(placed_rows((across_core, across_both), order, table), weights[...])
    first_n = table[2 * pair_n :, 0:1]
    zero = jnp.zeros((row_n, width), F32)
    copies = []
    for position in range(pair_n):
        term = terms[position * row_n : (position + 1) * row_n]
        is_first = first_n > position
        out_v[0, position] = jnp.where(is_first, own_rows[0] + term, zero).astype(BF16)
        out_v[1, pair_n - 1 - position] = jnp.where(is_first, zero, own_rows[1] + term).astype(BF16)
        for image, slot in ((0, position), (1, pair_n - 1 - position)):
            copies.append(
                pltpu.make_async_copy(out_v.at[image, slot], out.at[image, slot], sems.at[image, slot])
            )
            copies[-1].start()
    for copy in copies:
        copy.wait()


def local(owner_n, helper_n, states, partners, self_proj, self_out, cross_proj, cross_out, gains):
    image_n, patch_n, width = states.shape
    slot_n = partners.shape[1]
    columns = self_proj.shape[2]
    row_n = patch_n // helper_n
    row_all = image_n * patch_n
    swaps = owner_swaps(slot_n, owner_n)
    pair_n = len(swaps)
    self_proj_t = jnp.swapaxes(self_proj, 1, 2)
    cross_proj_t = jnp.swapaxes(cross_proj, 1, 2)
    chip_hop, core_hop = helper_n // 2, 1

    def across(value, k):
        return lax.ppermute(value, "helper", [(j, j ^ k) for j in range(helper_n)])

    def exchange(value, swap):
        return lax.ppermute(value, "owner", [(o, swap_target(o, swap, owner_n)) for o in range(owner_n)])

    def call(name, kernel, out_shape, in_specs, scratch, *operands, out_specs=None, flops=1):
        with jax.named_scope(name):
            return pl.pallas_call(
                kernel,
                out_shape=out_shape,
                in_specs=in_specs,
                out_specs=out_specs or jax.tree.map(lambda _: VMEM, out_shape),
                scratch_shapes=scratch,
                compiler_params=pltpu.CompilerParams(vmem_limit_bytes=VMEM_BYTES),
                cost_estimate=pl.CostEstimate(flops=flops, bytes_accessed=1, transcendentals=0),
            )(*operands)

    shape = jax.ShapeDtypeStruct
    dma = pltpu.SemaphoreType.DMA
    index_table = pltpu.SMEM(partners.shape, jnp.int32)
    block = shape((2 * columns, patch_n), BF16)

    partners_h = pltpu.with_memory_space_constraint(partners, pltpu.HBM)
    self_out_got = across(self_out, chip_hop)
    *outgoing, context, table, query_weight, cross_out_own = call(
        "own_images",
        functools.partial(own_images_kernel, swaps, owner_n),
        [block] * pair_n
        + [
            shape((row_all * columns // LANES, LANES), BF16),
            shape((2 * pair_n + 1, LANES), jnp.int32),
            shape((columns, width), BF16),
            shape(cross_out.shape, BF16),
        ],
        [HBM] * 6,
        [
            pltpu.VMEM(states.shape, BF16),
            pltpu.VMEM(gains.shape, F32),
            pltpu.VMEM((3, columns, width), BF16),
            pltpu.VMEM((2, columns, width), BF16),
            index_table,
            pltpu.VMEM((image_n, 2 * columns, patch_n), BF16),
            dma((7,)),
        ],
        *[pltpu.with_memory_space_constraint(x, pltpu.HBM) for x in (states, gains, self_proj_t, cross_proj_t)],
        partners_h,
        pltpu.with_memory_space_constraint(cross_out, pltpu.HBM),
    )
    arrived = [exchange(value, swap) for value, swap in zip(outgoing, swaps)]
    context_got = across(context, chip_hop)
    near = (slot_n - 1) // 2
    early = [2 * near - 2, 2 * near - 1]
    late = [at for at in range(pair_n) if at not in early]
    short = early
    cross_out_sent = call(
        "cross_output_rows",
        hand_on_kernel,
        shape(cross_out.shape, BF16),
        [VMEM] + [ANY] * len([arrived[short[0]]]),
        [],
        cross_out_own, *[arrived[short[0]]],
    )
    cross_out_got = across(cross_out_sent, chip_hop)
    before = [arrived[at] for at in short] + [self_out_got]
    gains_then = call(
        "gains",
        hand_on_kernel,
        shape(gains.shape, F32),
        [VMEM] + [ANY] * len(before),
        [],
        gains, *before,
    )

    made_shapes = [
        shape((image_n, row_n, width), F32),
        shape((image_n, patch_n, columns), BF16),
    ]

    def mixing(states, gains, query_weight, context, context_got, self_out, self_out_got):
        base, sent = call(
            "self_output_share",
            partial_kernel,
            [shape((row_all, width), F32), shape((row_all, width), BF16)],
            [VMEM] * 5,
            [],
            states, context, context_got, self_out, self_out_got,
        )
        made = call(
            "mixed_and_queries",
            functools.partial(query_kernel, helper_n),
            made_shapes,
            [VMEM] * 4,
            [pltpu.VMEM((image_n, patch_n, width), F32)],
            base, across(sent, core_hop), gains, query_weight,
        )
        return tuple(made)

    def no_images(*operands):
        return tuple(jnp.zeros(made.shape, made.dtype) for made in made_shapes)

    own_rows, queries = lax.cond(
        lax.axis_index("owner") < owner_n, mixing, no_images,
        states, gains_then, query_weight, context, context_got, self_out, self_out_got,
    )
    packed = columns * row_n // LANES
    early_sides = call(
        "early_cross_attention",
        functools.partial(cross_kernel, early, helper_n),
        shape((helper_n, len(early), packed, LANES), BF16),
        [VMEM] * (2 + len(early)),
        [],
        queries, table, *[arrived[at] for at in early],
    )
    arrived[0] = call(
        "half_way",
        hand_on_kernel,
        block,
        [VMEM, ANY],
        [],
        arrived[0], early_sides,
        flops=EARLY_WEIGHT,
    )
    sides = call(
        "late_cross_attention",
        functools.partial(last_cross_kernel, late, helper_n),
        [shape((pair_n, packed, LANES), BF16)] * helper_n,
        [VMEM] * (3 + len(late)),
        [pltpu.VMEM((helper_n, len(late), packed, LANES), BF16)],
        queries, table, early_sides, *[arrived[at] for at in late],
        flops=LATE_WEIGHT,
    )
    sides = [sides[0]] + [across(sides[k], k) for k in range(1, helper_n)]
    cross_out_both = call(
        "cross_output_both_rows",
        both_kernel,
        shape((2 * columns, width), BF16),
        [VMEM, ANY, ANY],
        [dma((2,))],
        cross_out, cross_out_got, early_sides,
    )
    cross_out_core = across(cross_out_both, core_hop)
    order = early + late
    first_terms = call(
        "first_terms",
        functools.partial(first_terms_kernel, order),
        shape((pair_n * row_n, width), F32),
        [VMEM] * 4,
        [],
        table, cross_out_both, sides[0], sides[chip_hop],
    )
    return call(
        "pair_output",
        functools.partial(out_kernel, order),
        shape((image_n, slot_n, row_n, width), BF16),
        [VMEM] * 6,
        [pltpu.VMEM((image_n, slot_n, row_n, width), BF16), dma((image_n, slot_n))],
        own_rows, table, cross_out_core, first_terms, sides[chip_hop ^ core_hop], sides[core_hop],
        out_specs=HBM,
    )


def solution(mesh):
    return jax.shard_map(
        functools.partial(local, mesh.shape["owner"], mesh.shape["helper"]),
        mesh=mesh,
        in_specs=(
            P("owner", None, None),
            P("owner", None),
            P(None, None, "helper"),
            P("helper", None),
            P(None, None, "helper"),
            P("helper", None),
            P(),
        ),
        out_specs=P("owner", None, "helper", None),
        check_vma=False,
    )
```

```python
import functools

import jax
import jax.numpy as jnp
from jax import lax
from jax.experimental import pallas as pl
from jax.experimental.pallas import tpu as pltpu
from jax.sharding import PartitionSpec as P

HEAD = 64
LANES = 128
F32 = jnp.float32
BF16 = jnp.bfloat16
VMEM_BYTES = 24 * 1024 * 1024
EARLY_WEIGHT = 3 * 10**9
LATE_WEIGHT = 10**11

VMEM = pl.BlockSpec(memory_space=pltpu.VMEM)
HBM = pl.BlockSpec(memory_space=pltpu.HBM)
ANY = pl.BlockSpec(memory_space=pl.ANY)


def owner_swaps(slot_count, owner_count):
    near = (slot_count - 1) // 2
    swaps = [(owner_count // 2, 0)]
    for k in range(near, 1, -1):
        swaps += [(k, 1), (k, 0)]
    return swaps + [(1, 0), (1, 1)]


def swap_target(owner, swap, owner_count):
    distance, colour = swap
    step = distance & -distance
    if isinstance(owner, int):
        up = (owner // step) % 2 == colour
        return (owner + (distance if up else owner_count - distance)) % owner_count
    up = jnp.bitwise_and(lax.shift_right_logical(owner, step.bit_length() - 1), 1) == colour
    return lax.rem(owner + jnp.where(up, distance, owner_count - distance), owner_count)


def nn(left, right):
    return lax.dot_general(left, right, (((1,), (0,)), ((), ())), preferred_element_type=F32)


def nt(left, right):
    return lax.dot_general(left, right, (((1,), (1,)), ((), ())), preferred_element_type=F32)


def norm_core(values):
    row_mean = jnp.mean(values, -1, keepdims=True)
    centred = values - row_mean
    row_var = jnp.mean(centred * centred, -1, keepdims=True)
    return centred * lax.rsqrt(row_var + 1e-05)


def head_stack(queries):
    head_of = lax.broadcasted_iota(jnp.int32, queries.shape, 1) // HEAD
    zero = jnp.zeros((), queries.dtype)
    return jnp.concatenate(
        [jnp.where(head_of == h, queries, zero) for h in range(queries.shape[1] // HEAD)], 0
    ).astype(BF16)


def attend(stacked, keys_t, values_t):
    column_n = keys_t.shape[0]
    head_n = column_n // HEAD
    row_n = stacked.shape[0] // head_n
    scores = nn(stacked, keys_t)
    powers = jnp.exp(scores - jnp.max(scores, -1, keepdims=True))
    weights = (powers * (1.0 / jnp.sum(powers, -1, keepdims=True))).astype(BF16)
    spread = nt(weights, values_t)
    head_of = lax.broadcasted_iota(jnp.int32, (row_n, column_n), 1) // HEAD
    context = spread[(head_n - 1) * row_n :]
    for h in range(head_n - 1):
        context = jnp.where(head_of == h, spread[h * row_n : (h + 1) * row_n], context)
    return context


def pack(block):
    row_n = block.shape[0]
    tail = block[:, LANES:]
    return jnp.concatenate(
        [block[:, :LANES], jnp.concatenate([tail[: row_n // 2], tail[row_n // 2 :]], 1)], 0
    ).astype(BF16)


def pair_place(partners, owner, image_n):
    low = owner * image_n
    found_image, found_slot = jnp.int32(0), jnp.int32(0)
    for image in range(image_n):
        for slot in range(partners.shape[1]):
            gap = partners[image, slot] - low
            hit = jnp.logical_and(gap >= 0, gap < image_n)
            found_image = jnp.where(hit, jnp.int32(image), found_image)
            found_slot = jnp.where(hit, jnp.int32(slot), found_slot)
    return found_image, found_slot


def live_count(partners, image):
    count = jnp.int32(0)
    for slot in range(partners.shape[1]):
        count = count + jnp.where(partners[image, slot] >= 0, jnp.int32(1), jnp.int32(0))
    return count


def own_images_kernel(swaps, owner_n, states, gains, self_t, cross_t, partners, weight, *rest):
    outs, rest = rest[: len(swaps)], rest[len(swaps) :]
    context_out, table, query_weight_out, weight_out, states_v, gains_v, self_v, cross_v, partners_s, held, sems = rest
    image_n, patch_n, width = states.shape
    columns = self_t.shape[1]
    copies = [
        pltpu.make_async_copy(states, states_v, sems.at[0]),
        pltpu.make_async_copy(gains, gains_v, sems.at[1]),
        pltpu.make_async_copy(cross_t.at[pl.ds(1, 2)], cross_v, sems.at[2]),
        pltpu.make_async_copy(partners, partners_s, sems.at[3]),
        pltpu.make_async_copy(self_t, self_v, sems.at[4]),
        pltpu.make_async_copy(cross_t.at[0], query_weight_out, sems.at[5]),
        pltpu.make_async_copy(weight, weight_out, sems.at[6]),
    ]
    for copy in copies:
        copy.start()
    copies[0].wait()
    rows = norm_core(states_v[...].reshape(image_n * patch_n, width).astype(F32))
    for copy in copies[1:5]:
        copy.wait()
    normed = (rows * gains_v[2:3, :]).astype(BF16)
    projected = nt(cross_v[...].reshape(2 * columns, width), normed).astype(BF16)
    for image in range(image_n):
        held[image] = projected[:, image * patch_n : (image + 1) * patch_n]
    normed = (rows * gains_v[0:1, :]).astype(BF16)
    queries = nt(normed, self_v[0]).astype(BF16).astype(F32) * HEAD ** (-0.5)
    key_value = nt(self_v[1:3].reshape(2 * columns, width), normed).astype(BF16)
    contexts = []
    for image in range(image_n):
        span = slice(image * patch_n, (image + 1) * patch_n)
        contexts.append(
            attend(head_stack(queries[span]), key_value[:columns, span], key_value[columns:, span])
        )
    me = lax.axis_index("owner")
    pair_n = len(swaps)
    for at, (out, swap) in enumerate(zip(outs, swaps)):
        image, slot = pair_place(partners_s, swap_target(me, swap, owner_n), image_n)
        out[...] = held[image]
        position = jnp.where(image == 0, slot, pair_n - 1 - slot)
        table[at : at + 1, :] = jnp.full((1, LANES), image, jnp.int32)
        table[pair_n + at : pair_n + at + 1, :] = jnp.full((1, LANES), position, jnp.int32)
    table[2 * pair_n :, :] = jnp.full((1, LANES), live_count(partners_s, 0), jnp.int32)
    context_out[...] = pack(jnp.concatenate(contexts, 0))
    copies[5].wait()
    copies[6].wait()


def unpack(block):
    row_n = block.shape[0] * 2 // 3
    tail = block[row_n:, :]
    return jnp.concatenate(
        [block[:row_n, :], jnp.concatenate([tail[:, :HEAD], tail[:, HEAD:]], 0)], 1
    )


def partial_kernel(states, own, got, own_weight, got_weight, base, sent):
    rows = jnp.concatenate([unpack(own[...]), unpack(got[...])], 1)
    part = nn(rows, jnp.concatenate([own_weight[...], got_weight[...]], 0))
    sent[...] = part.astype(BF16)
    base[...] = states[...].reshape(part.shape).astype(F32) + part


def query_kernel(helper_n, base, got, gains, weight, own_rows, queries_out, mixed_ref):
    mixed = base[...] + got[...].astype(F32)
    image_n, row_n, width = own_rows.shape
    patch_n = row_n * helper_n
    mixed_ref[...] = mixed.reshape(image_n, patch_n, width)
    normed = (norm_core(mixed) * gains[1:2, :]).astype(BF16)
    queries = nt(normed, weight[...]).astype(BF16).astype(F32) * HEAD ** (-0.5)
    queries_out[...] = queries.reshape(queries_out.shape).astype(BF16)
    start = pl.multiple_of(lax.axis_index("helper") * row_n, row_n)
    own_rows[...] = mixed_ref[:, pl.ds(start, row_n), :]


def hand_on_kernel(value, *rest):
    out = rest[-1]
    out[...] = value[...]


def both_kernel(own, got, waited, out, sems):
    del waited
    row_n = own.shape[0]
    copies = [
        pltpu.make_async_copy(own, out.at[pl.ds(0, row_n)], sems.at[0]),
        pltpu.make_async_copy(got, out.at[pl.ds(row_n, row_n)], sems.at[1]),
    ]
    for copy in copies:
        copy.start()
    for copy in copies:
        copy.wait()


def cross_pairs(places, helper_n, queries, table, arrived, put):
    for at, (place, block) in enumerate(zip(places, arrived)):
        chosen = queries[0].astype(F32)
        for image in range(1, queries.shape[0]):
            chosen = jnp.where(table[place : place + 1, 0:1] == image, queries[image].astype(F32), chosen)
        columns = block.shape[0] // 2
        context = attend(head_stack(chosen), block[:columns, :], block[columns:, :])
        row_n = context.shape[0] // helper_n
        for helper in range(helper_n):
            put(at, helper, pack(context[helper * row_n : (helper + 1) * row_n]))


def cross_kernel(places, helper_n, queries, table, *rest):
    *arrived, out = rest

    def put(at, helper, rows):
        out[helper, at] = rows

    cross_pairs(places, helper_n, queries, table, arrived, put)


def last_cross_kernel(places, helper_n, queries, table, before, *rest):
    arrived, (*outs, held) = rest[: len(places)], rest[len(places) :]
    first = before.shape[1]
    helper = lax.axis_index("helper")
    for k, out in enumerate(outs):
        out[:first] = before[jnp.bitwise_xor(helper, k)]

    def put(at, helper, rows):
        held[helper, at] = rows

    cross_pairs(places, helper_n, queries, table, arrived, put)
    for k, out in enumerate(outs):
        out[first:] = held[jnp.bitwise_xor(helper, k)]


def side_rows(block):
    row_n = block.shape[1] * 2 // 3
    main, tail = block[:, :row_n, :], block[:, row_n:, :]
    tail = jnp.concatenate([tail[:, :, :HEAD], tail[:, :, HEAD:]], 1)
    return jnp.concatenate([main.reshape(-1, LANES), tail.reshape(-1, HEAD)], 1)


def placed_rows(sides, order, table):
    pair_n = len(order)
    rows = []
    for side in sides:
        pairs = [side[at].astype(F32) for at in range(pair_n)]
        placed = []
        for position in range(pair_n):
            block = pairs[0]
            for at in range(1, pair_n):
                row = pair_n + order[at]
                block = jnp.where(table[row : row + 1, 0:1] == position, pairs[at], block)
            placed.append(block.astype(BF16)[None])
        rows.append(side_rows(jnp.concatenate(placed, 0)))
    return jnp.concatenate(rows, 1)


def first_terms_kernel(order, table, weights, own, across_chip, terms):
    terms[...] = nn(placed_rows((own, across_chip), order, table), weights[...])


def out_kernel(order, own_rows, table, weights, first, across_both, across_core, out, out_v, sems):
    row_n, width = own_rows.shape[1:]
    pair_n = len(order)
    terms = first[...] + nn(placed_rows((across_core, across_both), order, table), weights[...])
    first_n = table[2 * pair_n :, 0:1]
    zero = jnp.zeros((row_n, width), F32)
    copies = []
    for position in range(pair_n):
        term = terms[position * row_n : (position + 1) * row_n]
        is_first = first_n > position
        out_v[0, position] = jnp.where(is_first, own_rows[0] + term, zero).astype(BF16)
        out_v[1, pair_n - 1 - position] = jnp.where(is_first, zero, own_rows[1] + term).astype(BF16)
        for image, slot in ((0, position), (1, pair_n - 1 - position)):
            copies.append(
                pltpu.make_async_copy(out_v.at[image, slot], out.at[image, slot], sems.at[image, slot])
            )
            copies[-1].start()
    for copy in copies:
        copy.wait()


def local(owner_n, helper_n, states, partners, self_proj, self_out, cross_proj, cross_out, gains):
    image_n, patch_n, width = states.shape
    slot_n = partners.shape[1]
    columns = self_proj.shape[2]
    row_n = patch_n // helper_n
    row_all = image_n * patch_n
    swaps = owner_swaps(slot_n, owner_n)
    pair_n = len(swaps)
    self_proj_t = jnp.swapaxes(self_proj, 1, 2)
    cross_proj_t = jnp.swapaxes(cross_proj, 1, 2)
    chip_hop, core_hop = helper_n // 2, 1

    def across(value, k):
        return lax.ppermute(value, "helper", [(j, j ^ k) for j in range(helper_n)])

    def exchange(value, swap):
        return lax.ppermute(value, "owner", [(o, swap_target(o, swap, owner_n)) for o in range(owner_n)])

    def call(name, kernel, out_shape, in_specs, scratch, *operands, out_specs=None, flops=1):
        with jax.named_scope(name):
            return pl.pallas_call(
                kernel,
                out_shape=out_shape,
                in_specs=in_specs,
                out_specs=out_specs or jax.tree.map(lambda _: VMEM, out_shape),
                scratch_shapes=scratch,
                compiler_params=pltpu.CompilerParams(vmem_limit_bytes=VMEM_BYTES),
                cost_estimate=pl.CostEstimate(flops=flops, bytes_accessed=1, transcendentals=0),
            )(*operands)

    shape = jax.ShapeDtypeStruct
    dma = pltpu.SemaphoreType.DMA
    index_table = pltpu.SMEM(partners.shape, jnp.int32)
    block = shape((2 * columns, patch_n), BF16)

    partners_h = pltpu.with_memory_space_constraint(partners, pltpu.HBM)
    self_out_got = across(self_out, chip_hop)
    *outgoing, context, table, query_weight, cross_out_own = call(
        "own_images",
        functools.partial(own_images_kernel, swaps, owner_n),
        [block] * pair_n
        + [
            shape((row_all * columns // LANES, LANES), BF16),
            shape((2 * pair_n + 1, LANES), jnp.int32),
            shape((columns, width), BF16),
            shape(cross_out.shape, BF16),
        ],
        [HBM] * 6,
        [
            pltpu.VMEM(states.shape, BF16),
            pltpu.VMEM(gains.shape, F32),
            pltpu.VMEM((3, columns, width), BF16),
            pltpu.VMEM((2, columns, width), BF16),
            index_table,
            pltpu.VMEM((image_n, 2 * columns, patch_n), BF16),
            dma((7,)),
        ],
        *[pltpu.with_memory_space_constraint(x, pltpu.HBM) for x in (states, gains, self_proj_t, cross_proj_t)],
        partners_h,
        pltpu.with_memory_space_constraint(cross_out, pltpu.HBM),
    )
    arrived = [exchange(value, swap) for value, swap in zip(outgoing, swaps)]
    context_got = across(context, chip_hop)
    near = (slot_n - 1) // 2
    early = [2 * near - 2, 2 * near - 1]
    late = [at for at in range(pair_n) if at not in early]
    short = early
    cross_out_sent = call(
        "cross_output_rows",
        hand_on_kernel,
        shape(cross_out.shape, BF16),
        [VMEM] + [ANY] * len([arrived[short[0]]]),
        [],
        cross_out_own, *[arrived[short[0]]],
    )
    cross_out_got = across(cross_out_sent, chip_hop)
    before = [arrived[at] for at in short] + [self_out_got]
    gains_then = call(
        "gains",
        hand_on_kernel,
        shape(gains.shape, F32),
        [VMEM] + [ANY] * len(before),
        [],
        gains, *before,
    )

    made_shapes = [
        shape((image_n, row_n, width), F32),
        shape((image_n, patch_n, columns), BF16),
    ]

    def mixing(states, gains, query_weight, context, context_got, self_out, self_out_got):
        base, sent = call(
            "self_output_share",
            partial_kernel,
            [shape((row_all, width), F32), shape((row_all, width), BF16)],
            [VMEM] * 5,
            [],
            states, context, context_got, self_out, self_out_got,
        )
        made = call(
            "mixed_and_queries",
            functools.partial(query_kernel, helper_n),
            made_shapes,
            [VMEM] * 4,
            [pltpu.VMEM((image_n, patch_n, width), F32)],
            base, across(sent, core_hop), gains, query_weight,
        )
        return tuple(made)

    def no_images(*operands):
        return tuple(jnp.zeros(made.shape, made.dtype) for made in made_shapes)

    own_rows, queries = lax.cond(
        lax.axis_index("owner") < owner_n, mixing, no_images,
        states, gains_then, query_weight, context, context_got, self_out, self_out_got,
    )
    packed = columns * row_n // LANES
    early_sides = call(
        "early_cross_attention",
        functools.partial(cross_kernel, early, helper_n),
        shape((helper_n, len(early), packed, LANES), BF16),
        [VMEM] * (2 + len(early)),
        [],
        queries, table, *[arrived[at] for at in early],
    )
    arrived[0] = call(
        "half_way",
        hand_on_kernel,
        block,
        [VMEM, ANY],
        [],
        arrived[0], early_sides,
        flops=EARLY_WEIGHT,
    )
    sides = call(
        "late_cross_attention",
        functools.partial(last_cross_kernel, late, helper_n),
        [shape((pair_n, packed, LANES), BF16)] * helper_n,
        [VMEM] * (3 + len(late)),
        [pltpu.VMEM((helper_n, len(late), packed, LANES), BF16)],
        queries, table, early_sides, *[arrived[at] for at in late],
        flops=LATE_WEIGHT,
    )
    sides = [sides[0]] + [across(sides[k], k) for k in range(1, helper_n)]
    cross_out_both = call(
        "cross_output_both_rows",
        both_kernel,
        shape((2 * columns, width), BF16),
        [VMEM, ANY, ANY],
        [dma((2,))],
        cross_out_sent, cross_out_got, early_sides,
    )
    cross_out_core = across(cross_out_both, core_hop)
    order = early + late
    first_terms = call(
        "first_terms",
        functools.partial(first_terms_kernel, order),
        shape((pair_n * row_n, width), F32),
        [VMEM] * 4,
        [],
        table, cross_out_both, sides[0], sides[chip_hop],
    )
    return call(
        "pair_output",
        functools.partial(out_kernel, order),
        shape((image_n, slot_n, row_n, width), BF16),
        [VMEM] * 6,
        [pltpu.VMEM((image_n, slot_n, row_n, width), BF16), dma((image_n, slot_n))],
        own_rows, table, cross_out_core, first_terms, sides[chip_hop ^ core_hop], sides[core_hop],
        out_specs=HBM,
    )


def solution(mesh):
    return jax.shard_map(
        functools.partial(local, mesh.shape["owner"], mesh.shape["helper"]),
        mesh=mesh,
        in_specs=(
            P("owner", None, None),
            P("owner", None),
            P(None, None, "helper"),
            P("helper", None),
            P(None, None, "helper"),
            P("helper", None),
            P(),
        ),
        out_specs=P("owner", None, "helper", None),
        check_vma=False,
    )
```

```python
import functools

import jax
import jax.numpy as jnp
from jax import lax
from jax.experimental import pallas as pl
from jax.experimental.pallas import tpu as pltpu
from jax.sharding import PartitionSpec as P

HEAD = 64
LANES = 128
F32 = jnp.float32
BF16 = jnp.bfloat16
VMEM_BYTES = 24 * 1024 * 1024
EARLY_WEIGHT = 3 * 10**9
LATE_WEIGHT = 10**11

VMEM = pl.BlockSpec(memory_space=pltpu.VMEM)
HBM = pl.BlockSpec(memory_space=pltpu.HBM)
ANY = pl.BlockSpec(memory_space=pl.ANY)


def owner_swaps(slot_count, owner_count):
    near = (slot_count - 1) // 2
    swaps = [(owner_count // 2, 0)]
    for k in range(near, 1, -1):
        swaps += [(k, 1), (k, 0)]
    return swaps + [(1, 0), (1, 1)]


def swap_target(owner, swap, owner_count):
    distance, colour = swap
    step = distance & -distance
    if isinstance(owner, int):
        up = (owner // step) % 2 == colour
        return (owner + (distance if up else owner_count - distance)) % owner_count
    up = jnp.bitwise_and(lax.shift_right_logical(owner, step.bit_length() - 1), 1) == colour
    return lax.rem(owner + jnp.where(up, distance, owner_count - distance), owner_count)


def nn(left, right):
    return lax.dot_general(left, right, (((1,), (0,)), ((), ())), preferred_element_type=F32)


def nt(left, right):
    return lax.dot_general(left, right, (((1,), (1,)), ((), ())), preferred_element_type=F32)


def norm_core(values):
    row_mean = jnp.mean(values, -1, keepdims=True)
    centred = values - row_mean
    row_var = jnp.mean(centred * centred, -1, keepdims=True)
    return centred * lax.rsqrt(row_var + 1e-05)


def head_stack(queries):
    head_of = lax.broadcasted_iota(jnp.int32, queries.shape, 1) // HEAD
    zero = jnp.zeros((), queries.dtype)
    return jnp.concatenate(
        [jnp.where(head_of == h, queries, zero) for h in range(queries.shape[1] // HEAD)], 0
    ).astype(BF16)


def attend(stacked, keys_t, values_t):
    column_n = keys_t.shape[0]
    head_n = column_n // HEAD
    row_n = stacked.shape[0] // head_n
    scores = nn(stacked, keys_t)
    powers = jnp.exp(scores - jnp.max(scores, -1, keepdims=True))
    weights = (powers * (1.0 / jnp.sum(powers, -1, keepdims=True))).astype(BF16)
    spread = nt(weights, values_t)
    head_of = lax.broadcasted_iota(jnp.int32, (row_n, column_n), 1) // HEAD
    context = spread[(head_n - 1) * row_n :]
    for h in range(head_n - 1):
        context = jnp.where(head_of == h, spread[h * row_n : (h + 1) * row_n], context)
    return context


def pack(block):
    row_n = block.shape[0]
    tail = block[:, LANES:]
    return jnp.concatenate(
        [block[:, :LANES], jnp.concatenate([tail[: row_n // 2], tail[row_n // 2 :]], 1)], 0
    ).astype(BF16)


def pair_place(partners, owner, image_n):
    low = owner * image_n
    found_image, found_slot = jnp.int32(0), jnp.int32(0)
    for image in range(image_n):
        for slot in range(partners.shape[1]):
            gap = partners[image, slot] - low
            hit = jnp.logical_and(gap >= 0, gap < image_n)
            found_image = jnp.where(hit, jnp.int32(image), found_image)
            found_slot = jnp.where(hit, jnp.int32(slot), found_slot)
    return found_image, found_slot


def live_count(partners, image):
    count = jnp.int32(0)
    for slot in range(partners.shape[1]):
        count = count + jnp.where(partners[image, slot] >= 0, jnp.int32(1), jnp.int32(0))
    return count


def own_images_kernel(swaps, owner_n, states, gains, self_t, cross_t, partners, weight, *rest):
    outs, rest = rest[: len(swaps)], rest[len(swaps) :]
    context_out, table, query_weight_out, weight_out, states_v, gains_v, self_v, cross_v, partners_s, held, sems = rest
    image_n, patch_n, width = states.shape
    columns = self_t.shape[1]
    copies = [
        pltpu.make_async_copy(states, states_v, sems.at[0]),
        pltpu.make_async_copy(gains, gains_v, sems.at[1]),
        pltpu.make_async_copy(cross_t.at[pl.ds(1, 2)], cross_v, sems.at[2]),
        pltpu.make_async_copy(partners, partners_s, sems.at[3]),
        pltpu.make_async_copy(self_t, self_v, sems.at[4]),
        pltpu.make_async_copy(cross_t.at[0], query_weight_out, sems.at[5]),
        pltpu.make_async_copy(weight, weight_out, sems.at[6]),
    ]
    for copy in copies:
        copy.start()
    copies[0].wait()
    rows = norm_core(states_v[...].reshape(image_n * patch_n, width).astype(F32))
    for copy in copies[1:5]:
        copy.wait()
    normed = (rows * gains_v[2:3, :]).astype(BF16)
    projected = nt(cross_v[...].reshape(2 * columns, width), normed).astype(BF16)
    for image in range(image_n):
        held[image] = projected[:, image * patch_n : (image + 1) * patch_n]
    normed = (rows * gains_v[0:1, :]).astype(BF16)
    queries = nt(normed, self_v[0]).astype(BF16).astype(F32) * HEAD ** (-0.5)
    key_value = nt(self_v[1:3].reshape(2 * columns, width), normed).astype(BF16)
    contexts = []
    for image in range(image_n):
        span = slice(image * patch_n, (image + 1) * patch_n)
        contexts.append(
            attend(head_stack(queries[span]), key_value[:columns, span], key_value[columns:, span])
        )
    me = lax.axis_index("owner")
    pair_n = len(swaps)
    for at, (out, swap) in enumerate(zip(outs, swaps)):
        image, slot = pair_place(partners_s, swap_target(me, swap, owner_n), image_n)
        out[...] = held[image]
        position = jnp.where(image == 0, slot, pair_n - 1 - slot)
        table[at : at + 1, :] = jnp.full((1, LANES), image, jnp.int32)
        table[pair_n + at : pair_n + at + 1, :] = jnp.full((1, LANES), position, jnp.int32)
    table[2 * pair_n :, :] = jnp.full((1, LANES), live_count(partners_s, 0), jnp.int32)
    context_out[...] = pack(jnp.concatenate(contexts, 0))
    copies[5].wait()
    copies[6].wait()


def unpack(block):
    row_n = block.shape[0] * 2 // 3
    tail = block[row_n:, :]
    return jnp.concatenate(
        [block[:row_n, :], jnp.concatenate([tail[:, :HEAD], tail[:, HEAD:]], 0)], 1
    )


def partial_kernel(states, own, got, own_weight, got_weight, base, sent):
    rows = jnp.concatenate([unpack(own[...]), unpack(got[...])], 1)
    part = nn(rows, jnp.concatenate([own_weight[...], got_weight[...]], 0))
    sent[...] = part.astype(BF16)
    base[...] = states[...].reshape(part.shape).astype(F32) + part


def query_kernel(helper_n, base, got, gains, weight, own_rows, queries_out, mixed_ref):
    mixed = base[...] + got[...].astype(F32)
    image_n, row_n, width = own_rows.shape
    patch_n = row_n * helper_n
    mixed_ref[...] = mixed.reshape(image_n, patch_n, width)
    normed = (norm_core(mixed) * gains[1:2, :]).astype(BF16)
    queries = nt(normed, weight[...]).astype(BF16).astype(F32) * HEAD ** (-0.5)
    queries_out[...] = queries.reshape(queries_out.shape).astype(BF16)
    start = pl.multiple_of(lax.axis_index("helper") * row_n, row_n)
    own_rows[...] = mixed_ref[:, pl.ds(start, row_n), :]


def hand_on_kernel(value, *rest):
    out = rest[-1]
    out[...] = value[...]


def both_kernel(own, got, waited, out, sems):
    del waited
    row_n = own.shape[0]
    copies = [
        pltpu.make_async_copy(own, out.at[pl.ds(0, row_n)], sems.at[0]),
        pltpu.make_async_copy(got, out.at[pl.ds(row_n, row_n)], sems.at[1]),
    ]
    for copy in copies:
        copy.start()
    for copy in copies:
        copy.wait()


def cross_pairs(places, helper_n, queries, table, arrived, put):
    for at, (place, block) in enumerate(zip(places, arrived)):
        chosen = queries[0].astype(F32)
        for image in range(1, queries.shape[0]):
            chosen = jnp.where(table[place : place + 1, 0:1] == image, queries[image].astype(F32), chosen)
        columns = block.shape[0] // 2
        context = attend(head_stack(chosen), block[:columns, :], block[columns:, :])
        row_n = context.shape[0] // helper_n
        for helper in range(helper_n):
            put(at, helper, pack(context[helper * row_n : (helper + 1) * row_n]))


def cross_kernel(places, helper_n, queries, table, *rest):
    *arrived, out = rest

    def put(at, helper, rows):
        out[helper, at] = rows

    cross_pairs(places, helper_n, queries, table, arrived, put)


def last_cross_kernel(places, helper_n, queries, table, before, *rest):
    arrived, (*outs, held) = rest[: len(places)], rest[len(places) :]
    first = before.shape[1]
    helper = lax.axis_index("helper")
    for k, out in enumerate(outs):
        out[:first] = before[jnp.bitwise_xor(helper, k)]

    def put(at, helper, rows):
        held[helper, at] = rows

    cross_pairs(places, helper_n, queries, table, arrived, put)
    for k, out in enumerate(outs):
        out[first:] = held[jnp.bitwise_xor(helper, k)]


def side_rows(block):
    row_n = block.shape[1] * 2 // 3
    main, tail = block[:, :row_n, :], block[:, row_n:, :]
    tail = jnp.concatenate([tail[:, :, :HEAD], tail[:, :, HEAD:]], 1)
    return jnp.concatenate([main.reshape(-1, LANES), tail.reshape(-1, HEAD)], 1)


def placed_rows(sides, order, table):
    pair_n = len(order)
    rows = []
    for side in sides:
        pairs = [side[at].astype(F32) for at in range(pair_n)]
        placed = []
        for position in range(pair_n):
            block = pairs[0]
            for at in range(1, pair_n):
                row = pair_n + order[at]
                block = jnp.where(table[row : row + 1, 0:1] == position, pairs[at], block)
            placed.append(block.astype(BF16)[None])
        rows.append(side_rows(jnp.concatenate(placed, 0)))
    return jnp.concatenate(rows, 1)


def first_terms_kernel(order, table, weights, own, across_chip, terms):
    terms[...] = nn(placed_rows((own, across_chip), order, table), weights[...])


def out_kernel(order, own_rows, table, weights, first, across_core, across_both, out, out_v, sems):
    row_n, width = own_rows.shape[1:]
    pair_n = len(order)
    terms = first[...] + nn(placed_rows((across_core, across_both), order, table), weights[...])
    first_n = table[2 * pair_n :, 0:1]
    zero = jnp.zeros((row_n, width), F32)
    for position in range(pair_n):
        term = terms[position * row_n : (position + 1) * row_n]
        is_first = first_n > position
        out_v[0, position] = jnp.where(is_first, own_rows[0] + term, zero).astype(BF16)
        out_v[1, pair_n - 1 - position] = jnp.where(is_first, zero, own_rows[1] + term).astype(BF16)
    copies = [pltpu.make_async_copy(out_v.at[image], out.at[image], sems.at[image]) for image in range(2)]
    for copy in copies:
        copy.start()
    for copy in copies:
        copy.wait()


def local(owner_n, helper_n, states, partners, self_proj, self_out, cross_proj, cross_out, gains):
    image_n, patch_n, width = states.shape
    slot_n = partners.shape[1]
    columns = self_proj.shape[2]
    row_n = patch_n // helper_n
    row_all = image_n * patch_n
    swaps = owner_swaps(slot_n, owner_n)
    pair_n = len(swaps)
    self_proj_t = jnp.swapaxes(self_proj, 1, 2)
    cross_proj_t = jnp.swapaxes(cross_proj, 1, 2)
    chip_hop, core_hop = helper_n // 2, 1

    def across(value, k):
        return lax.ppermute(value, "helper", [(j, j ^ k) for j in range(helper_n)])

    def exchange(value, swap):
        return lax.ppermute(value, "owner", [(o, swap_target(o, swap, owner_n)) for o in range(owner_n)])

    def call(name, kernel, out_shape, in_specs, scratch, *operands, out_specs=None, flops=1):
        with jax.named_scope(name):
            return pl.pallas_call(
                kernel,
                out_shape=out_shape,
                in_specs=in_specs,
                out_specs=out_specs or jax.tree.map(lambda _: VMEM, out_shape),
                scratch_shapes=scratch,
                compiler_params=pltpu.CompilerParams(vmem_limit_bytes=VMEM_BYTES),
                cost_estimate=pl.CostEstimate(flops=flops, bytes_accessed=1, transcendentals=0),
            )(*operands)

    shape = jax.ShapeDtypeStruct
    dma = pltpu.SemaphoreType.DMA
    index_table = pltpu.SMEM(partners.shape, jnp.int32)
    block = shape((2 * columns, patch_n), BF16)

    partners_h = pltpu.with_memory_space_constraint(partners, pltpu.HBM)
    self_out_got = across(self_out, chip_hop)
    *outgoing, context, table, query_weight, cross_out_own = call(
        "own_images",
        functools.partial(own_images_kernel, swaps, owner_n),
        [block] * pair_n
        + [
            shape((row_all * columns // LANES, LANES), BF16),
            shape((2 * pair_n + 1, LANES), jnp.int32),
            shape((columns, width), BF16),
            shape(cross_out.shape, BF16),
        ],
        [HBM] * 6,
        [
            pltpu.VMEM(states.shape, BF16),
            pltpu.VMEM(gains.shape, F32),
            pltpu.VMEM((3, columns, width), BF16),
            pltpu.VMEM((2, columns, width), BF16),
            index_table,
            pltpu.VMEM((image_n, 2 * columns, patch_n), BF16),
            dma((7,)),
        ],
        *[pltpu.with_memory_space_constraint(x, pltpu.HBM) for x in (states, gains, self_proj_t, cross_proj_t)],
        partners_h,
        pltpu.with_memory_space_constraint(cross_out, pltpu.HBM),
    )
    arrived = [exchange(value, swap) for value, swap in zip(outgoing, swaps)]
    context_got = across(context, chip_hop)
    near = (slot_n - 1) // 2
    late = [at for at, (_, colour) in enumerate(swaps) if colour]
    early = [at for at in range(pair_n) if at not in late]
    short = [2 * near - 2, 2 * near - 1]
    cross_out_sent = call(
        "cross_output_rows",
        hand_on_kernel,
        shape(cross_out.shape, BF16),
        [VMEM] + [ANY] * len([arrived[short[0]]]),
        [],
        cross_out_own, *[arrived[short[0]]],
    )
    cross_out_got = across(cross_out_sent, chip_hop)
    before = [arrived[at] for at in short] + [self_out_got]
    gains_then = call(
        "gains",
        hand_on_kernel,
        shape(gains.shape, F32),
        [VMEM] + [ANY] * len(before),
        [],
        gains, *before,
    )

    made_shapes = [
        shape((image_n, row_n, width), F32),
        shape((image_n, patch_n, columns), BF16),
    ]

    def mixing(states, gains, query_weight, context, context_got, self_out, self_out_got):
        base, sent = call(
            "self_output_share",
            partial_kernel,
            [shape((row_all, width), F32), shape((row_all, width), BF16)],
            [VMEM] * 5,
            [],
            states, context, context_got, self_out, self_out_got,
        )
        made = call(
            "mixed_and_queries",
            functools.partial(query_kernel, helper_n),
            made_shapes,
            [VMEM] * 4,
            [pltpu.VMEM((image_n, patch_n, width), F32)],
            base, across(sent, core_hop), gains, query_weight,
        )
        return tuple(made)

    def no_images(*operands):
        return tuple(jnp.zeros(made.shape, made.dtype) for made in made_shapes)

    own_rows, queries = lax.cond(
        lax.axis_index("owner") < owner_n, mixing, no_images,
        states, gains_then, query_weight, context, context_got, self_out, self_out_got,
    )
    packed = columns * row_n // LANES
    early_sides = call(
        "early_cross_attention",
        functools.partial(cross_kernel, early, helper_n),
        shape((helper_n, len(early), packed, LANES), BF16),
        [VMEM] * (2 + len(early)),
        [],
        queries, table, *[arrived[at] for at in early],
        flops=EARLY_WEIGHT,
    )
    sides = call(
        "late_cross_attention",
        functools.partial(last_cross_kernel, late, helper_n),
        [shape((pair_n, packed, LANES), BF16)] * helper_n,
        [VMEM] * (3 + len(late)),
        [pltpu.VMEM((helper_n, len(late), packed, LANES), BF16)],
        queries, table, early_sides, *[arrived[at] for at in late],
        flops=LATE_WEIGHT,
    )
    sides = [sides[0]] + [across(sides[k], k) for k in range(1, helper_n)]
    cross_out_both = call(
        "cross_output_both_rows",
        both_kernel,
        shape((2 * columns, width), BF16),
        [VMEM, ANY, ANY],
        [dma((2,))],
        cross_out_sent, cross_out_got, early_sides,
    )
    cross_out_core = across(cross_out_both, core_hop)
    order = early + late
    first_terms = call(
        "first_terms",
        functools.partial(first_terms_kernel, order),
        shape((pair_n * row_n, width), F32),
        [VMEM] * 4,
        [],
        table, cross_out_both, sides[0], sides[chip_hop],
    )
    return call(
        "pair_output",
        functools.partial(out_kernel, order),
        shape((image_n, slot_n, row_n, width), BF16),
        [VMEM] * 6,
        [pltpu.VMEM((image_n, slot_n, row_n, width), BF16), dma((image_n,))],
        own_rows, table, cross_out_core, first_terms, sides[core_hop], sides[chip_hop ^ core_hop],
        out_specs=HBM,
    )


def solution(mesh):
    return jax.shard_map(
        functools.partial(local, mesh.shape["owner"], mesh.shape["helper"]),
        mesh=mesh,
        in_specs=(
            P("owner", None, None),
            P("owner", None),
            P(None, None, "helper"),
            P("helper", None),
            P(None, None, "helper"),
            P("helper", None),
            P(),
        ),
        out_specs=P("owner", None, "helper", None),
        check_vma=False,
    )
```

```python
import functools

import jax
import jax.numpy as jnp
from jax import lax
from jax.experimental import pallas as pl
from jax.experimental.pallas import tpu as pltpu
from jax.sharding import PartitionSpec as P

HEAD = 64
LANES = 128
F32 = jnp.float32
BF16 = jnp.bfloat16
VMEM_BYTES = 24 * 1024 * 1024
EARLY_WEIGHT = 3 * 10**9
LATE_WEIGHT = 10**11

VMEM = pl.BlockSpec(memory_space=pltpu.VMEM)
HBM = pl.BlockSpec(memory_space=pltpu.HBM)
ANY = pl.BlockSpec(memory_space=pl.ANY)


def owner_swaps(slot_count, owner_count):
    near = (slot_count - 1) // 2
    swaps = [(owner_count // 2, 0)]
    for k in range(near, 1, -1):
        swaps += [(k, 1), (k, 0)]
    return swaps + [(1, 0), (1, 1)]


def swap_target(owner, swap, owner_count):
    distance, colour = swap
    step = distance & -distance
    if isinstance(owner, int):
        up = (owner // step) % 2 == colour
        return (owner + (distance if up else owner_count - distance)) % owner_count
    up = jnp.bitwise_and(lax.shift_right_logical(owner, step.bit_length() - 1), 1) == colour
    return lax.rem(owner + jnp.where(up, distance, owner_count - distance), owner_count)


def nn(left, right):
    return lax.dot_general(left, right, (((1,), (0,)), ((), ())), preferred_element_type=F32)


def nt(left, right):
    return lax.dot_general(left, right, (((1,), (1,)), ((), ())), preferred_element_type=F32)


def norm_core(values):
    row_mean = jnp.mean(values, -1, keepdims=True)
    centred = values - row_mean
    row_var = jnp.mean(centred * centred, -1, keepdims=True)
    return centred * lax.rsqrt(row_var + 1e-05)


def head_stack(queries):
    head_of = lax.broadcasted_iota(jnp.int32, queries.shape, 1) // HEAD
    zero = jnp.zeros((), queries.dtype)
    return jnp.concatenate(
        [jnp.where(head_of == h, queries, zero) for h in range(queries.shape[1] // HEAD)], 0
    ).astype(BF16)


def attend(stacked, keys_t, values_t):
    column_n = keys_t.shape[0]
    head_n = column_n // HEAD
    row_n = stacked.shape[0] // head_n
    scores = nn(stacked, keys_t)
    powers = jnp.exp(scores - jnp.max(scores, -1, keepdims=True))
    weights = (powers * (1.0 / jnp.sum(powers, -1, keepdims=True))).astype(BF16)
    spread = nt(weights, values_t)
    head_of = lax.broadcasted_iota(jnp.int32, (row_n, column_n), 1) // HEAD
    context = spread[(head_n - 1) * row_n :]
    for h in range(head_n - 1):
        context = jnp.where(head_of == h, spread[h * row_n : (h + 1) * row_n], context)
    return context


def pack(block):
    row_n = block.shape[0]
    tail = block[:, LANES:]
    return jnp.concatenate(
        [block[:, :LANES], jnp.concatenate([tail[: row_n // 2], tail[row_n // 2 :]], 1)], 0
    ).astype(BF16)


def pair_place(partners, owner, image_n):
    low = owner * image_n
    found_image, found_slot = jnp.int32(0), jnp.int32(0)
    for image in range(image_n):
        for slot in range(partners.shape[1]):
            gap = partners[image, slot] - low
            hit = jnp.logical_and(gap >= 0, gap < image_n)
            found_image = jnp.where(hit, jnp.int32(image), found_image)
            found_slot = jnp.where(hit, jnp.int32(slot), found_slot)
    return found_image, found_slot


def live_count(partners, image):
    count = jnp.int32(0)
    for slot in range(partners.shape[1]):
        count = count + jnp.where(partners[image, slot] >= 0, jnp.int32(1), jnp.int32(0))
    return count


def own_images_kernel(swaps, owner_n, states, gains, self_t, cross_t, partners, weight, *rest):
    outs, rest = rest[: len(swaps)], rest[len(swaps) :]
    context_out, table, query_weight_out, weight_out, states_v, gains_v, self_v, cross_v, partners_s, held, sems = rest
    image_n, patch_n, width = states.shape
    columns = self_t.shape[1]
    copies = [
        pltpu.make_async_copy(states, states_v, sems.at[0]),
        pltpu.make_async_copy(gains, gains_v, sems.at[1]),
        pltpu.make_async_copy(cross_t.at[pl.ds(1, 2)], cross_v, sems.at[2]),
        pltpu.make_async_copy(partners, partners_s, sems.at[3]),
        pltpu.make_async_copy(self_t, self_v, sems.at[4]),
        pltpu.make_async_copy(cross_t.at[0], query_weight_out, sems.at[5]),
        pltpu.make_async_copy(weight, weight_out, sems.at[6]),
    ]
    for copy in copies:
        copy.start()
    copies[0].wait()
    rows = norm_core(states_v[...].reshape(image_n * patch_n, width).astype(F32))
    for copy in copies[1:5]:
        copy.wait()
    normed = (rows * gains_v[2:3, :]).astype(BF16)
    projected = nt(cross_v[...].reshape(2 * columns, width), normed).astype(BF16)
    for image in range(image_n):
        held[image] = projected[:, image * patch_n : (image + 1) * patch_n]
    normed = (rows * gains_v[0:1, :]).astype(BF16)
    queries = nt(normed, self_v[0]).astype(BF16).astype(F32) * HEAD ** (-0.5)
    key_value = nt(self_v[1:3].reshape(2 * columns, width), normed).astype(BF16)
    contexts = []
    for image in range(image_n):
        span = slice(image * patch_n, (image + 1) * patch_n)
        contexts.append(
            attend(head_stack(queries[span]), key_value[:columns, span], key_value[columns:, span])
        )
    me = lax.axis_index("owner")
    pair_n = len(swaps)
    for at, (out, swap) in enumerate(zip(outs, swaps)):
        image, slot = pair_place(partners_s, swap_target(me, swap, owner_n), image_n)
        out[...] = held[image]
        position = jnp.where(image == 0, slot, pair_n - 1 - slot)
        table[at : at + 1, :] = jnp.full((1, LANES), image, jnp.int32)
        table[pair_n + at : pair_n + at + 1, :] = jnp.full((1, LANES), position, jnp.int32)
    table[2 * pair_n :, :] = jnp.full((1, LANES), live_count(partners_s, 0), jnp.int32)
    context_out[...] = pack(jnp.concatenate(contexts, 0))
    copies[5].wait()
    copies[6].wait()


def unpack(block):
    row_n = block.shape[0] * 2 // 3
    tail = block[row_n:, :]
    return jnp.concatenate(
        [block[:row_n, :], jnp.concatenate([tail[:, :HEAD], tail[:, HEAD:]], 0)], 1
    )


def partial_kernel(states, own, got, own_weight, got_weight, base, sent):
    rows = jnp.concatenate([unpack(own[...]), unpack(got[...])], 1)
    part = nn(rows, jnp.concatenate([own_weight[...], got_weight[...]], 0))
    sent[...] = part.astype(BF16)
    base[...] = states[...].reshape(part.shape).astype(F32) + part


def query_kernel(helper_n, base, got, gains, weight, own_rows, queries_out, mixed_ref):
    mixed = base[...] + got[...].astype(F32)
    image_n, row_n, width = own_rows.shape
    patch_n = row_n * helper_n
    mixed_ref[...] = mixed.reshape(image_n, patch_n, width)
    normed = (norm_core(mixed) * gains[1:2, :]).astype(BF16)
    queries = nt(normed, weight[...]).astype(BF16).astype(F32) * HEAD ** (-0.5)
    queries_out[...] = queries.reshape(queries_out.shape).astype(BF16)
    start = pl.multiple_of(lax.axis_index("helper") * row_n, row_n)
    own_rows[...] = mixed_ref[:, pl.ds(start, row_n), :]


def hand_on_kernel(value, *rest):
    out = rest[-1]
    out[...] = value[...]


def both_kernel(own, got, waited, out, sems):
    del waited
    row_n = own.shape[0]
    copies = [
        pltpu.make_async_copy(own, out.at[pl.ds(0, row_n)], sems.at[0]),
        pltpu.make_async_copy(got, out.at[pl.ds(row_n, row_n)], sems.at[1]),
    ]
    for copy in copies:
        copy.start()
    for copy in copies:
        copy.wait()


def cross_pairs(places, helper_n, queries, table, arrived, put):
    for at, (place, block) in enumerate(zip(places, arrived)):
        chosen = queries[0].astype(F32)
        for image in range(1, queries.shape[0]):
            chosen = jnp.where(table[place : place + 1, 0:1] == image, queries[image].astype(F32), chosen)
        columns = block.shape[0] // 2
        context = attend(head_stack(chosen), block[:columns, :], block[columns:, :])
        row_n = context.shape[0] // helper_n
        for helper in range(helper_n):
            put(at, helper, pack(context[helper * row_n : (helper + 1) * row_n]))


def cross_kernel(places, helper_n, queries, table, *rest):
    *arrived, out = rest

    def put(at, helper, rows):
        out[helper, at] = rows

    cross_pairs(places, helper_n, queries, table, arrived, put)


def last_cross_kernel(places, helper_n, queries, table, before, *rest):
    arrived, (*outs, held) = rest[: len(places)], rest[len(places) :]
    first = before.shape[1]
    helper = lax.axis_index("helper")
    for k, out in enumerate(outs):
        out[:first] = before[jnp.bitwise_xor(helper, k)]

    def put(at, helper, rows):
        held[helper, at] = rows

    cross_pairs(places, helper_n, queries, table, arrived, put)
    for k, out in enumerate(outs):
        out[first:] = held[jnp.bitwise_xor(helper, k)]


def side_rows(block):
    row_n = block.shape[1] * 2 // 3
    main, tail = block[:, :row_n, :], block[:, row_n:, :]
    tail = jnp.concatenate([tail[:, :, :HEAD], tail[:, :, HEAD:]], 1)
    return jnp.concatenate([main.reshape(-1, LANES), tail.reshape(-1, HEAD)], 1)


def placed_rows(sides, order, table):
    pair_n = len(order)
    rows = []
    for side in sides:
        pairs = [side[at].astype(F32) for at in range(pair_n)]
        placed = []
        for position in range(pair_n):
            block = pairs[0]
            for at in range(1, pair_n):
                row = pair_n + order[at]
                block = jnp.where(table[row : row + 1, 0:1] == position, pairs[at], block)
            placed.append(block.astype(BF16)[None])
        rows.append(side_rows(jnp.concatenate(placed, 0)))
    return jnp.concatenate(rows, 1)


def first_terms_kernel(order, table, weights, core_weights, own, across_chip, across_core, terms):
    columns = core_weights.shape[0] // 2
    both = nn(placed_rows((own, across_chip), order, table), weights[...])
    terms[...] = both + nn(placed_rows((across_core,), order, table), core_weights[:columns, :])


def out_kernel(order, own_rows, table, weights, first, across_both, out, out_v, sems):
    row_n, width = own_rows.shape[1:]
    pair_n = len(order)
    columns = weights.shape[0] // 2
    terms = first[...] + nn(placed_rows((across_both,), order, table), weights[columns:, :])
    first_n = table[2 * pair_n :, 0:1]
    zero = jnp.zeros((row_n, width), F32)
    for position in range(pair_n):
        term = terms[position * row_n : (position + 1) * row_n]
        is_first = first_n > position
        out_v[0, position] = jnp.where(is_first, own_rows[0] + term, zero).astype(BF16)
        out_v[1, pair_n - 1 - position] = jnp.where(is_first, zero, own_rows[1] + term).astype(BF16)
    copies = [pltpu.make_async_copy(out_v.at[image], out.at[image], sems.at[image]) for image in range(2)]
    for copy in copies:
        copy.start()
    for copy in copies:
        copy.wait()


def local(owner_n, helper_n, states, partners, self_proj, self_out, cross_proj, cross_out, gains):
    image_n, patch_n, width = states.shape
    slot_n = partners.shape[1]
    columns = self_proj.shape[2]
    row_n = patch_n // helper_n
    row_all = image_n * patch_n
    swaps = owner_swaps(slot_n, owner_n)
    pair_n = len(swaps)
    self_proj_t = jnp.swapaxes(self_proj, 1, 2)
    cross_proj_t = jnp.swapaxes(cross_proj, 1, 2)
    chip_hop, core_hop = helper_n // 2, 1

    def across(value, k):
        return lax.ppermute(value, "helper", [(j, j ^ k) for j in range(helper_n)])

    def exchange(value, swap):
        return lax.ppermute(value, "owner", [(o, swap_target(o, swap, owner_n)) for o in range(owner_n)])

    def call(name, kernel, out_shape, in_specs, scratch, *operands, out_specs=None, flops=1):
        with jax.named_scope(name):
            return pl.pallas_call(
                kernel,
                out_shape=out_shape,
                in_specs=in_specs,
                out_specs=out_specs or jax.tree.map(lambda _: VMEM, out_shape),
                scratch_shapes=scratch,
                compiler_params=pltpu.CompilerParams(vmem_limit_bytes=VMEM_BYTES),
                cost_estimate=pl.CostEstimate(flops=flops, bytes_accessed=1, transcendentals=0),
            )(*operands)

    shape = jax.ShapeDtypeStruct
    dma = pltpu.SemaphoreType.DMA
    index_table = pltpu.SMEM(partners.shape, jnp.int32)
    block = shape((2 * columns, patch_n), BF16)

    partners_h = pltpu.with_memory_space_constraint(partners, pltpu.HBM)
    self_out_got = across(self_out, chip_hop)
    *outgoing, context, table, query_weight, cross_out_own = call(
        "own_images",
        functools.partial(own_images_kernel, swaps, owner_n),
        [block] * pair_n
        + [
            shape((row_all * columns // LANES, LANES), BF16),
            shape((2 * pair_n + 1, LANES), jnp.int32),
            shape((columns, width), BF16),
            shape(cross_out.shape, BF16),
        ],
        [HBM] * 6,
        [
            pltpu.VMEM(states.shape, BF16),
            pltpu.VMEM(gains.shape, F32),
            pltpu.VMEM((3, columns, width), BF16),
            pltpu.VMEM((2, columns, width), BF16),
            index_table,
            pltpu.VMEM((image_n, 2 * columns, patch_n), BF16),
            dma((7,)),
        ],
        *[pltpu.with_memory_space_constraint(x, pltpu.HBM) for x in (states, gains, self_proj_t, cross_proj_t)],
        partners_h,
        pltpu.with_memory_space_constraint(cross_out, pltpu.HBM),
    )
    arrived = [exchange(value, swap) for value, swap in zip(outgoing, swaps)]
    context_got = across(context, chip_hop)
    near = (slot_n - 1) // 2
    late = [at for at, (_, colour) in enumerate(swaps) if colour]
    early = [at for at in range(pair_n) if at not in late]
    short = [2 * near - 2, 2 * near - 1]
    cross_out_sent = call(
        "cross_output_rows",
        hand_on_kernel,
        shape(cross_out.shape, BF16),
        [VMEM] + [ANY] * len([arrived[short[0]]]),
        [],
        cross_out_own, *[arrived[short[0]]],
    )
    cross_out_got = across(cross_out_sent, chip_hop)
    before = [arrived[at] for at in short] + [self_out_got]
    gains_then = call(
        "gains",
        hand_on_kernel,
        shape(gains.shape, F32),
        [VMEM] + [ANY] * len(before),
        [],
        gains, *before,
    )

    made_shapes = [
        shape((image_n, row_n, width), F32),
        shape((image_n, patch_n, columns), BF16),
    ]

    def mixing(states, gains, query_weight, context, context_got, self_out, self_out_got):
        base, sent = call(
            "self_output_share",
            partial_kernel,
            [shape((row_all, width), F32), shape((row_all, width), BF16)],
            [VMEM] * 5,
            [],
            states, context, context_got, self_out, self_out_got,
        )
        made = call(
            "mixed_and_queries",
            functools.partial(query_kernel, helper_n),
            made_shapes,
            [VMEM] * 4,
            [pltpu.VMEM((image_n, patch_n, width), F32)],
            base, across(sent, core_hop), gains, query_weight,
        )
        return tuple(made)

    def no_images(*operands):
        return tuple(jnp.zeros(made.shape, made.dtype) for made in made_shapes)

    own_rows, queries = lax.cond(
        lax.axis_index("owner") < owner_n, mixing, no_images,
        states, gains_then, query_weight, context, context_got, self_out, self_out_got,
    )
    packed = columns * row_n // LANES
    early_sides = call(
        "early_cross_attention",
        functools.partial(cross_kernel, early, helper_n),
        shape((helper_n, len(early), packed, LANES), BF16),
        [VMEM] * (2 + len(early)),
        [],
        queries, table, *[arrived[at] for at in early],
        flops=EARLY_WEIGHT,
    )
    sides = call(
        "late_cross_attention",
        functools.partial(last_cross_kernel, late, helper_n),
        [shape((pair_n, packed, LANES), BF16)] * helper_n,
        [VMEM] * (3 + len(late)),
        [pltpu.VMEM((helper_n, len(late), packed, LANES), BF16)],
        queries, table, early_sides, *[arrived[at] for at in late],
        flops=LATE_WEIGHT,
    )
    sides = [sides[0]] + [across(sides[k], k) for k in range(1, helper_n)]
    cross_out_both = call(
        "cross_output_both_rows",
        both_kernel,
        shape((2 * columns, width), BF16),
        [VMEM, ANY, ANY],
        [dma((2,))],
        cross_out_sent, cross_out_got, early_sides,
    )
    cross_out_core = across(cross_out_both, core_hop)
    order = early + late
    first_terms = call(
        "first_terms",
        functools.partial(first_terms_kernel, order),
        shape((pair_n * row_n, width), F32),
        [VMEM] * 6,
        [],
        table, cross_out_both, cross_out_core, sides[0], sides[chip_hop], sides[core_hop],
    )
    return call(
        "pair_output",
        functools.partial(out_kernel, order),
        shape((image_n, slot_n, row_n, width), BF16),
        [VMEM] * 5,
        [pltpu.VMEM((image_n, slot_n, row_n, width), BF16), dma((image_n,))],
        own_rows, table, cross_out_core, first_terms, sides[chip_hop ^ core_hop],
        out_specs=HBM,
    )


def solution(mesh):
    return jax.shard_map(
        functools.partial(local, mesh.shape["owner"], mesh.shape["helper"]),
        mesh=mesh,
        in_specs=(
            P("owner", None, None),
            P("owner", None),
            P(None, None, "helper"),
            P("helper", None),
            P(None, None, "helper"),
            P("helper", None),
            P(),
        ),
        out_specs=P("owner", None, "helper", None),
        check_vma=False,
    )
```
